32 devices in a mesh: dp: 8 (over z, x), tp: 4 (over y, core).
Axes of the slice: x: 2, y: 2, z: 4, core: 2. Of those that a mesh axis runs over, the one named last changes fastest.
Arguments:
- tokens: bfloat16 [8192, 1024], P('dp'), may hold values from -6 to 6
- query_weight: bfloat16 [1024, 1024], P(None, 'tp'), may hold values from -0.1875 to 0.1875
- key_weight: bfloat16 [1024, 1024], P(None, 'tp'), may hold values from -0.1875 to 0.1875
- value_weight: bfloat16 [1024, 1024], P(None, 'tp'), may hold values from -0.1875 to 0.1875
- out_weight: bfloat16 [1024, 1024], P('tp'), may hold values from -0.75 to 0.75
- up_weight: bfloat16 [1024, 4096], P(None, 'tp'), may hold values from -0.1875 to 0.1875
- down_weight: bfloat16 [4096, 1024], P('tp'), may hold values from -0.09375 to 0.09375
- bias_table: float32 [32, 16], P(None, 'tp'), may hold values from -4 to 4
- gain_one: float32 [1024], replicated, may hold values from 0.5 to 1.5
- shift_one: float32 [1024], replicated, may hold values from -3 to 3
- gain_two: float32 [1024], replicated, may hold values from 0.5 to 1.5
- shift_two: float32 [1024], replicated, may hold values from -3 to 3
- single_item: int32 [8], P('dp'), may hold values 0 or 1
- cotangent: bfloat16 [8192, 1024], P('dp'), may hold values from -6 to 6
Outputs:
- result: bfloat16 [8192, 1024], P('dp')
- grad_tokens: float32 [8192, 1024], P('dp')
- grad_query_weight: float32 [1024, 1024], P(None, 'tp')
- grad_key_weight: float32 [1024, 1024], P(None, 'tp')
- grad_value_weight: float32 [1024, 1024], P(None, 'tp')
- grad_out_weight: float32 [1024, 1024], P('tp')
- grad_up_weight: float32 [1024, 4096], P(None, 'tp')
- grad_down_weight: float32 [4096, 1024], P('tp')
- grad_bias_table: float32 [32, 16], P(None, 'tp')
- grad_gain_one: float32 [1024], replicated
- grad_shift_one: float32 [1024], replicated
- grad_gain_two: float32 [1024], replicated
- grad_shift_two: float32 [1024], replicated
The draws below stay inside these ranges and needn't reach their ends.
All inputs are finite; a program needn't handle non-finite values. No bound on the sum of `single_item` on one device may be relied on, other than what follows from the above.
Results may differ from the reference program's by a relative error of at most 0.023.
Values may be sent and summed in bfloat16 or wider, within the bound.
No kernel may reach another device: no remote copies, remote signals or barrier semaphores. Data moves between devices by JAX's collectives and lax.ppermute only.
A program may use at most 832 MiB of HBM per device.

```python
import math
from functools import partial
import jax
import jax.numpy as jnp
from jax import lax

D = 1024
H = 16
HD = 64
FF = 4096
NB = 32
MAXDIST = 128
TOK_DEV = 1024
TOKENS = 8192
N_DP = 8
N_TP = 4


def touch_ends(entries, key, smallest, high):
    extent = entries.shape
    place = [jax.random.randint(jax.random.fold_in(key, axis), (), 0, extent[axis]) for axis in range(len(extent))]
    entries = entries.at[tuple(place)].set(smallest)
    longest = extent.index(max(extent))
    place[longest] = (place[longest] + 1) % extent[longest]
    return entries.at[tuple(place)].set(high)


def levels(key, shape, cuts, low, high):
    level = 1.0
    for dim, parts in cuts:
        draws = jax.random.uniform(jax.random.fold_in(jax.random.fold_in(key, 6), dim), (parts,), jnp.float32, low / len(cuts), high / len(cuts))
        level = level * jnp.repeat(jnp.exp(draws), shape[dim] // parts).reshape((-1,) + (1,) * (len(shape) - 1 - dim))
    return level


def gaussian(key, extent, deviation, reach, cuts=(), held_as=jnp.bfloat16):
    result = jax.random.normal(key, extent, jnp.float32) * deviation
    if len(cuts) > 0:
        result = levels(key, extent, cuts, -0.22, 0.18) * result
    return jnp.clip(result, min=-reach, max=reach).astype(held_as)


def setup_inputs(seed: int = 0) -> dict:
    key_list = jax.random.split(jax.random.key(seed), 15)
    return {
        "tokens": gaussian(key_list[0], (TOKENS, D), 1.0, 6.0, ((0, 8),)),
        "query_weight": gaussian(key_list[1], (D, H * HD), D ** -0.5, 0.1875, ((1, 4),)),
        "key_weight": gaussian(key_list[2], (D, H * HD), D ** -0.5, 0.1875, ((1, 4),)),
        "value_weight": gaussian(key_list[3], (D, H * HD), D ** -0.5, 0.1875, ((1, 4),)),
        "out_weight": gaussian(key_list[4], (H * HD, D), (H * HD // 16) ** -0.5, 0.75, ((0, 4),)),
        "up_weight": gaussian(key_list[5], (D, FF), D ** -0.5, 0.1875, ((1, 4),)),
        "down_weight": gaussian(key_list[6], (FF, D), FF ** -0.5, 0.09375, ((0, 4),)),
        "bias_table": gaussian(key_list[7], (NB, H), 1.0, 4.0, ((1, 4),), jnp.float32),
        "gain_one": jnp.clip(1.0 + 0.1 * jax.random.normal(key_list[8], (D,), jnp.float32), 0.5, 1.5),
        "shift_one": gaussian(key_list[9], (D,), 0.5, 3.0, (), jnp.float32),
        "gain_two": jnp.clip(1.0 + 0.1 * jax.random.normal(key_list[10], (D,), jnp.float32), 0.5, 1.5),
        "shift_two": gaussian(key_list[11], (D,), 0.5, 3.0, (), jnp.float32),
        "single_item": touch_ends((jax.random.randint(key_list[12], (N_DP,), 0, 2) < 1).astype(jnp.int32), jax.random.fold_in(key_list[12], 1), 0, 1),
        "cotangent": gaussian(key_list[13], (TOKENS, D), 1.0, 6.0, ((0, 8),)),
    }


epsilon = 1e-05

@jax.custom_vjp
def low(v):
    return lax.optimization_barrier(v.astype(jnp.bfloat16)).astype(jnp.float32)

@jax.custom_vjp
def low_back(v):
    return v

def low_keep(v):
    return (low(v), None)

def low_pass(kept, grad):
    return (grad,)

def back_keep(v):
    return (v, None)

def back_low(kept, grad):
    return (low(grad),)
low.defvjp(low_keep, low_pass)
low_back.defvjp(back_keep, back_low)

def thresholds_list():
    exact_count = NB // 2
    thresholds = []
    for bucket in range(1, NB):
        if bucket <= exact_count:
            thresholds.append(bucket)
        else:
            thresholds.append(int(math.ceil(exact_count * (MAXDIST / exact_count) ** ((bucket - exact_count) / exact_count))))
    return thresholds

def bucket_matrix(row_count):
    positions = jnp.arange(row_count, dtype=jnp.int32)
    distance = jnp.maximum(positions[:, None] - positions[None, :], 0)
    buckets = jnp.zeros((row_count, row_count), jnp.int32)
    for threshold in thresholds_list():
        buckets = buckets + (distance >= threshold).astype(jnp.int32)
    return buckets

def layer_norm(values, gain, shift):
    center = values - lax.optimization_barrier(jnp.mean(values, axis=-1, keepdims=True))
    spread = lax.optimization_barrier(jnp.mean(center * center, axis=-1, keepdims=True))
    return center * lax.rsqrt(spread + epsilon) * gain + shift

def gelu(values):
    return 0.5 * values * (1.0 + lax.erf(values * (1.0 / math.sqrt(2.0))))

def matmul(operand, other):
    return jnp.dot(operand, other, precision=lax.Precision.HIGHEST, preferred_element_type=jnp.float32)

def attend_block(queries, key_rows, value_rows, table_cols, single):
    row_count = queries.shape[0]
    head_count = table_cols.shape[1]
    queries = queries.reshape(row_count, head_count, HD)
    key_rows = key_rows.reshape(row_count, head_count, HD)
    value_rows = value_rows.reshape(row_count, head_count, HD)
    positions = jnp.arange(row_count, dtype=jnp.int32)
    segment = jnp.where(single == 1, 0, (positions >= row_count // 2).astype(jnp.int32))
    allowed = (segment[:, None] == segment[None, :]) & (positions[None, :] <= positions[:, None])
    scores = jnp.einsum('qhd,khd->hqk', queries, key_rows, precision=lax.Precision.HIGHEST) * HD ** (-0.5)
    scores = low_back(scores)
    rel_bias = jnp.transpose(jnp.take(table_cols, bucket_matrix(row_count), axis=0), (2, 0, 1))
    scores = jnp.where(allowed[None], scores + rel_bias, -1000000000.0)
    row_max = lax.optimization_barrier(jnp.max(scores, axis=-1, keepdims=True))
    exponent = jnp.exp(scores - row_max)
    weights = exponent / lax.optimization_barrier(jnp.sum(exponent, axis=-1, keepdims=True))
    output = jnp.einsum('hqk,khd->qhd', low(weights), value_rows, precision=lax.Precision.HIGHEST)
    return output.reshape(row_count, head_count * HD)

def attention(queries, key_rows, value_rows, table_cols, single_item):
    block_shape = (N_DP, TOK_DEV, queries.shape[1])
    per_block = jax.checkpoint(lambda pieces: attend_block(pieces[0], pieces[1], pieces[2], table_cols, pieces[3]))
    output = lax.map(per_block, (queries.reshape(block_shape), key_rows.reshape(block_shape), value_rows.reshape(block_shape), single_item))
    return output.reshape(N_DP * TOK_DEV, queries.shape[1])

def forward(tokens, query_weight, key_weight, value_weight, out_weight, up_weight, down_weight, bias_table, gain_one, shift_one, gain_two, shift_two, single_item=None):
    col_width = H * HD // N_TP
    head_count = H // N_TP
    hidden_cols = FF // N_TP
    normed = low(layer_norm(tokens, gain_one, shift_one))
    attn_sum = jnp.zeros_like(tokens)
    for tp_rank in range(N_TP):
        columns = slice(tp_rank * col_width, (tp_rank + 1) * col_width)
        local_in = low_back(normed)
        queries = low(low_back(matmul(local_in, query_weight[:, columns])))
        key_rows = low(low_back(matmul(local_in, key_weight[:, columns])))
        value_rows = low(low_back(matmul(local_in, value_weight[:, columns])))
        table_cols = bias_table[:, tp_rank * head_count:(tp_rank + 1) * head_count]
        mixture = low(low_back(attention(queries, key_rows, value_rows, table_cols, single_item)))
        attn_sum = attn_sum + low(matmul(mixture, out_weight[columns, :]))
    residual = tokens + low_back(attn_sum)
    normed_two = low(layer_norm(residual, gain_two, shift_two))
    ffn_sum = jnp.zeros_like(tokens)
    for tp_rank in range(N_TP):
        columns = slice(tp_rank * hidden_cols, (tp_rank + 1) * hidden_cols)
        local_in = low_back(normed_two)
        inner_act = low_back(matmul(local_in, up_weight[:, columns]))
        active = low(gelu(inner_act))
        ffn_sum = ffn_sum + low(matmul(active, down_weight[columns, :]))
    return residual + low_back(ffn_sum)

def reference(tokens, query_weight, key_weight, value_weight, out_weight, up_weight, down_weight, bias_table, gain_one, shift_one, gain_two, shift_two, single_item, cotangent):
    floats = [argument.astype(jnp.float32) for argument in (tokens, query_weight, key_weight, value_weight, out_weight, up_weight, down_weight, bias_table, gain_one, shift_one, gain_two, shift_two)]
    output, pullback = jax.vjp(partial(forward, single_item=single_item), *floats)
    gradients = pullback(cotangent.astype(jnp.float32))
    return (output.astype(jnp.bfloat16), gradients[0], gradients[1], gradients[2], gradients[3], gradients[4], gradients[5], gradients[6], gradients[7], gradients[8], gradients[9], gradients[10], gradients[11])
```

```python
import functools
import math

import jax
import jax.numpy as jnp
from jax import lax
from jax.experimental import pallas as pl
from jax.experimental.pallas import tpu as pltpu
from jax.sharding import PartitionSpec as P

HD = 64
NB = 32
MAXDIST = 128


epsilon = 1e-05


def thresholds_list():
    exact_count = NB // 2
    thresholds = []
    for bucket in range(1, NB):
        if bucket <= exact_count:
            thresholds.append(bucket)
        else:
            thresholds.append(
                int(
                    math.ceil(
                        exact_count
                        * (MAXDIST / exact_count) ** ((bucket - exact_count) / exact_count)
                    )
                )
            )
    return thresholds


def distance_onehot(count):
    distance = jnp.arange(count, dtype=jnp.int32)
    buckets = jnp.zeros((count,), jnp.int32)
    for threshold in thresholds_list():
        buckets = buckets + (distance >= threshold).astype(jnp.int32)
    return (buckets[:, None] == jnp.arange(NB, dtype=jnp.int32)[None, :]).astype(jnp.float32)


def norm_parts(values, gain, shift):
    center = values - jnp.mean(values, axis=-1, keepdims=True)
    scaled = lax.rsqrt(jnp.mean(center * center, axis=-1, keepdims=True) + epsilon)
    normal = center * scaled
    return (normal, scaled, normal * gain + shift)


def norm_back(grad_out, normal, scaled, gain):
    grad_norm = grad_out * gain
    inner_mean = jnp.mean(grad_norm * normal, axis=-1, keepdims=True)
    return scaled * (grad_norm - jnp.mean(grad_norm, axis=-1, keepdims=True) - normal * inner_mean)


def gelu_pair(values):
    cdf_part = 0.5 * (1.0 + lax.erf(values * (1.0 / math.sqrt(2.0))))
    slope = cdf_part + values * jnp.exp(-0.5 * values * values) * (1.0 / math.sqrt(2.0 * math.pi))
    return (0.5 * values * (1.0 + lax.erf(values * (1.0 / math.sqrt(2.0)))), slope)


BLK = 256
NEAR = 128
NEG = -1000000000.0
NT = (((1,), (1,)), ((), ()))
TN = (((0,), (0,)), ((), ()))


def dotf(a, b, dims=(((1,), (0,)), ((), ()))):
    return lax.dot_general(a, b, dims, preferred_element_type=jnp.float32)


def fill_bias(g_ref, bias_ref):
    row = lax.broadcasted_iota(jnp.int32, (2 * NEAR, NEAR), 0)
    col = lax.broadcasted_iota(jnp.int32, (2 * NEAR, NEAR), 1)
    hidden = row - NEAR > col
    for h in range(2):
        spread = jnp.broadcast_to(g_ref[h : h + 1, :], (2 * NEAR, 2 * NEAR))
        tile = pltpu.roll(spread, 0, 1, stride=1, stride_axis=0)[:, :NEAR]
        tile = jnp.where(hidden, NEG, tile)
        bias_ref[h, : 2 * NEAR, :NEAR] = tile
        bias_ref[h, 2 * NEAR :, :NEAR] = jnp.full((NEAR, NEAR), NEG, jnp.float32)
        bias_ref[h, :NEAR, NEAR:] = jnp.zeros((NEAR, NEAR), jnp.float32)
        bias_ref[h, NEAR:, NEAR:] = tile


def head_mask(x, h):
    lane = lax.broadcasted_iota(jnp.int32, x.shape, 1)
    return jnp.where((lane < HD) == (h == 0), x, jnp.zeros_like(x))


def add_near(st, bias_ref, h, low, blk):
    near = max(blk * BLK - NEAR, low)
    top = near - low
    tile = bias_ref[h, near - (blk * BLK - NEAR) :, :]
    if top == 0:
        return st + tile
    return jnp.concatenate([st[:top], st[top:] + tile], axis=0)


def each_block(row_count, single_ref, work):
    half = row_count // 2
    single = single_ref[0] == 1
    for blk in range(row_count // BLK):
        if blk * BLK < half:
            work(blk, 0)
        else:
            pl.when(single)(functools.partial(work, blk, 0))
            pl.when(jnp.logical_not(single))(functools.partial(work, blk, half))


def attn_fwd_kernel(single_ref, g_ref, q_ref, k_ref, v_ref, o_ref, lse_ref, bias_ref, vt_ref):
    row_count = q_ref.shape[0]
    fill_bias(g_ref, bias_ref)
    vt_ref[...] = v_ref[...].T

    def work(blk, low):
        high = (blk + 1) * BLK
        rows = slice(blk * BLK, high)
        q = q_ref[rows, :] * jnp.asarray(HD ** (-0.5), jnp.bfloat16)
        outs = []
        for h in range(2):
            st = dotf(k_ref[low:high, :], head_mask(q, h), NT)
            st = add_near(st, bias_ref, h, low, blk)
            m = jnp.max(st, axis=0, keepdims=True)
            p = jnp.exp(st - m)
            total = jnp.sum(p, axis=0, keepdims=True)
            ot = dotf(vt_ref[h * HD : (h + 1) * HD, low:high], p.astype(jnp.bfloat16))
            outs.append(ot / total)
            lse_ref[h : h + 1, rows] = m + jnp.log(total)
        o_ref[rows, :] = jnp.concatenate(outs, axis=0).T.astype(jnp.bfloat16)

    each_block(row_count, single_ref, work)


def attn_bwd_kernel(
    single_ref, g_ref, q_ref, k_ref, v_ref, o_ref, lse_ref, da_ref,
    dq_ref, dk_ref, dv_ref, near_ref, bias_ref, kt_ref, dk_acc, dv_acc, near_acc,
):
    row_count = q_ref.shape[0]
    fill_bias(g_ref, bias_ref)
    kt_ref[...] = k_ref[...].T
    dk_acc[...] = jnp.zeros_like(dk_acc)
    dv_acc[...] = jnp.zeros_like(dv_acc)
    near_acc[...] = jnp.zeros_like(near_acc)

    def work(blk, low):
        high = (blk + 1) * BLK
        rows = slice(blk * BLK, high)
        q = q_ref[rows, :] * jnp.asarray(HD ** (-0.5), jnp.bfloat16)
        da = da_ref[rows, :]
        prod_t = (da.astype(jnp.float32) * o_ref[rows, :].astype(jnp.float32)).T
        ps, dss, qms, dams, dqts = [], [], [], [], []
        for h in range(2):
            qm, dam = head_mask(q, h), head_mask(da, h)
            st = dotf(k_ref[low:high, :], qm, NT)
            st = add_near(st, bias_ref, h, low, blk)
            p = jnp.exp(st - lse_ref[h : h + 1, rows])
            dpt = dotf(v_ref[low:high, :], dam, NT)
            dd = jnp.sum(prod_t[h * HD : (h + 1) * HD], axis=0, keepdims=True)
            ds = p * (dpt - dd)
            own = blk * BLK - low
            if own:
                near_acc[h] += ds[own - NEAR : own + NEAR, :NEAR]
            else:
                near_acc[h, NEAR:] += ds[:NEAR, :NEAR]
            near_acc[h] += ds[own : own + 2 * NEAR, NEAR:]
            dsb = ds.astype(jnp.bfloat16)
            ps.append(p.astype(jnp.bfloat16))
            dss.append(dsb)
            qms.append(qm)
            dams.append(dam)
            dqts.append(dotf(kt_ref[h * HD : (h + 1) * HD, low:high], dsb))
        dv_acc[low:high] += dotf(jnp.concatenate(ps, axis=1), jnp.concatenate(dams, axis=0))
        dk_acc[low:high] += dotf(jnp.concatenate(dss, axis=1), jnp.concatenate(qms, axis=0))
        dq = jnp.concatenate(dqts, axis=0).T * HD ** (-0.5)
        dq_ref[rows, :] = dq.astype(jnp.bfloat16)

    each_block(row_count, single_ref, work)
    dk_ref[...] = dk_acc[...].astype(jnp.bfloat16)
    dv_ref[...] = dv_acc[...].astype(jnp.bfloat16)
    near_ref[...] = jnp.zeros_like(near_ref)
    for h in range(2):
        acc = jnp.concatenate([near_acc[h], jnp.zeros((2 * NEAR, NEAR), jnp.float32)], axis=1)
        row = lax.broadcasted_iota(jnp.int32, acc.shape, 0)
        for bit in range((2 * NEAR - 1).bit_length()):
            moved = pltpu.roll(acc, 2 * NEAR - (1 << bit), 1)
            acc = jnp.where((row & (1 << bit)) != 0, moved, acc)
        near_ref[h : h + 1, :] = jnp.sum(acc, axis=0, keepdims=True)


def pair_specs(row_count):
    smem = pl.BlockSpec(memory_space=pltpu.SMEM)
    cols = pl.BlockSpec((row_count, 2 * HD), lambda p: (0, p))
    near = pl.BlockSpec((None, 8, 2 * NEAR), lambda p: (p, 0, 0))
    lse = pl.BlockSpec((None, 8, row_count), lambda p: (p, 0, 0))
    return smem, cols, near, lse


def attn_forward(single_item, g, q, k, v):
    row_count, width = q.shape
    pairs = width // (2 * HD)
    smem, cols, near, lse = pair_specs(row_count)
    return pl.pallas_call(
        attn_fwd_kernel,
        grid=(pairs,),
        in_specs=[smem, near, cols, cols, cols],
        out_specs=[cols, lse],
        out_shape=[
            jax.ShapeDtypeStruct((row_count, width), jnp.bfloat16),
            jax.ShapeDtypeStruct((pairs, 8, row_count), jnp.float32),
        ],
        scratch_shapes=[
            pltpu.VMEM((2, 3 * NEAR, BLK), jnp.float32),
            pltpu.VMEM((2 * HD, row_count), jnp.bfloat16),
        ],
        compiler_params=pltpu.CompilerParams(vmem_limit_bytes=48 * 1024 * 1024),
        cost_estimate=pl.CostEstimate(
            flops=2 * row_count * row_count * width * 2,
            bytes_accessed=8 * row_count * width,
            transcendentals=row_count * row_count * width // HD // 2,
        ),
        name="attn_forward",
    )(single_item, g, q, k, v)


def attn_backward(single_item, g, q, k, v, o, lse_rows, da):
    row_count, width = q.shape
    pairs = width // (2 * HD)
    smem, cols, near, lse = pair_specs(row_count)
    flat = jax.ShapeDtypeStruct((row_count, width), jnp.bfloat16)
    return pl.pallas_call(
        attn_bwd_kernel,
        grid=(pairs,),
        in_specs=[smem, near, cols, cols, cols, cols, lse, cols],
        out_specs=[cols, cols, cols, near],
        out_shape=[flat, flat, flat, jax.ShapeDtypeStruct((pairs, 8, 2 * NEAR), jnp.float32)],
        scratch_shapes=[
            pltpu.VMEM((2, 3 * NEAR, BLK), jnp.float32),
            pltpu.VMEM((2 * HD, row_count), jnp.bfloat16),
            pltpu.VMEM((row_count, 2 * HD), jnp.float32),
            pltpu.VMEM((row_count, 2 * HD), jnp.float32),
            pltpu.VMEM((2, 2 * NEAR, NEAR), jnp.float32),
        ],
        compiler_params=pltpu.CompilerParams(vmem_limit_bytes=48 * 1024 * 1024),
        cost_estimate=pl.CostEstimate(
            flops=2 * row_count * row_count * width * 5,
            bytes_accessed=16 * row_count * width,
            transcendentals=row_count * row_count * width // HD // 2,
        ),
        name="attn_backward",
    )(single_item, g, q, k, v, o, lse_rows, da)


def near_bias(bias_table):
    head_count = bias_table.shape[1]
    rows = jnp.dot(
        distance_onehot(NEAR), bias_table - bias_table[NB - 1 :],
        precision=lax.Precision.HIGHEST, preferred_element_type=jnp.float32,
    ).T
    rows = jnp.pad(rows, ((0, 0), (NEAR, 0))).reshape(head_count // 2, 2, 2 * NEAR)
    return jnp.pad(rows, ((0, 0), (0, 6), (0, 0)))


def table_grad(near, head_count):
    by_dist = near[:, :2, NEAR:].reshape(head_count, NEAR)
    grad = jnp.dot(
        by_dist, distance_onehot(NEAR)[:, : NB - 1],
        precision=lax.Precision.HIGHEST, preferred_element_type=jnp.float32,
    )
    return jnp.concatenate([grad, -jnp.sum(grad, axis=1, keepdims=True)], axis=1).T


def shards(
    tokens,
    query_weight,
    key_weight,
    value_weight,
    out_weight,
    up_weight,
    down_weight,
    bias_table,
    gain_one,
    shift_one,
    gain_two,
    shift_two,
    single_item,
    cotangent,
):
    row_count = tokens.shape[0]
    head_count = bias_table.shape[1]
    near_rows = near_bias(bias_table)
    token_full = tokens.astype(jnp.float32)
    normal_one, scaled_one, normed = norm_parts(token_full, gain_one, shift_one)
    normed_low = normed.astype(jnp.bfloat16)
    queries = jnp.dot(normed_low, query_weight, preferred_element_type=jnp.float32).astype(
        jnp.bfloat16
    )
    key_rows = jnp.dot(normed_low, key_weight, preferred_element_type=jnp.float32).astype(
        jnp.bfloat16
    )
    value_rows = jnp.dot(normed_low, value_weight, preferred_element_type=jnp.float32).astype(
        jnp.bfloat16
    )
    attended, lse_rows = attn_forward(single_item, near_rows, queries, key_rows, value_rows)
    attn_sum = lax.psum(
        jnp.dot(attended, out_weight, preferred_element_type=jnp.float32).astype(jnp.bfloat16), "tp"
    ).astype(jnp.float32)
    residual = token_full + attn_sum
    normal_two, scaled_two, normed_two = norm_parts(residual, gain_two, shift_two)
    normed_two_low = normed_two.astype(jnp.bfloat16)
    inner_act = jnp.dot(normed_two_low, up_weight, preferred_element_type=jnp.float32)
    gelu_out, gelu_slope = gelu_pair(inner_act)
    active = gelu_out.astype(jnp.bfloat16)
    ffn_sum = lax.psum(
        jnp.dot(active, down_weight, preferred_element_type=jnp.float32).astype(jnp.bfloat16), "tp"
    ).astype(jnp.float32)
    result = (residual + ffn_sum).astype(jnp.bfloat16)
    grad_down = jnp.dot(active.T, cotangent, preferred_element_type=jnp.float32)
    grad_active = jnp.dot(cotangent, down_weight.T, preferred_element_type=jnp.float32)
    grad_inner = (grad_active * gelu_slope).astype(jnp.bfloat16)
    grad_up = jnp.dot(normed_two_low.T, grad_inner, preferred_element_type=jnp.float32)
    grad_normed_two = lax.psum(
        jnp.dot(grad_inner, up_weight.T, preferred_element_type=jnp.float32).astype(jnp.bfloat16),
        "tp",
    ).astype(jnp.float32)
    grad_gain_two = jnp.sum(grad_normed_two * normal_two, axis=0)
    grad_shift_two = jnp.sum(grad_normed_two, axis=0)
    grad_residual = cotangent.astype(jnp.float32) + norm_back(
        grad_normed_two, normal_two, scaled_two, gain_two
    )
    grad_residual_low = grad_residual.astype(jnp.bfloat16)
    grad_out = jnp.dot(attended.T, grad_residual_low, preferred_element_type=jnp.float32)
    grad_attended = jnp.dot(grad_residual_low, out_weight.T, preferred_element_type=jnp.float32)
    grad_query, grad_key, grad_value, near_totals = attn_backward(
        single_item, near_rows, queries, key_rows, value_rows, attended, lse_rows,
        grad_attended.astype(jnp.bfloat16),
    )
    grad_table = table_grad(near_totals, head_count)
    grad_qw = jnp.dot(normed_low.T, grad_query, preferred_element_type=jnp.float32)
    grad_kw = jnp.dot(normed_low.T, grad_key, preferred_element_type=jnp.float32)
    grad_vw = jnp.dot(normed_low.T, grad_value, preferred_element_type=jnp.float32)
    grad_normed = jnp.dot(grad_query, query_weight.T, preferred_element_type=jnp.float32)
    grad_normed = grad_normed + jnp.dot(grad_key, key_weight.T, preferred_element_type=jnp.float32)
    grad_normed = grad_normed + jnp.dot(
        grad_value, value_weight.T, preferred_element_type=jnp.float32
    )
    grad_normed = lax.psum(grad_normed.astype(jnp.bfloat16), "tp").astype(jnp.float32)
    grad_gain_one = jnp.sum(grad_normed * normal_one, axis=0)
    grad_shift_one = jnp.sum(grad_normed, axis=0)
    grad_tokens = grad_residual + norm_back(grad_normed, normal_one, scaled_one, gain_one)
    summed = (
        lax.psum(grad_qw.astype(jnp.bfloat16), "dp").astype(jnp.float32),
        lax.psum(grad_kw.astype(jnp.bfloat16), "dp").astype(jnp.float32),
        lax.psum(grad_vw.astype(jnp.bfloat16), "dp").astype(jnp.float32),
        lax.psum(grad_out.astype(jnp.bfloat16), "dp").astype(jnp.float32),
        lax.psum(grad_up.astype(jnp.bfloat16), "dp").astype(jnp.float32),
        lax.psum(grad_down.astype(jnp.bfloat16), "dp").astype(jnp.float32),
        lax.psum(grad_table.astype(jnp.bfloat16), "dp").astype(jnp.float32),
        lax.psum(grad_gain_one.astype(jnp.bfloat16), "dp").astype(jnp.float32),
        lax.psum(grad_shift_one.astype(jnp.bfloat16), "dp").astype(jnp.float32),
        lax.psum(grad_gain_two.astype(jnp.bfloat16), "dp").astype(jnp.float32),
        lax.psum(grad_shift_two.astype(jnp.bfloat16), "dp").astype(jnp.float32),
    )
    return (
        result,
        grad_tokens,
        summed[0],
        summed[1],
        summed[2],
        summed[3],
        summed[4],
        summed[5],
        summed[6],
        summed[7],
        summed[8],
        summed[9],
        summed[10],
    )


def solution(mesh):
    placed = (
        P("dp", None),
        P(None, "tp"),
        P(None, "tp"),
        P(None, "tp"),
        P("tp", None),
        P(None, "tp"),
        P("tp", None),
        P(None, "tp"),
        P(),
        P(),
        P(),
        P(),
        P("dp"),
        P("dp", None),
    )
    return jax.shard_map(
        shards,
        mesh=mesh,
        in_specs=placed,
        out_specs=(
            P("dp", None),
            P("dp", None),
            P(None, "tp"),
            P(None, "tp"),
            P(None, "tp"),
            P("tp", None),
            P(None, "tp"),
            P("tp", None),
            P(None, "tp"),
            P(),
            P(),
            P(),
            P(),
        ),
        check_vma=False,
    )
```

```python
import functools
import math

import jax
import jax.numpy as jnp
from jax import lax
from jax.experimental import pallas as pl
from jax.experimental.pallas import tpu as pltpu
from jax.sharding import PartitionSpec as P

HD = 64
NB = 32
MAXDIST = 128


epsilon = 1e-05
FRONT = {"norm_qkv": 3.5, "attn_forward": 4.5, "project_out": 6.0, "feed_forward": 7.0}
REST = {"split_add": 1.5, "join_rows": 2.0, "weight_grad": 3.0, "norm_back": 2.0, "product": 1.5, "product_back": 1.5, "attn_backward": 7.0, "add_own": 1.3, "add_up": 1.0, "join_four": 4.0, "add_small": 0.5}


def cost_of(name):
    us = FRONT[name] * 1.000000 if name in FRONT else REST[name] * 0.300000
    return pl.CostEstimate(flops=max(1, int(us * 1.15e9)), bytes_accessed=1, transcendentals=0)

VMEM_LIMIT = 32 * 1024 * 1024
PIECES = 2


def thresholds_list():
    exact_count = NB // 2
    thresholds = []
    for bucket in range(1, NB):
        if bucket <= exact_count:
            thresholds.append(bucket)
        else:
            thresholds.append(
                int(
                    math.ceil(
                        exact_count
                        * (MAXDIST / exact_count) ** ((bucket - exact_count) / exact_count)
                    )
                )
            )
    return thresholds


def distance_onehot(count):
    distance = jnp.arange(count, dtype=jnp.int32)
    buckets = jnp.zeros((count,), jnp.int32)
    for threshold in thresholds_list():
        buckets = buckets + (distance >= threshold).astype(jnp.int32)
    return (buckets[:, None] == jnp.arange(NB, dtype=jnp.int32)[None, :]).astype(jnp.float32)


def norm_parts(values, gain, shift):
    center = values - jnp.mean(values, axis=-1, keepdims=True)
    scaled = lax.rsqrt(jnp.mean(center * center, axis=-1, keepdims=True) + epsilon)
    normal = center * scaled
    return (normal, scaled, normal * gain + shift)


def norm_back(grad_out, normal, scaled, gain):
    grad_norm = grad_out * gain
    inner_mean = jnp.mean(grad_norm * normal, axis=-1, keepdims=True)
    return scaled * (grad_norm - jnp.mean(grad_norm, axis=-1, keepdims=True) - normal * inner_mean)


def gelu_pair(values):
    bell = jnp.exp(-0.5 * values * values)
    t = 1.0 / (1.0 + (0.3275911 * math.sqrt(0.5)) * jnp.abs(values))
    poly = 0.5 * 1.061405429
    for factor in (-1.453152027, 1.421413741, -0.284496736, 0.254829592):
        poly = poly * t + 0.5 * factor
    tail = poly * t * bell
    cdf = jnp.where(values < 0.0, tail, 1.0 - tail)
    return values * cdf, cdf + values * bell * (1.0 / math.sqrt(2.0 * math.pi))


BLK = 256
NEAR = 128
NEG = -1000000000.0
NT = (((1,), (1,)), ((), ()))
TN = (((0,), (0,)), ((), ()))


def dotf(a, b, dims=(((1,), (0,)), ((), ()))):
    return lax.dot_general(a, b, dims, preferred_element_type=jnp.float32)


def fill_bias(g_ref, bias_ref):
    row = lax.broadcasted_iota(jnp.int32, (2 * NEAR, NEAR), 0)
    col = lax.broadcasted_iota(jnp.int32, (2 * NEAR, NEAR), 1)
    hidden = row - NEAR > col
    for h in range(2):
        spread = jnp.broadcast_to(g_ref[h : h + 1, :], (2 * NEAR, 2 * NEAR))
        tile = pltpu.roll(spread, 0, 1, stride=1, stride_axis=0)[:, :NEAR]
        tile = jnp.where(hidden, NEG, tile)
        bias_ref[h, : 2 * NEAR, :NEAR] = tile
        bias_ref[h, 2 * NEAR :, :NEAR] = jnp.full((NEAR, NEAR), NEG, jnp.float32)
        bias_ref[h, :NEAR, NEAR:] = jnp.zeros((NEAR, NEAR), jnp.float32)
        bias_ref[h, NEAR:, NEAR:] = tile


def head_mask(x, h):
    lane = lax.broadcasted_iota(jnp.int32, x.shape, 1)
    return jnp.where((lane < HD) == (h == 0), x, jnp.zeros_like(x))


def add_near(st, bias_ref, h, low, blk):
    near = max(blk * BLK - NEAR, low)
    top = near - low
    tile = bias_ref[h, near - (blk * BLK - NEAR) :, :]
    if top == 0:
        return st + tile
    return jnp.concatenate([st[:top], st[top:] + tile], axis=0)


def each_block(row_count, single_ref, work):
    half = row_count // 2
    single = single_ref[0] == 1
    for blk in range(row_count // BLK):
        if blk * BLK < half:
            work(blk, 0)
        else:
            pl.when(single)(functools.partial(work, blk, 0))
            pl.when(jnp.logical_not(single))(functools.partial(work, blk, half))


def attn_fwd_kernel(single_ref, g_ref, q_ref, k_ref, v_ref, o_ref, lse_ref, bias_ref, vt_ref):
    row_count = q_ref.shape[0]
    fill_bias(g_ref, bias_ref)
    vt_ref[...] = v_ref[...].T

    def work(blk, low):
        high = (blk + 1) * BLK
        rows = slice(blk * BLK, high)
        q = q_ref[rows, :] * jnp.asarray(HD ** (-0.5), jnp.bfloat16)
        outs = []
        for h in range(2):
            st = dotf(k_ref[low:high, :], head_mask(q, h), NT)
            st = add_near(st, bias_ref, h, low, blk)
            m = jnp.max(st, axis=0, keepdims=True)
            p = jnp.exp(st - m)
            total = jnp.sum(p, axis=0, keepdims=True)
            ot = dotf(vt_ref[h * HD : (h + 1) * HD, low:high], p.astype(jnp.bfloat16))
            outs.append(ot / total)
            lse_ref[h : h + 1, rows] = m + jnp.log(total)
        o_ref[rows, :] = jnp.concatenate(outs, axis=0).T.astype(jnp.bfloat16)

    each_block(row_count, single_ref, work)


def attn_bwd_kernel(
    single_ref, g_ref, q_ref, k_ref, v_ref, o_ref, lse_ref, gr_ref, w_ref,
    dq_ref, dk_ref, dv_ref, near_ref, bias_ref, kt_ref, dk_acc, dv_acc, near_acc,
):
    row_count = q_ref.shape[0]
    fill_bias(g_ref, bias_ref)
    kt_ref[...] = k_ref[...].T
    dk_acc[...] = jnp.zeros_like(dk_acc)
    dv_acc[...] = jnp.zeros_like(dv_acc)
    near_acc[...] = jnp.zeros_like(near_acc)

    def work(blk, low):
        high = (blk + 1) * BLK
        rows = slice(blk * BLK, high)
        q = q_ref[rows, :] * jnp.asarray(HD ** (-0.5), jnp.bfloat16)
        da = dotf(gr_ref[rows, :], w_ref[...], NT).astype(jnp.bfloat16)
        prod_t = (da.astype(jnp.float32) * o_ref[rows, :].astype(jnp.float32)).T
        ps, dss, qms, dams, dqts = [], [], [], [], []
        for h in range(2):
            qm, dam = head_mask(q, h), head_mask(da, h)
            st = dotf(k_ref[low:high, :], qm, NT)
            st = add_near(st, bias_ref, h, low, blk)
            p = jnp.exp(st - lse_ref[h : h + 1, rows])
            dpt = dotf(v_ref[low:high, :], dam, NT)
            dd = jnp.sum(prod_t[h * HD : (h + 1) * HD], axis=0, keepdims=True)
            ds = p * (dpt - dd)
            own = blk * BLK - low
            if own:
                near_acc[h] += ds[own - NEAR : own + NEAR, :NEAR]
            else:
                near_acc[h, NEAR:] += ds[:NEAR, :NEAR]
            near_acc[h] += ds[own : own + 2 * NEAR, NEAR:]
            dsb = ds.astype(jnp.bfloat16)
            ps.append(p.astype(jnp.bfloat16))
            dss.append(dsb)
            qms.append(qm)
            dams.append(dam)
            dqts.append(dotf(kt_ref[h * HD : (h + 1) * HD, low:high], dsb))
        dv_acc[low:high] += dotf(jnp.concatenate(ps, axis=1), jnp.concatenate(dams, axis=0))
        dk_acc[low:high] += dotf(jnp.concatenate(dss, axis=1), jnp.concatenate(qms, axis=0))
        dq = jnp.concatenate(dqts, axis=0).T * HD ** (-0.5)
        dq_ref[rows, :] = dq.astype(jnp.bfloat16)

    each_block(row_count, single_ref, work)
    dk_ref[...] = dk_acc[...].astype(jnp.bfloat16)
    dv_ref[...] = dv_acc[...].astype(jnp.bfloat16)
    near_ref[...] = jnp.zeros_like(near_ref)
    for h in range(2):
        acc = jnp.concatenate([near_acc[h], jnp.zeros((2 * NEAR, NEAR), jnp.float32)], axis=1)
        row = lax.broadcasted_iota(jnp.int32, acc.shape, 0)
        for bit in range((2 * NEAR - 1).bit_length()):
            moved = pltpu.roll(acc, 2 * NEAR - (1 << bit), 1)
            acc = jnp.where((row & (1 << bit)) != 0, moved, acc)
        near_ref[h : h + 1, :] = jnp.sum(acc, axis=0, keepdims=True)


def pair_specs(row_count, first):
    smem = pl.BlockSpec(memory_space=pltpu.SMEM)
    cols = pl.BlockSpec((row_count, 2 * HD), lambda p: (0, first + p))
    near = pl.BlockSpec((None, 8, 2 * NEAR), lambda p: (first + p, 0, 0))
    lse = pl.BlockSpec((None, 8, row_count), lambda p: (first + p, 0, 0))
    return smem, cols, near, lse


def held(arrays):
    return [pl.BlockSpec(memory_space=pl.ANY)] * len(arrays)


def attn_forward(line, pair, single_item, g, q, k, v, also=()):
    row_count = q.shape[0]
    after = line + list(also)
    smem, cols, near, _ = pair_specs(row_count, pair)
    own = pl.BlockSpec((row_count, 2 * HD), lambda p: (0, 0))
    lse = pl.BlockSpec((8, row_count), lambda p: (0, 0))

    def kernel(*refs):
        attn_fwd_kernel(*refs[:5], *refs[5 + len(after) :])

    attended, lse_rows = pl.pallas_call(
        kernel,
        grid=(1,),
        in_specs=[smem, near, cols, cols, cols] + held(after),
        out_specs=[own, lse],
        out_shape=[
            jax.ShapeDtypeStruct((row_count, 2 * HD), jnp.bfloat16),
            jax.ShapeDtypeStruct((8, row_count), jnp.float32),
        ],
        scratch_shapes=[
            pltpu.VMEM((2, 3 * NEAR, BLK), jnp.float32),
            pltpu.VMEM((2 * HD, row_count), jnp.bfloat16),
        ],
        compiler_params=pltpu.CompilerParams(vmem_limit_bytes=VMEM_LIMIT),
        cost_estimate=cost_of("attn_forward"),
        name="attn_forward",
    )(single_item, g, q, k, v, *after)
    line[:] = [lse_rows]
    return attended, lse_rows


def attn_backward(line, pair, single_item, g, q, k, v, o, lse_rows, grad, out_weight):
    row_count = q.shape[0]
    after = list(line)
    smem, cols, near, _ = pair_specs(row_count, pair)
    own = pl.BlockSpec((row_count, 2 * HD), lambda p: (0, 0))
    lse = pl.BlockSpec((8, row_count), lambda p: (0, 0))
    near_out = pl.BlockSpec((8, 2 * NEAR), lambda p: (0, 0))
    flat = jax.ShapeDtypeStruct((row_count, 2 * HD), jnp.bfloat16)

    def kernel(*refs):
        attn_bwd_kernel(*refs[:9], *refs[9 + len(after) :])

    *grads, near_totals = pl.pallas_call(
        kernel,
        grid=(1,),
        in_specs=[smem, near, cols, cols, cols, own, lse]
        + [
            pl.BlockSpec(grad.shape, lambda p: (0, 0)),
            pl.BlockSpec((2 * HD, grad.shape[1]), lambda p: (pair, 0)),
        ]
        + held(after),
        out_specs=[own, own, own, near_out],
        out_shape=[flat, flat, flat, jax.ShapeDtypeStruct((8, 2 * NEAR), jnp.float32)],
        scratch_shapes=[
            pltpu.VMEM((2, 3 * NEAR, BLK), jnp.float32),
            pltpu.VMEM((2 * HD, row_count), jnp.bfloat16),
            pltpu.VMEM((row_count, 2 * HD), jnp.float32),
            pltpu.VMEM((row_count, 2 * HD), jnp.float32),
            pltpu.VMEM((2, 2 * NEAR, NEAR), jnp.float32),
        ],
        compiler_params=pltpu.CompilerParams(vmem_limit_bytes=VMEM_LIMIT),
        cost_estimate=cost_of("attn_backward"),
        name="attn_backward",
    )(single_item, g, q, k, v, o, lse_rows, grad, out_weight, *after)
    line[:] = [near_totals]
    return *grads, near_totals


def near_bias(bias_table):
    head_count = bias_table.shape[1]
    rows = jnp.dot(
        distance_onehot(NEAR), bias_table - bias_table[NB - 1 :],
        precision=lax.Precision.HIGHEST, preferred_element_type=jnp.float32,
    ).T
    rows = jnp.pad(rows, ((0, 0), (NEAR, 0))).reshape(head_count // 2, 2, 2 * NEAR)
    return jnp.pad(rows, ((0, 0), (0, 6), (0, 0)))


def table_grad(near, head_count):
    by_dist = near[:, :2, NEAR:].reshape(head_count, NEAR)
    grad = jnp.dot(
        by_dist, distance_onehot(NEAR)[:, : NB - 1],
        precision=lax.Precision.HIGHEST, preferred_element_type=jnp.float32,
    )
    return jnp.concatenate([grad, -jnp.sum(grad, axis=1, keepdims=True)], axis=1).T


def index_bits(count):
    return [1 << i for i in range(count.bit_length() - 1)]


def swap(values, axis, count, bit):
    return lax.ppermute(values, axis, [(i, i ^ bit) for i in range(count)])


def rank_bit(axis, bit):
    return (lax.axis_index(axis) // bit) % 2


def gather_parts(values, axis, count, bits):
    parts = {0: values}
    for bit in bits:
        for k in list(parts):
            parts[k ^ bit] = swap(parts[k], axis, count, bit)
    return [parts[k] for k in range(count)]


def own_start(axis, bits, size):
    start = 0
    for bit in bits:
        size //= 2
        start = start + rank_bit(axis, bit) * size
    return start, size


def sum_over(values, axis, count, bits):
    for bit in bits:
        values = values + swap(values, axis, count, bit)
    return values


def spec(shape, index):
    return pl.BlockSpec(shape, index)


def scalars(values):
    values = values if isinstance(values, list) else [values]
    return jnp.stack([jnp.asarray(v, jnp.int32) for v in values])


def stage(line, name, body, grid, upper, ins, outs, scratch=(), also=()):
    after = line + list(also)
    shapes = [shape for shape, _ in outs] + [jax.ShapeDtypeStruct((8, 128), jnp.float32)]
    token = pl.BlockSpec((8, 128), lambda *a: (0, 0))
    held = pl.BlockSpec(memory_space=pl.ANY)

    def kernel(upper_ref, *refs):
        used = refs[: len(ins)]
        rest = refs[len(ins) + len(after) :]
        body(upper_ref, *used, *rest[: len(outs)], *rest[len(outs) + 1 :])
        rest[len(outs)][...] = jnp.zeros((8, 128), jnp.float32)

    *results, mark = pl.pallas_call(
        kernel,
        grid_spec=pltpu.PrefetchScalarGridSpec(
            num_scalar_prefetch=1,
            grid=grid,
            in_specs=[where for _, where in ins] + [held] * len(after),
            out_specs=[where for _, where in outs] + [token],
            scratch_shapes=list(scratch),
        ),
        out_shape=shapes,
        compiler_params=pltpu.CompilerParams(vmem_limit_bytes=VMEM_LIMIT),
        cost_estimate=cost_of(name),
        name=name,
    )(scalars(upper), *[x for x, _ in ins], *after)
    line[:] = [mark]
    return results if len(results) > 1 else results[0]


def cat(refs):
    return refs[0][...] if len(refs) == 1 else jnp.concatenate([r[...] for r in refs], axis=1)


def put(refs, values):
    at = 0
    for ref in refs:
        size = ref.shape[1]
        ref[...] = values[:, at : at + size].astype(ref.dtype)
        at += size


def columns(arrays, blk, index):
    return [(x, spec((blk, x.shape[1]), index)) for x in arrays]


def pieces_of(rows, cols, count, dtype=jnp.bfloat16):
    return [jax.ShapeDtypeStruct((rows, cols // count), dtype)] * count


def split_add(line, upper, kept, got, count=1):
    rows, cols = got[0].shape[0], sum(x.shape[1] for x in got)
    half = rows // 2
    blk = min(half, 128)
    n = half // blk
    a, b = len(kept), len(got)

    def body(u, *refs):
        for at, outs in ((0, refs[2 * a + 2 * b : -1]), (a + b, refs[-1:])):
            total = cat(refs[at : at + a]).astype(jnp.float32)
            put(outs, total + cat(refs[at + a : at + a + b]).astype(jnp.float32))

    away = lambda j, u: ((1 - u[0]) * n + j, 0)
    here = lambda j, u: (u[0] * n + j, 0)
    outs = pieces_of(half, cols, count) + pieces_of(half, cols, 1)
    *send, keep = stage(
        line, "split_add", body, (n,), upper,
        columns(kept + got, blk, away) + columns(kept + got, blk, here),
        [(x, spec((blk, x.shape[1]), lambda j, u: (j, 0))) for x in outs],
    )
    return send, [keep]


def add_up(line, kept, got):
    rows, cols = kept.shape
    blk = min(rows, 128)
    flat = lambda j, u: (j, 0)

    def body(u, k, g, out):
        out[...] = (k[...].astype(jnp.float32) + g[...].astype(jnp.float32)).astype(out.dtype)

    where = spec((blk, cols), flat)
    return stage(
        line, "add_up", body, (rows // blk,), 0, [(kept, where), (got, where)],
        [(jax.ShapeDtypeStruct(kept.shape, jnp.bfloat16), where)],
    )


def join_rows(line, upper, mine, got, dtype, count=1):
    rows, cols = mine[0].shape[0], sum(x.shape[1] for x in mine)
    blk = min(rows, 256)
    n = rows // blk
    a = len(mine)

    def body(u, *refs):
        i = pl.program_id(0)

        @pl.when(i == 0)
        def _():
            put(refs[2 * a :], cat(refs[:a]))

        @pl.when(i == 1)
        def _():
            put(refs[2 * a :], cat(refs[a : 2 * a]))

    joined = stage(
        line, "join_rows", body, (2, n), upper,
        columns(mine, blk, lambda i, j, u: (jnp.where(i == 0, j, n - 1), 0))
        + columns(got, blk, lambda i, j, u: (jnp.where(i == 0, 0, j), 0)),
        [
            (x, spec((blk, x.shape[1]), lambda i, j, u: (jnp.where(i == 0, u[0], 1 - u[0]) * n + j, 0)))
            for x in pieces_of(2 * rows, cols, count, dtype)
        ],
    )
    return joined if count > 1 else [joined]


def join_four(line, uppers, pieces, outs):
    rows, cols = pieces[0].shape
    blk = min(rows, 128)
    n = rows // blk

    def body(u, *refs):
        for p in range(4):

            @pl.when(pl.program_id(0) == p)
            def _():
                for out, (first, size, turned) in zip(refs[4:], outs):
                    x = refs[p][:, first : first + size].astype(jnp.float32)
                    out[...] = x.T if turned else x

    def place(i, j, u):
        high = jnp.where(i < 2, u[0], 1 - u[0])
        return (high * 2 + jnp.where(i % 2 == 0, u[1], 1 - u[1])) * n + j

    def turn(p):
        return lambda i, j, u: (jnp.where(i == p, j, jnp.where(i < p, 0, n - 1)), 0)

    results = []
    for _, size, turned in outs:
        if turned:
            results.append((jax.ShapeDtypeStruct((size, 4 * rows), jnp.float32), spec((size, blk), lambda i, j, u: (0, place(i, j, u)))))
        else:
            results.append((jax.ShapeDtypeStruct((4 * rows, size), jnp.float32), spec((blk, size), lambda i, j, u: (place(i, j, u), 0))))
    return stage(
        line, "join_four", body, (4, n), uppers,
        [(x, spec((blk, cols), turn(p))) for p, x in enumerate(pieces)], results,
    )


def weight_grad(line, upper, away, groups):
    left = groups[0][0][0]
    half = left.shape[1] // 2
    blk = min(half, 256)
    n = half // blk

    def row_spec(x, rows, cols, column, turn):
        if turn is None:
            return (x, spec((x.shape[0], cols), lambda j, u: (0, column(j, u))))
        pick = (lambda u: u[1]) if turn else (lambda u: 1 - u[1])
        if x.shape[0] == rows:
            pick = lambda u: 0
        return (x, spec((rows, cols), lambda j, u: (pick(u), column(j, u))))

    if away:
        block = lambda j, u: (1 - u[0]) * n + j
    else:
        block = lambda j, u: u[0] * n + j
    ins, plan = [], []
    for group in groups:
        terms = []
        for left, turn, rights, right_turn in group:
            rows = left.shape[0] if turn is None and right_turn is None else min(left.shape[0], rights[0].shape[0])
            if rows == left.shape[0] == rights[0].shape[0] and turn is not None:
                rows = left.shape[0] // 2
            terms.append((len(ins), len(rights)))
            ins.append(row_spec(left, rows, blk, block, turn))
            ins.extend(row_spec(r, rows, r.shape[1], lambda j, u: 0, right_turn) for r in rights)
        plan.append(terms)
    width = sum(r.shape[1] for group in groups for r in group[0][2])

    def body(u, *refs):
        out, col = refs[-1], 0
        for terms in plan:
            lefts = [refs[at][...] for at, _ in terms]
            for i in range(terms[0][1]):
                total = 0.0
                for (at, _), left_rows in zip(terms, lefts):
                    total = total + dotf(left_rows, refs[at + 1 + i][...], TN)
                out[:, col : col + total.shape[1]] = total.astype(jnp.bfloat16)
                col += total.shape[1]

    return stage(
        line, "weight_grad", body, (n,), upper, ins,
        [(jax.ShapeDtypeStruct((half, width), jnp.bfloat16), spec((blk, width), lambda j, u: (j, 0)))],
    )


def norm_back_own(line, kept, got, source, base, gain, start):
    rows, cols = kept.shape
    blk = min(rows, 128)
    n = rows // blk

    def body(s, k, g, x, b, gain_ref, out, low, sums):
        grad = k[...].astype(jnp.float32) + g[...].astype(jnp.float32)
        center = x[...].astype(jnp.float32)
        center = center - jnp.mean(center, axis=1, keepdims=True)
        scaled = lax.rsqrt(jnp.mean(center * center, axis=1, keepdims=True) + epsilon)
        normal = center * scaled
        moved = b[...].astype(jnp.float32) + norm_back(grad, normal, scaled, gain_ref[...])
        out[...] = moved
        low[...] = moved.astype(jnp.bfloat16)

        @pl.when(pl.program_id(0) == 0)
        def _():
            sums[...] = jnp.zeros_like(sums)

        sums[0:1, :] += jnp.sum(grad * normal, axis=0, keepdims=True)
        sums[1:2, :] += jnp.sum(grad, axis=0, keepdims=True)

    flat = lambda j, s: (j, 0)
    at = lambda j, s: (s[0] // blk + j, 0)
    base_at = at if base.shape[0] != rows else flat
    source_at = at if source.shape[0] != rows else flat
    whole = spec((blk, cols), flat)
    return stage(
        line, "norm_back", body, (n,), start,
        [
            (kept, whole), (got, whole), (source, spec((blk, cols), source_at)), (base, spec((blk, cols), base_at)),
            (gain.reshape(1, cols), spec((1, cols), lambda j, s: (0, 0))),
        ],
        [
            (jax.ShapeDtypeStruct((rows, cols), jnp.float32), whole),
            (jax.ShapeDtypeStruct((rows, cols), jnp.bfloat16), whole),
            (jax.ShapeDtypeStruct((8, cols), jnp.float32), spec((8, cols), lambda j, s: (0, 0))),
        ],
    )


def add_own(line, kept, got, source):
    rows, cols = kept.shape
    blk = min(rows, 128)
    flat = lambda j, s: (j, 0)

    def body(s, k, g, x, out):
        total = k[...].astype(jnp.float32) + g[...].astype(jnp.float32)
        out[...] = (x[...] + total).astype(jnp.bfloat16)

    whole = spec((blk, cols), flat)
    return stage(
        line, "add_own", body, (rows // blk,), 0,
        [(kept, whole), (got, whole), (source, whole)],
        [(jax.ShapeDtypeStruct((rows, cols), jnp.bfloat16), whole)],
    )


def fixed(x):
    return (x, spec(x.shape, lambda *a: (0, 0)))


def row(x):
    return x.reshape(1, x.shape[0])


def norm_qkv(line, tokens, gain, shift, weights):
    rows, features = tokens.shape
    blk = min(rows, 256)
    flat = lambda j, u: (j, 0)
    outs = [jax.ShapeDtypeStruct((rows, features), jnp.bfloat16)]
    outs += [jax.ShapeDtypeStruct((rows, w.shape[1]), jnp.bfloat16) for w in weights]

    def body(u, token_ref, gain_ref, shift_ref, *refs):
        count = len(weights)
        for part in range(2):
            at = slice(part * blk // 2, (part + 1) * blk // 2)
            normed = norm_parts(token_ref[at, :].astype(jnp.float32), gain_ref[...], shift_ref[...])[2].astype(jnp.bfloat16)
            refs[count][at, :] = normed
            for w, out in zip(refs[:count], refs[count + 1 :]):
                out[at, :] = dotf(normed, w[...]).astype(jnp.bfloat16)

    return stage(
        line, "norm_qkv", body, (rows // blk,), 0,
        [(tokens, spec((blk, features), flat)), fixed(row(gain)), fixed(row(shift))] + [fixed(w) for w in weights],
        [(out, spec((blk, out.shape[1]), flat)) for out in outs],
    )


def project_out(line, start, own, parts, weights, tokens, gain, shift):
    rows, features = tokens.shape
    blk = min(rows, 256)
    flat = lambda j, u: (j, 0)
    pieces = [x for part in parts for x in part]
    depth = sum(w.shape[0] for w in weights)
    ins = [(tokens, spec((blk, features), flat)), fixed(row(gain)), fixed(row(shift))]
    ins += [fixed(w) for w in weights]
    ins += [(x, spec((blk, x.shape[1]), flat)) for x in pieces]

    def body(u, *refs):
        token_ref, gain_ref, shift_ref = refs[:3]
        total_ref, normed_ref, weight = refs[-3:]
        at = 3 + len(weights)

        @pl.when(pl.program_id(0) == 0)
        def _():
            top = 0
            for ref in refs[3:at]:
                weight[top : top + ref.shape[0], :] = ref[...]
                top += ref.shape[0]

        for part in range(2):
            here = slice(part * blk // 2, (part + 1) * blk // 2)
            left = jnp.concatenate([r[here, :] for r in refs[at : at + len(pieces)]], axis=1)
            total = token_ref[here, :].astype(jnp.float32) + dotf(left, weight[...])
            first = pl.program_id(0) * blk + part * (blk // 2) - u[0]

            @pl.when(jnp.logical_and(first >= 0, first < own))
            def _():
                total_ref[pl.ds(pl.multiple_of(first, 16), blk // 2), :] = total

            normed_ref[here, :] = norm_parts(total, gain_ref[...], shift_ref[...])[2].astype(jnp.bfloat16)

    whole = spec((blk, features), flat)
    return stage(
        line, "project_out", body, (rows // blk,), start, ins,
        [
            (jax.ShapeDtypeStruct((own, features), jnp.float32), spec((own, features), lambda j, u: (0, 0))),
            (jax.ShapeDtypeStruct((rows, features), jnp.bfloat16), whole),
        ],
        scratch=[pltpu.VMEM((depth, features), jnp.bfloat16)],
    )


def turn_rows(rows, blk, turn):
    n = rows // 2 // blk
    if turn:
        return lambda j, u: (u[0] * n + j, 0)
    return lambda j, u: ((1 - u[0]) * n + j, 0)


def feed_forward(line, upper, turn, normed, cotangent, up, down, count):
    rows, features = normed.shape
    hidden = up.shape[1]
    blk = min(rows // 2, 256)
    at = turn_rows(rows, blk, turn)
    flat = lambda j, u: (j, 0)

    def body(u, normed_ref, cot_ref, up_ref, down_ref, active_ref, inner_ref, *back_refs):
        for part in range(2):
            here = slice(part * blk // 2, (part + 1) * blk // 2)
            gelu, slope = gelu_pair(dotf(normed_ref[here, :], up_ref[...]))
            active_ref[here, :] = gelu.astype(jnp.bfloat16)
            grad = (dotf(cot_ref[here, :], down_ref[...], NT) * slope).astype(jnp.bfloat16)
            inner_ref[here, :] = grad
            put([r.at[here, :] for r in back_refs], dotf(grad, up_ref[...], NT))

    outs = pieces_of(rows // 2, 2 * hidden, 2) + pieces_of(rows // 2, features, count)
    return stage(
        line, "feed_forward", body, (rows // 2 // blk,), upper,
        columns([normed, cotangent], blk, at) + [fixed(up), fixed(down)],
        [(out, spec((blk, out.shape[1]), flat)) for out in outs],
    )


def product(line, left, right, count):
    rows = left.shape[0]
    blk = min(rows, 256)
    flat = lambda j, u: (j, 0)

    def body(u, l, r, *outs):
        put(outs, dotf(l[...], r[...]))

    made = stage(
        line, "product", body, (rows // blk,), 0,
        columns([left], blk, flat) + [fixed(right)],
        [(x, spec((blk, x.shape[1]), flat)) for x in pieces_of(rows, right.shape[1], count)],
    )
    return made if count > 1 else [made]


def product_back(line, upper, turn, lefts, rights, pieces):
    rows = lefts[0][0].shape[0]
    features, width = rights[0].shape
    blk = min(rows // 2, 256)
    at = turn_rows(rows, blk, turn)
    flat = [x for left in lefts for x in left]

    def body(u, *refs):
        weight = refs[-1]

        @pl.when(pl.program_id(0) == 0)
        def _():
            for i, r in enumerate(refs[len(flat) : len(flat) + len(rights)]):
                weight[:, i * width : (i + 1) * width] = r[...]

        put(refs[len(flat) + len(rights) : -1], dotf(cat(refs[: len(flat)]), weight[...], NT))

    made = stage(
        line, "product_back", body, (rows // 2 // blk,), upper,
        columns(flat, blk, at) + [fixed(r) for r in rights],
        [(x, spec((blk, x.shape[1]), lambda j, u: (j, 0))) for x in pieces_of(rows // 2, features, pieces)],
        scratch=[pltpu.VMEM((features, len(rights) * width), jnp.bfloat16)],
    )
    return made if pieces > 1 else [made]


def add_small(line, mine, got):
    def body(u, m, g, out):
        out[...] = m[...] + g[...]

    return stage(line, "add_small", body, (1,), 0, [fixed(mine), fixed(got)], [(jax.ShapeDtypeStruct(mine.shape, mine.dtype), fixed(mine)[1])])


def shards(
    n_dp,
    n_tp,
    tokens,
    query_weight,
    key_weight,
    value_weight,
    out_weight,
    up_weight,
    down_weight,
    bias_table,
    gain_one,
    shift_one,
    gain_two,
    shift_two,
    single_item,
    cotangent,
):
    tp_bits = index_bits(n_tp)
    dp_bits = index_bits(n_dp)
    far_first = tp_bits[1:] + tp_bits[:1]
    low = jnp.bfloat16
    full = jnp.float32
    row_count, features = tokens.shape
    head_count = bias_table.shape[1]
    width = head_count * HD
    tp_up = [rank_bit("tp", bit) for bit in tp_bits]
    dp_up = [rank_bit("dp", bit) for bit in dp_bits]
    start, own_count = own_start("tp", tp_bits, row_count)

    def tp_swap(values, i):
        return swap(values, "tp", n_tp, tp_bits[i])

    def dp_swap(values, i):
        return swap(values, "dp", n_dp, dp_bits[i])

    line = []

    class Sum:
        def __init__(self, axis, send, keep):
            self.axis = axis
            self.up = tp_up if axis == "tp" else dp_up
            self.keep, self.at = keep, 0
            self.swap(send)

        def swap(self, arrays):
            self.got = [(tp_swap if self.axis == "tp" else dp_swap)(x, self.at) for x in arrays]

        def count(self, at):
            return PIECES if self.axis == "tp" and at == 0 else 1

        def halve(self):
            self.at += 1
            send, self.keep = split_add(line, self.up[self.at], self.keep, self.got, self.count(self.at))
            self.swap(send)

        def spread(self, values):
            self.keep = values
            self.swap(values)

        def total(self):
            self.spread([add_up(line, self.keep[0], self.got[0])])
            for _ in range(len(self.up) - 3):
                self.double()

        def fan(self):
            joined = join_rows(line, self.up[self.at], self.keep, self.got, low) if self.at > 1 else self.keep
            self.mine = joined[0]
            self.near = dp_swap(self.mine, 1)
            self.far = [dp_swap(self.mine, 0), dp_swap(self.near, 0)]

        def finish(self, outs):
            return join_four(line, self.up[:2], [self.mine, self.near] + self.far, outs)

        def double(self, dtype=low):
            count = self.count(self.at - 1) if self.at else 1
            joined = join_rows(line, self.up[self.at], self.keep, self.got, dtype, count)
            if self.at == 0:
                return joined[0]
            self.at -= 1
            self.spread(joined)

    out_parts = gather_parts(out_weight, "tp", n_tp, far_first)
    near_rows = near_bias(bias_table)
    normed_low, queries, key_rows, value_rows = norm_qkv(
        line, tokens, gain_one, shift_one, [query_weight, key_weight, value_weight]
    )
    pairs = width // (2 * HD)
    attended, lse_rows, parts = [], [], []
    for pair in range(pairs):
        also = [out_parts[far_first[0]][:8, :128]] if pair == pairs - 1 else ()
        columns, sums = attn_forward(
            line, pair, single_item, near_rows, queries, key_rows, value_rows, also
        )
        attended.append(columns)
        lse_rows.append(sums)
        parts.append(gather_parts(columns, "tp", n_tp, far_first))
    parts = [[parts[pair][k] for pair in range(pairs)] for k in range(n_tp)]
    residual, normed_two_low = project_out(
        line, start, own_count, parts, out_parts, tokens, gain_two, shift_two
    )
    fed = [
        feed_forward(line, tp_up[0], turn, normed_two_low, cotangent, up_weight, down_weight, PIECES)
        for turn in (0, 1)
    ]
    two = Sum("tp", fed[0][2:], fed[1][2:])
    ups = [dp_up[0], tp_up[0]]
    down_group = [[(fed[turn][0], turn, [cotangent], turn) for turn in (0, 1)]]
    up_group = [[(normed_two_low, turn, [fed[turn][1]], turn) for turn in (0, 1)]]

    def halve_to_last(total, done):
        for _ in range(len(total.up) - 1 - done):
            total.halve()

    halve_to_last(two, 0)
    down_send = weight_grad(line, ups, True, down_group)
    down_keep = weight_grad(line, ups, False, down_group)
    down = Sum("dp", [down_send], [down_keep])
    ffn = Sum("tp", *[product(line, fed[turn][0], down_weight, PIECES) for turn in (0, 1)])
    up_keep = weight_grad(line, ups, False, up_group)
    grad_residual, grad_residual_low, sums_two = norm_back_own(
        line, two.keep[0], two.got[0], residual, cotangent, gain_two, start
    )
    two.spread([grad_residual_low])
    down.halve()
    up_send = weight_grad(line, ups, True, up_group)
    up = Sum("dp", [up_send], [up_keep])
    for _ in tp_bits[1:]:
        two.double()
    halve_to_last(ffn, 0)
    grad_residual_low = two.double()

    backs = []
    for pair in range(pairs):
        if pair == 1:
            halve_to_last(down, 1)
        backs.append(
            attn_backward(
                line, pair, single_item, near_rows, queries, key_rows, value_rows,
                attended[pair], lse_rows[pair], grad_residual_low, out_weight,
            )
        )
    if pairs == 1:
        halve_to_last(down, 1)
    grad_query, grad_key, grad_value, near_totals = zip(*backs)
    grad_table = table_grad(jnp.stack(near_totals), head_count)
    heads_back = [list(grad_query), list(grad_key), list(grad_value)]
    head_weights = [query_weight, key_weight, value_weight]
    ffn.spread([add_own(line, ffn.keep[0], ffn.got[0], residual)])
    one = Sum("tp", *[product_back(line, tp_up[0], turn, heads_back, head_weights, PIECES) for turn in (0, 1)])
    up.halve()
    mixed_group = [
        [(normed_low, None, heads_back[2], None)],
        [(grad_residual_low, None, attended, None)],
    ]
    heads_group = [[(normed_low, None, heads_back[0] + heads_back[1], None)]]
    mixed_send = weight_grad(line, ups, True, mixed_group)
    halve_to_last(one, 0)
    down.total()
    mixed = Sum("dp", [mixed_send], [weight_grad(line, ups, False, mixed_group)])
    heads_send = weight_grad(line, ups, True, heads_group)
    heads_keep = weight_grad(line, ups, False, heads_group)
    halve_to_last(up, 1)
    down.fan()
    _, grad_tokens, sums_one = norm_back_own(
        line, one.keep[0], one.got[0], tokens, grad_residual, gain_one, start
    )
    one.spread([grad_tokens])
    mixed.halve()
    heads = Sum("dp", [heads_send], [heads_keep])

    table_size = NB * head_count
    slot = jnp.zeros((n_tp * table_size,), full)
    me_tp = lax.axis_index("tp")
    slot = lax.dynamic_update_slice(slot, grad_table.reshape(table_size), (me_tp * table_size,))
    slot = jnp.pad(slot, (0, -slot.size % features)).reshape(-1, features)
    small = [jnp.concatenate([sums_one[:2], sums_two[:2], slot])]
    steps = [("dp", n_dp, bit) for bit in dp_bits] + [("tp", n_tp, bit) for bit in tp_bits]

    def small_step():
        if steps:
            axis, count, bit = steps.pop(0)
            small[0] = add_small(line, small[0], swap(small[0], axis, count, bit))

    up.total()
    for _ in tp_bits[1:]:
        ffn.double()
    small_step()
    halve_to_last(mixed, 1)
    heads.halve()
    small_step()
    for _ in tp_bits[1:]:
        one.double()
    result = ffn.double()
    small_step()
    up.fan()
    mixed.total()
    small_step()
    grad_down = down.finish([(0, features, False)])
    halve_to_last(heads, 1)
    small_step()
    grad_tokens = one.double(full)
    mixed.fan()
    heads.total()
    grad_up = up.finish([(0, up_weight.shape[1], False)])
    heads.fan()
    while steps:
        small_step()
    grad_vw, grad_out = mixed.finish([(0, width, False), (width, width, True)])
    grad_qw, grad_kw = heads.finish([(0, width, False), (width, width, False)])
    small = small[0]
    grad_table = lax.dynamic_slice(
        small[4:].reshape(-1), (me_tp * table_size,), (table_size,)
    ).reshape(NB, head_count)
    return (
        result,
        grad_tokens,
        grad_qw,
        grad_kw,
        grad_vw,
        grad_out,
        grad_up,
        grad_down,
        grad_table,
        small[0],
        small[1],
        small[2],
        small[3],
    )


def solution(mesh):
    placed = (
        P("dp", None),
        P(None, "tp"),
        P(None, "tp"),
        P(None, "tp"),
        P("tp", None),
        P(None, "tp"),
        P("tp", None),
        P(None, "tp"),
        P(),
        P(),
        P(),
        P(),
        P("dp"),
        P("dp", None),
    )
    return jax.shard_map(
        functools.partial(shards, mesh.shape["dp"], mesh.shape["tp"]),
        mesh=mesh,
        in_specs=placed,
        out_specs=(
            P("dp", None),
            P("dp", None),
            P(None, "tp"),
            P(None, "tp"),
            P(None, "tp"),
            P("tp", None),
            P(None, "tp"),
            P("tp", None),
            P(None, "tp"),
            P(),
            P(),
            P(),
            P(),
        ),
        check_vma=False,
    )
```

```python
import functools
import math

import jax
import jax.numpy as jnp
from jax import lax
from jax.experimental import pallas as pl
from jax.experimental.pallas import tpu as pltpu
from jax.sharding import PartitionSpec as P

HD = 64
NB = 32
MAXDIST = 128


epsilon = 1e-05
FRONT = {"norm_qkv": 3.5, "attn_forward": 4.5, "project_out": 6.0, "feed_forward": 7.0}
REST = {"split_add": 1.5, "join_rows": 2.0, "weight_grad": 3.0, "norm_back": 2.0, "product": 1.5, "product_back": 1.5, "attn_backward": 7.0, "add_own": 1.3, "add_up": 1.0, "join_four": 4.0, "add_small": 0.5}


def cost_of(name):
    us = FRONT[name] * 1.000000 if name in FRONT else REST[name] * 0.300000
    return pl.CostEstimate(flops=max(1, int(us * 1.15e9)), bytes_accessed=1, transcendentals=0)

VMEM_LIMIT = 32 * 1024 * 1024
PIECES = 2


def thresholds_list():
    exact_count = NB // 2
    thresholds = []
    for bucket in range(1, NB):
        if bucket <= exact_count:
            thresholds.append(bucket)
        else:
            thresholds.append(
                int(
                    math.ceil(
                        exact_count
                        * (MAXDIST / exact_count) ** ((bucket - exact_count) / exact_count)
                    )
                )
            )
    return thresholds


def distance_onehot(count):
    distance = jnp.arange(count, dtype=jnp.int32)
    buckets = jnp.zeros((count,), jnp.int32)
    for threshold in thresholds_list():
        buckets = buckets + (distance >= threshold).astype(jnp.int32)
    return (buckets[:, None] == jnp.arange(NB, dtype=jnp.int32)[None, :]).astype(jnp.float32)


def norm_parts(values, gain, shift):
    center = values - jnp.mean(values, axis=-1, keepdims=True)
    scaled = lax.rsqrt(jnp.mean(center * center, axis=-1, keepdims=True) + epsilon)
    normal = center * scaled
    return (normal, scaled, normal * gain + shift)


def norm_back(grad_out, normal, scaled, gain):
    grad_norm = grad_out * gain
    inner_mean = jnp.mean(grad_norm * normal, axis=-1, keepdims=True)
    return scaled * (grad_norm - jnp.mean(grad_norm, axis=-1, keepdims=True) - normal * inner_mean)


def gelu_pair(values):
    bell = jnp.exp(-0.5 * values * values)
    t = 1.0 / (1.0 + (0.3275911 * math.sqrt(0.5)) * jnp.abs(values))
    poly = 0.5 * 1.061405429
    for factor in (-1.453152027, 1.421413741, -0.284496736, 0.254829592):
        poly = poly * t + 0.5 * factor
    tail = poly * t * bell
    cdf = jnp.where(values < 0.0, tail, 1.0 - tail)
    return values * cdf, cdf + values * bell * (1.0 / math.sqrt(2.0 * math.pi))


BLK = 256
NEAR = 128
NEG = -1000000000.0
NT = (((1,), (1,)), ((), ()))
TN = (((0,), (0,)), ((), ()))


def dotf(a, b, dims=(((1,), (0,)), ((), ()))):
    return lax.dot_general(a, b, dims, preferred_element_type=jnp.float32)


def fill_bias(g_ref, bias_ref):
    row = lax.broadcasted_iota(jnp.int32, (2 * NEAR, NEAR), 0)
    col = lax.broadcasted_iota(jnp.int32, (2 * NEAR, NEAR), 1)
    hidden = row - NEAR > col
    for h in range(2):
        spread = jnp.broadcast_to(g_ref[h : h + 1, :], (2 * NEAR, 2 * NEAR))
        tile = pltpu.roll(spread, 0, 1, stride=1, stride_axis=0)[:, :NEAR]
        tile = jnp.where(hidden, NEG, tile)
        bias_ref[h, : 2 * NEAR, :NEAR] = tile
        bias_ref[h, 2 * NEAR :, :NEAR] = jnp.full((NEAR, NEAR), NEG, jnp.float32)
        bias_ref[h, :NEAR, NEAR:] = jnp.zeros((NEAR, NEAR), jnp.float32)
        bias_ref[h, NEAR:, NEAR:] = tile


def head_mask(x, h):
    lane = lax.broadcasted_iota(jnp.int32, x.shape, 1)
    return jnp.where((lane < HD) == (h == 0), x, jnp.zeros_like(x))


def add_near(st, bias_ref, h, low, blk):
    near = max(blk * BLK - NEAR, low)
    top = near - low
    tile = bias_ref[h, near - (blk * BLK - NEAR) :, :]
    if top == 0:
        return st + tile
    return jnp.concatenate([st[:top], st[top:] + tile], axis=0)


def each_block(row_count, single_ref, work):
    half = row_count // 2
    single = single_ref[0] == 1
    for blk in range(row_count // BLK):
        if blk * BLK < half:
            work(blk, 0)
        else:
            pl.when(single)(functools.partial(work, blk, 0))
            pl.when(jnp.logical_not(single))(functools.partial(work, blk, half))


def attn_fwd_kernel(single_ref, g_ref, q_ref, k_ref, v_ref, o_ref, lse_ref, bias_ref, vt_ref):
    row_count = q_ref.shape[0]
    fill_bias(g_ref, bias_ref)
    vt_ref[...] = v_ref[...].T

    def work(blk, low):
        high = (blk + 1) * BLK
        rows = slice(blk * BLK, high)
        q = q_ref[rows, :] * jnp.asarray(HD ** (-0.5), jnp.bfloat16)
        outs = []
        for h in range(2):
            st = dotf(k_ref[low:high, :], head_mask(q, h), NT)
            st = add_near(st, bias_ref, h, low, blk)
            m = jnp.max(st, axis=0, keepdims=True)
            p = jnp.exp(st - m)
            total = jnp.sum(p, axis=0, keepdims=True)
            ot = dotf(vt_ref[h * HD : (h + 1) * HD, low:high], p.astype(jnp.bfloat16))
            outs.append(ot / total)
            lse_ref[h : h + 1, rows] = m + jnp.log(total)
        o_ref[rows, :] = jnp.concatenate(outs, axis=0).T.astype(jnp.bfloat16)

    each_block(row_count, single_ref, work)


def attn_bwd_kernel(
    single_ref, g_ref, q_ref, k_ref, v_ref, o_ref, lse_ref, gr_ref, w_ref,
    dq_ref, dk_ref, dv_ref, near_ref, bias_ref, kt_ref, dk_acc, dv_acc, near_acc,
):
    row_count = q_ref.shape[0]
    fill_bias(g_ref, bias_ref)
    kt_ref[...] = k_ref[...].T
    dk_acc[...] = jnp.zeros_like(dk_acc)
    dv_acc[...] = jnp.zeros_like(dv_acc)
    near_acc[...] = jnp.zeros_like(near_acc)

    def work(blk, low):
        high = (blk + 1) * BLK
        rows = slice(blk * BLK, high)
        q = q_ref[rows, :] * jnp.asarray(HD ** (-0.5), jnp.bfloat16)
        da = dotf(gr_ref[rows, :], w_ref[...], NT).astype(jnp.bfloat16)
        prod_t = (da.astype(jnp.float32) * o_ref[rows, :].astype(jnp.float32)).T
        ps, dss, qms, dams, dqts = [], [], [], [], []
        for h in range(2):
            qm, dam = head_mask(q, h), head_mask(da, h)
            st = dotf(k_ref[low:high, :], qm, NT)
            st = add_near(st, bias_ref, h, low, blk)
            p = jnp.exp(st - lse_ref[h : h + 1, rows])
            dpt = dotf(v_ref[low:high, :], dam, NT)
            dd = jnp.sum(prod_t[h * HD : (h + 1) * HD], axis=0, keepdims=True)
            ds = p * (dpt - dd)
            own = blk * BLK - low
            if own:
                near_acc[h] += ds[own - NEAR : own + NEAR, :NEAR]
            else:
                near_acc[h, NEAR:] += ds[:NEAR, :NEAR]
            near_acc[h] += ds[own : own + 2 * NEAR, NEAR:]
            dsb = ds.astype(jnp.bfloat16)
            ps.append(p.astype(jnp.bfloat16))
            dss.append(dsb)
            qms.append(qm)
            dams.append(dam)
            dqts.append(dotf(kt_ref[h * HD : (h + 1) * HD, low:high], dsb))
        dv_acc[low:high] += dotf(jnp.concatenate(ps, axis=1), jnp.concatenate(dams, axis=0))
        dk_acc[low:high] += dotf(jnp.concatenate(dss, axis=1), jnp.concatenate(qms, axis=0))
        dq = jnp.concatenate(dqts, axis=0).T * HD ** (-0.5)
        dq_ref[rows, :] = dq.astype(jnp.bfloat16)

    each_block(row_count, single_ref, work)
    dk_ref[...] = dk_acc[...].astype(jnp.bfloat16)
    dv_ref[...] = dv_acc[...].astype(jnp.bfloat16)
    near_ref[...] = jnp.zeros_like(near_ref)
    for h in range(2):
        acc = jnp.concatenate([near_acc[h], jnp.zeros((2 * NEAR, NEAR), jnp.float32)], axis=1)
        row = lax.broadcasted_iota(jnp.int32, acc.shape, 0)
        for bit in range((2 * NEAR - 1).bit_length()):
            moved = pltpu.roll(acc, 2 * NEAR - (1 << bit), 1)
            acc = jnp.where((row & (1 << bit)) != 0, moved, acc)
        near_ref[h : h + 1, :] = jnp.sum(acc, axis=0, keepdims=True)


def pair_specs(row_count, first):
    smem = pl.BlockSpec(memory_space=pltpu.SMEM)
    cols = pl.BlockSpec((row_count, 2 * HD), lambda p: (0, first + p))
    near = pl.BlockSpec((None, 8, 2 * NEAR), lambda p: (first + p, 0, 0))
    lse = pl.BlockSpec((None, 8, row_count), lambda p: (first + p, 0, 0))
    return smem, cols, near, lse


def held(arrays):
    return [pl.BlockSpec(memory_space=pl.ANY)] * len(arrays)


def attn_forward(line, pair, single_item, g, q, k, v, also=()):
    row_count = q.shape[0]
    after = line + list(also)
    smem, cols, near, _ = pair_specs(row_count, pair)
    own = pl.BlockSpec((row_count, 2 * HD), lambda p: (0, 0))
    lse = pl.BlockSpec((8, row_count), lambda p: (0, 0))

    def kernel(*refs):
        attn_fwd_kernel(*refs[:5], *refs[5 + len(after) :])

    attended, lse_rows = pl.pallas_call(
        kernel,
        grid=(1,),
        in_specs=[smem, near, cols, cols, cols] + held(after),
        out_specs=[own, lse],
        out_shape=[
            jax.ShapeDtypeStruct((row_count, 2 * HD), jnp.bfloat16),
            jax.ShapeDtypeStruct((8, row_count), jnp.float32),
        ],
        scratch_shapes=[
            pltpu.VMEM((2, 3 * NEAR, BLK), jnp.float32),
            pltpu.VMEM((2 * HD, row_count), jnp.bfloat16),
        ],
        compiler_params=pltpu.CompilerParams(vmem_limit_bytes=VMEM_LIMIT),
        cost_estimate=cost_of("attn_forward"),
        name="attn_forward",
    )(single_item, g, q, k, v, *after)
    line[:] = [lse_rows]
    return attended, lse_rows


def attn_backward(line, pair, single_item, g, q, k, v, o, lse_rows, grad, out_weight):
    row_count = q.shape[0]
    after = list(line)
    smem, cols, near, _ = pair_specs(row_count, pair)
    own = pl.BlockSpec((row_count, 2 * HD), lambda p: (0, 0))
    lse = pl.BlockSpec((8, row_count), lambda p: (0, 0))
    near_out = pl.BlockSpec((8, 2 * NEAR), lambda p: (0, 0))
    flat = jax.ShapeDtypeStruct((row_count, 2 * HD), jnp.bfloat16)

    def kernel(*refs):
        attn_bwd_kernel(*refs[:9], *refs[9 + len(after) :])

    *grads, near_totals = pl.pallas_call(
        kernel,
        grid=(1,),
        in_specs=[smem, near, cols, cols, cols, own, lse]
        + [
            pl.BlockSpec(grad.shape, lambda p: (0, 0)),
            pl.BlockSpec((2 * HD, grad.shape[1]), lambda p: (pair, 0)),
        ]
        + held(after),
        out_specs=[own, own, own, near_out],
        out_shape=[flat, flat, flat, jax.ShapeDtypeStruct((8, 2 * NEAR), jnp.float32)],
        scratch_shapes=[
            pltpu.VMEM((2, 3 * NEAR, BLK), jnp.float32),
            pltpu.VMEM((2 * HD, row_count), jnp.bfloat16),
            pltpu.VMEM((row_count, 2 * HD), jnp.float32),
            pltpu.VMEM((row_count, 2 * HD), jnp.float32),
            pltpu.VMEM((2, 2 * NEAR, NEAR), jnp.float32),
        ],
        compiler_params=pltpu.CompilerParams(vmem_limit_bytes=VMEM_LIMIT),
        cost_estimate=cost_of("attn_backward"),
        name="attn_backward",
    )(single_item, g, q, k, v, o, lse_rows, grad, out_weight, *after)
    line[:] = [near_totals]
    return *grads, near_totals


def near_bias(bias_table):
    head_count = bias_table.shape[1]
    rows = jnp.dot(
        distance_onehot(NEAR), bias_table - bias_table[NB - 1 :],
        precision=lax.Precision.HIGHEST, preferred_element_type=jnp.float32,
    ).T
    rows = jnp.pad(rows, ((0, 0), (NEAR, 0))).reshape(head_count // 2, 2, 2 * NEAR)
    return jnp.pad(rows, ((0, 0), (0, 6), (0, 0)))


def table_grad(near, head_count):
    by_dist = near[:, :2, NEAR:].reshape(head_count, NEAR)
    grad = jnp.dot(
        by_dist, distance_onehot(NEAR)[:, : NB - 1],
        precision=lax.Precision.HIGHEST, preferred_element_type=jnp.float32,
    )
    return jnp.concatenate([grad, -jnp.sum(grad, axis=1, keepdims=True)], axis=1).T


def index_bits(count):
    return [1 << i for i in range(count.bit_length() - 1)]


def far(x):
    return pltpu.with_memory_space_constraint(x, pltpu.HBM)


def keep_far(x):
    return x


def swap(values, axis, count, bit):
    return lax.ppermute(values, axis, [(i, i ^ bit) for i in range(count)])


def rank_bit(axis, bit):
    return (lax.axis_index(axis) // bit) % 2


def gather_parts(values, axis, count, bits):
    parts = {0: values}
    for bit in bits:
        for k in list(parts):
            parts[k ^ bit] = swap(parts[k], axis, count, bit)
    return [parts[k] for k in range(count)]


def own_start(axis, bits, size):
    start = 0
    for bit in bits:
        size //= 2
        start = start + rank_bit(axis, bit) * size
    return start, size


def sum_over(values, axis, count, bits):
    for bit in bits:
        values = values + swap(values, axis, count, bit)
    return values


def spec(shape, index):
    return pl.BlockSpec(shape, index)


def scalars(values):
    values = values if isinstance(values, list) else [values]
    return jnp.stack([jnp.asarray(v, jnp.int32) for v in values])


def stage(line, name, body, grid, upper, ins, outs, scratch=(), also=()):
    after = line + list(also)
    shapes = [shape for shape, _ in outs] + [jax.ShapeDtypeStruct((8, 128), jnp.float32)]
    token = pl.BlockSpec((8, 128), lambda *a: (0, 0))
    held = pl.BlockSpec(memory_space=pl.ANY)

    def kernel(upper_ref, *refs):
        used = refs[: len(ins)]
        rest = refs[len(ins) + len(after) :]
        body(upper_ref, *used, *rest[: len(outs)], *rest[len(outs) + 1 :])
        rest[len(outs)][...] = jnp.zeros((8, 128), jnp.float32)

    *results, mark = pl.pallas_call(
        kernel,
        grid_spec=pltpu.PrefetchScalarGridSpec(
            num_scalar_prefetch=1,
            grid=grid,
            in_specs=[where for _, where in ins] + [held] * len(after),
            out_specs=[where for _, where in outs] + [token],
            scratch_shapes=list(scratch),
        ),
        out_shape=shapes,
        compiler_params=pltpu.CompilerParams(vmem_limit_bytes=VMEM_LIMIT),
        cost_estimate=cost_of(name),
        name=name,
    )(scalars(upper), *[x for x, _ in ins], *after)
    line[:] = [mark]
    return results if len(results) > 1 else results[0]


def cat(refs):
    return refs[0][...] if len(refs) == 1 else jnp.concatenate([r[...] for r in refs], axis=1)


def put(refs, values):
    at = 0
    for ref in refs:
        size = ref.shape[1]
        ref[...] = values[:, at : at + size].astype(ref.dtype)
        at += size


def columns(arrays, blk, index):
    return [(x, spec((blk, x.shape[1]), index)) for x in arrays]


def pieces_of(rows, cols, count, dtype=jnp.bfloat16):
    return [jax.ShapeDtypeStruct((rows, cols // count), dtype)] * count


def split_add(line, upper, kept, got, count=1):
    rows, cols = got[0].shape[0], sum(x.shape[1] for x in got)
    half = rows // 2
    blk = min(half, 128)
    n = half // blk
    a, b = len(kept), len(got)

    def body(u, *refs):
        for at, outs in ((0, refs[2 * a + 2 * b : -1]), (a + b, refs[-1:])):
            total = cat(refs[at : at + a]).astype(jnp.float32)
            put(outs, total + cat(refs[at + a : at + a + b]).astype(jnp.float32))

    away = lambda j, u: ((1 - u[0]) * n + j, 0)
    here = lambda j, u: (u[0] * n + j, 0)
    outs = pieces_of(half, cols, count) + pieces_of(half, cols, 1)
    *send, keep = stage(
        line, "split_add", body, (n,), upper,
        columns(kept + got, blk, away) + columns(kept + got, blk, here),
        [(x, spec((blk, x.shape[1]), lambda j, u: (j, 0))) for x in outs],
    )
    return send, [keep]


def add_up(line, kept, got):
    rows, cols = kept.shape
    blk = min(rows, 128)
    flat = lambda j, u: (j, 0)

    def body(u, k, g, out):
        out[...] = (k[...].astype(jnp.float32) + g[...].astype(jnp.float32)).astype(out.dtype)

    where = spec((blk, cols), flat)
    return stage(
        line, "add_up", body, (rows // blk,), 0, [(kept, where), (got, where)],
        [(jax.ShapeDtypeStruct(kept.shape, jnp.bfloat16), where)],
    )


def join_rows(line, upper, mine, got, dtype, count=1):
    rows, cols = mine[0].shape[0], sum(x.shape[1] for x in mine)
    blk = min(rows, 256)
    n = rows // blk
    a = len(mine)

    def body(u, *refs):
        i = pl.program_id(0)

        @pl.when(i == 0)
        def _():
            put(refs[2 * a :], cat(refs[:a]))

        @pl.when(i == 1)
        def _():
            put(refs[2 * a :], cat(refs[a : 2 * a]))

    joined = stage(
        line, "join_rows", body, (2, n), upper,
        columns(mine, blk, lambda i, j, u: (jnp.where(i == 0, j, n - 1), 0))
        + columns(got, blk, lambda i, j, u: (jnp.where(i == 0, 0, j), 0)),
        [
            (x, spec((blk, x.shape[1]), lambda i, j, u: (jnp.where(i == 0, u[0], 1 - u[0]) * n + j, 0)))
            for x in pieces_of(2 * rows, cols, count, dtype)
        ],
    )
    return joined if count > 1 else [joined]


def join_four(line, uppers, pieces, outs):
    rows, cols = pieces[0].shape
    blk = min(rows, 128)
    n = rows // blk

    def body(u, *refs):
        for p in range(4):

            @pl.when(pl.program_id(0) == p)
            def _():
                for out, (first, size, turned) in zip(refs[4:], outs):
                    x = refs[p][:, first : first + size].astype(jnp.float32)
                    out[...] = x.T if turned else x

    def place(i, j, u):
        high = jnp.where(i < 2, u[0], 1 - u[0])
        return (high * 2 + jnp.where(i % 2 == 0, u[1], 1 - u[1])) * n + j

    def turn(p):
        return lambda i, j, u: (jnp.where(i == p, j, jnp.where(i < p, 0, n - 1)), 0)

    results = []
    for _, size, turned in outs:
        if turned:
            results.append((jax.ShapeDtypeStruct((size, 4 * rows), jnp.float32), spec((size, blk), lambda i, j, u: (0, place(i, j, u)))))
        else:
            results.append((jax.ShapeDtypeStruct((4 * rows, size), jnp.float32), spec((blk, size), lambda i, j, u: (place(i, j, u), 0))))
    return stage(
        line, "join_four", body, (4, n), uppers,
        [(x, spec((blk, cols), turn(p))) for p, x in enumerate(pieces)], results,
    )


def weight_grad(line, upper, away, groups):
    left = groups[0][0][0]
    half = left.shape[1] // 2
    blk = min(half, 256)
    n = half // blk

    def row_spec(x, rows, cols, column, turn):
        if turn is None:
            return (x, spec((x.shape[0], cols), lambda j, u: (0, column(j, u))))
        pick = (lambda u: u[1]) if turn else (lambda u: 1 - u[1])
        if x.shape[0] == rows:
            pick = lambda u: 0
        return (x, spec((rows, cols), lambda j, u: (pick(u), column(j, u))))

    if away:
        block = lambda j, u: (1 - u[0]) * n + j
    else:
        block = lambda j, u: u[0] * n + j
    ins, plan = [], []
    for group in groups:
        terms = []
        for left, turn, rights, right_turn in group:
            rows = left.shape[0] if turn is None and right_turn is None else min(left.shape[0], rights[0].shape[0])
            if rows == left.shape[0] == rights[0].shape[0] and turn is not None:
                rows = left.shape[0] // 2
            terms.append((len(ins), len(rights)))
            ins.append(row_spec(left, rows, blk, block, turn))
            ins.extend(row_spec(r, rows, r.shape[1], lambda j, u: 0, right_turn) for r in rights)
        plan.append(terms)
    width = sum(r.shape[1] for group in groups for r in group[0][2])

    def body(u, *refs):
        out, col = refs[-1], 0
        for terms in plan:
            lefts = [refs[at][...] for at, _ in terms]
            for i in range(terms[0][1]):
                total = 0.0
                for (at, _), left_rows in zip(terms, lefts):
                    total = total + dotf(left_rows, refs[at + 1 + i][...], TN)
                out[:, col : col + total.shape[1]] = total.astype(jnp.bfloat16)
                col += total.shape[1]

    return stage(
        line, "weight_grad", body, (n,), upper, ins,
        [(jax.ShapeDtypeStruct((half, width), jnp.bfloat16), spec((blk, width), lambda j, u: (j, 0)))],
    )


def norm_back_own(line, kept, got, source, base, gain, start):
    rows, cols = kept.shape
    blk = min(rows, 128)
    n = rows // blk

    def body(s, k, g, x, b, gain_ref, out, low, sums):
        grad = k[...].astype(jnp.float32) + g[...].astype(jnp.float32)
        center = x[...].astype(jnp.float32)
        center = center - jnp.mean(center, axis=1, keepdims=True)
        scaled = lax.rsqrt(jnp.mean(center * center, axis=1, keepdims=True) + epsilon)
        normal = center * scaled
        moved = b[...].astype(jnp.float32) + norm_back(grad, normal, scaled, gain_ref[...])
        out[...] = moved
        low[...] = moved.astype(jnp.bfloat16)

        @pl.when(pl.program_id(0) == 0)
        def _():
            sums[...] = jnp.zeros_like(sums)

        sums[0:1, :] += jnp.sum(grad * normal, axis=0, keepdims=True)
        sums[1:2, :] += jnp.sum(grad, axis=0, keepdims=True)

    flat = lambda j, s: (j, 0)
    at = lambda j, s: (s[0] // blk + j, 0)
    base_at = at if base.shape[0] != rows else flat
    source_at = at if source.shape[0] != rows else flat
    whole = spec((blk, cols), flat)
    return stage(
        line, "norm_back", body, (n,), start,
        [
            (kept, whole), (got, whole), (source, spec((blk, cols), source_at)), (base, spec((blk, cols), base_at)),
            (gain.reshape(1, cols), spec((1, cols), lambda j, s: (0, 0))),
        ],
        [
            (jax.ShapeDtypeStruct((rows, cols), jnp.float32), whole),
            (jax.ShapeDtypeStruct((rows, cols), jnp.bfloat16), whole),
            (jax.ShapeDtypeStruct((8, cols), jnp.float32), spec((8, cols), lambda j, s: (0, 0))),
        ],
    )


def add_own(line, kept, got, source):
    rows, cols = kept.shape
    blk = min(rows, 128)
    flat = lambda j, s: (j, 0)

    def body(s, k, g, x, out):
        total = k[...].astype(jnp.float32) + g[...].astype(jnp.float32)
        out[...] = (x[...] + total).astype(jnp.bfloat16)

    whole = spec((blk, cols), flat)
    return stage(
        line, "add_own", body, (rows // blk,), 0,
        [(kept, whole), (got, whole), (source, whole)],
        [(jax.ShapeDtypeStruct((rows, cols), jnp.bfloat16), whole)],
    )


def fixed(x):
    return (x, spec(x.shape, lambda *a: (0, 0)))


def row(x):
    return x.reshape(1, x.shape[0])


def norm_qkv(line, tokens, gain, shift, weights):
    rows, features = tokens.shape
    blk = min(rows, 256)
    flat = lambda j, u: (j, 0)
    outs = [jax.ShapeDtypeStruct((rows, features), jnp.bfloat16)]
    outs += [jax.ShapeDtypeStruct((rows, w.shape[1]), jnp.bfloat16) for w in weights]

    def body(u, token_ref, gain_ref, shift_ref, *refs):
        count = len(weights)
        for part in range(2):
            at = slice(part * blk // 2, (part + 1) * blk // 2)
            normed = norm_parts(token_ref[at, :].astype(jnp.float32), gain_ref[...], shift_ref[...])[2].astype(jnp.bfloat16)
            refs[count][at, :] = normed
            for w, out in zip(refs[:count], refs[count + 1 :]):
                out[at, :] = dotf(normed, w[...]).astype(jnp.bfloat16)

    return stage(
        line, "norm_qkv", body, (rows // blk,), 0,
        [(tokens, spec((blk, features), flat)), fixed(row(gain)), fixed(row(shift))] + [fixed(w) for w in weights],
        [(out, spec((blk, out.shape[1]), flat)) for out in outs],
    )


def project_out(line, start, own, parts, weights, tokens, gain, shift):
    rows, features = tokens.shape
    blk = min(rows, 256)
    flat = lambda j, u: (j, 0)
    pieces = [x for part in parts for x in part]
    depth = sum(w.shape[0] for w in weights)
    ins = [(tokens, spec((blk, features), flat)), fixed(row(gain)), fixed(row(shift))]
    ins += [fixed(w) for w in weights]
    ins += [(x, spec((blk, x.shape[1]), flat)) for x in pieces]

    def body(u, *refs):
        token_ref, gain_ref, shift_ref = refs[:3]
        total_ref, normed_ref, weight = refs[-3:]
        at = 3 + len(weights)

        @pl.when(pl.program_id(0) == 0)
        def _():
            top = 0
            for ref in refs[3:at]:
                weight[top : top + ref.shape[0], :] = ref[...]
                top += ref.shape[0]

        for part in range(2):
            here = slice(part * blk // 2, (part + 1) * blk // 2)
            left = jnp.concatenate([r[here, :] for r in refs[at : at + len(pieces)]], axis=1)
            total = token_ref[here, :].astype(jnp.float32) + dotf(left, weight[...])
            first = pl.program_id(0) * blk + part * (blk // 2) - u[0]

            @pl.when(jnp.logical_and(first >= 0, first < own))
            def _():
                total_ref[pl.ds(pl.multiple_of(first, 16), blk // 2), :] = total

            normed_ref[here, :] = norm_parts(total, gain_ref[...], shift_ref[...])[2].astype(jnp.bfloat16)

    whole = spec((blk, features), flat)
    return stage(
        line, "project_out", body, (rows // blk,), start, ins,
        [
            (jax.ShapeDtypeStruct((own, features), jnp.float32), spec((own, features), lambda j, u: (0, 0))),
            (jax.ShapeDtypeStruct((rows, features), jnp.bfloat16), whole),
        ],
        scratch=[pltpu.VMEM((depth, features), jnp.bfloat16)],
    )


def turn_rows(rows, blk, turn):
    n = rows // 2 // blk
    if turn:
        return lambda j, u: (u[0] * n + j, 0)
    return lambda j, u: ((1 - u[0]) * n + j, 0)


def feed_forward(line, upper, turn, normed, cotangent, up, down, count):
    rows, features = normed.shape
    hidden = up.shape[1]
    blk = min(rows // 2, 256)
    at = turn_rows(rows, blk, turn)
    flat = lambda j, u: (j, 0)

    def body(u, normed_ref, cot_ref, up_ref, down_ref, active_ref, inner_ref, *back_refs):
        for part in range(2):
            here = slice(part * blk // 2, (part + 1) * blk // 2)
            gelu, slope = gelu_pair(dotf(normed_ref[here, :], up_ref[...]))
            active_ref[here, :] = gelu.astype(jnp.bfloat16)
            grad = (dotf(cot_ref[here, :], down_ref[...], NT) * slope).astype(jnp.bfloat16)
            inner_ref[here, :] = grad
            put([r.at[here, :] for r in back_refs], dotf(grad, up_ref[...], NT))

    outs = pieces_of(rows // 2, 2 * hidden, 2) + pieces_of(rows // 2, features, count)
    return stage(
        line, "feed_forward", body, (rows // 2 // blk,), upper,
        columns([normed, cotangent], blk, at) + [fixed(up), fixed(down)],
        [(out, spec((blk, out.shape[1]), flat)) for out in outs],
    )


def product(line, left, right, count):
    rows = left.shape[0]
    blk = min(rows, 256)
    flat = lambda j, u: (j, 0)

    def body(u, l, r, *outs):
        put(outs, dotf(l[...], r[...]))

    made = stage(
        line, "product", body, (rows // blk,), 0,
        columns([left], blk, flat) + [fixed(right)],
        [(x, spec((blk, x.shape[1]), flat)) for x in pieces_of(rows, right.shape[1], count)],
    )
    return made if count > 1 else [made]


def product_back(line, upper, turn, lefts, rights, pieces):
    rows = lefts[0][0].shape[0]
    features, width = rights[0].shape
    blk = min(rows // 2, 256)
    at = turn_rows(rows, blk, turn)
    flat = [x for left in lefts for x in left]

    def body(u, *refs):
        weight = refs[-1]

        @pl.when(pl.program_id(0) == 0)
        def _():
            for i, r in enumerate(refs[len(flat) : len(flat) + len(rights)]):
                weight[:, i * width : (i + 1) * width] = r[...]

        put(refs[len(flat) + len(rights) : -1], dotf(cat(refs[: len(flat)]), weight[...], NT))

    made = stage(
        line, "product_back", body, (rows // 2 // blk,), upper,
        columns(flat, blk, at) + [fixed(r) for r in rights],
        [(x, spec((blk, x.shape[1]), lambda j, u: (j, 0))) for x in pieces_of(rows // 2, features, pieces)],
        scratch=[pltpu.VMEM((features, len(rights) * width), jnp.bfloat16)],
    )
    return made if pieces > 1 else [made]


def add_small(line, mine, got):
    def body(u, m, g, out):
        out[...] = m[...] + g[...]

    return stage(line, "add_small", body, (1,), 0, [fixed(mine), fixed(got)], [(jax.ShapeDtypeStruct(mine.shape, mine.dtype), fixed(mine)[1])])


def shards(
    n_dp,
    n_tp,
    tokens,
    query_weight,
    key_weight,
    value_weight,
    out_weight,
    up_weight,
    down_weight,
    bias_table,
    gain_one,
    shift_one,
    gain_two,
    shift_two,
    single_item,
    cotangent,
):
    tp_bits = index_bits(n_tp)
    dp_bits = index_bits(n_dp)
    far_first = tp_bits[1:] + tp_bits[:1]
    low = jnp.bfloat16
    full = jnp.float32
    row_count, features = tokens.shape
    head_count = bias_table.shape[1]
    width = head_count * HD
    tp_up = [rank_bit("tp", bit) for bit in tp_bits]
    dp_up = [rank_bit("dp", bit) for bit in dp_bits]
    start, own_count = own_start("tp", tp_bits, row_count)

    def tp_swap(values, i):
        return swap(values, "tp", n_tp, tp_bits[i])

    def dp_swap(values, i):
        return swap(values, "dp", n_dp, dp_bits[i])

    line = []

    class Sum:
        def __init__(self, axis, send, keep):
            self.axis = axis
            self.up = tp_up if axis == "tp" else dp_up
            self.keep, self.at = keep, 0
            self.swap(send)

        def swap(self, arrays):
            self.got = [keep_far((tp_swap if self.axis == "tp" else dp_swap)(x, self.at)) for x in arrays]

        def count(self, at):
            return PIECES if self.axis == "tp" and at == 0 else 1

        def halve(self):
            self.at += 1
            send, self.keep = split_add(line, self.up[self.at], self.keep, self.got, self.count(self.at))
            self.swap(send)

        def spread(self, values):
            self.keep = values
            self.swap(values)

        def total(self):
            self.spread([add_up(line, self.keep[0], self.got[0])])
            for _ in range(len(self.up) - 3):
                self.double()

        def fan(self):
            joined = join_rows(line, self.up[self.at], self.keep, self.got, low) if self.at > 1 else self.keep
            self.mine = joined[0]
            self.near = dp_swap(self.mine, 1)
            self.far = [dp_swap(self.mine, 0), dp_swap(self.near, 0)]

        def finish(self, outs):
            return join_four(line, self.up[:2], [self.mine, self.near] + self.far, outs)

        def double(self, dtype=low):
            count = self.count(self.at - 1) if self.at else 1
            joined = join_rows(line, self.up[self.at], self.keep, self.got, dtype, count)
            if self.at == 0:
                return joined[0]
            self.at -= 1
            self.spread(joined)

    out_parts = gather_parts(out_weight, "tp", n_tp, far_first)
    near_rows = near_bias(bias_table)
    normed_low, queries, key_rows, value_rows = norm_qkv(
        line, far(tokens), gain_one, shift_one, [far(w) for w in (query_weight, key_weight, value_weight)]
    )
    pairs = width // (2 * HD)
    attended, lse_rows, parts = [], [], []
    for pair in range(pairs):
        also = [out_parts[far_first[0]][:8, :128]] if pair == pairs - 1 else ()
        columns, sums = attn_forward(
            line, pair, single_item, near_rows, queries, key_rows, value_rows, also
        )
        attended.append(columns)
        lse_rows.append(sums)
        parts.append(gather_parts(columns, "tp", n_tp, far_first))
    parts = [[far(parts[pair][k]) if k else parts[pair][k] for pair in range(pairs)] for k in range(n_tp)]
    out_parts = [far(w) for w in out_parts]
    residual, normed_two_low = project_out(
        line, start, own_count, parts, out_parts, tokens, gain_two, shift_two
    )
    fed = [
        feed_forward(line, tp_up[0], turn, normed_two_low, cotangent, up_weight, down_weight, PIECES)
        for turn in (0, 1)
    ]
    two = Sum("tp", fed[0][2:], fed[1][2:])
    ups = [dp_up[0], tp_up[0]]
    down_group = [[(fed[turn][0], turn, [cotangent], turn) for turn in (0, 1)]]
    up_group = [[(normed_two_low, turn, [fed[turn][1]], turn) for turn in (0, 1)]]

    def halve_to_last(total, done):
        for _ in range(len(total.up) - 1 - done):
            total.halve()

    halve_to_last(two, 0)
    down_send = weight_grad(line, ups, True, down_group)
    down_keep = weight_grad(line, ups, False, down_group)
    down = Sum("dp", [down_send], [down_keep])
    ffn = Sum("tp", *[product(line, fed[turn][0], down_weight, PIECES) for turn in (0, 1)])
    up_keep = weight_grad(line, ups, False, up_group)
    grad_residual, grad_residual_low, sums_two = norm_back_own(
        line, two.keep[0], two.got[0], residual, cotangent, gain_two, start
    )
    two.spread([grad_residual_low])
    down.halve()
    up_send = weight_grad(line, ups, True, up_group)
    up = Sum("dp", [up_send], [up_keep])
    for _ in tp_bits[1:]:
        two.double()
    halve_to_last(ffn, 0)
    grad_residual_low = two.double()

    backs = []
    for pair in range(pairs):
        if pair == 1:
            halve_to_last(down, 1)
        backs.append(
            attn_backward(
                line, pair, single_item, near_rows, queries, key_rows, value_rows,
                attended[pair], lse_rows[pair], grad_residual_low, out_weight,
            )
        )
    if pairs == 1:
        halve_to_last(down, 1)
    grad_query, grad_key, grad_value, near_totals = zip(*backs)
    grad_table = table_grad(jnp.stack(near_totals), head_count)
    heads_back = [list(grad_query), list(grad_key), list(grad_value)]
    head_weights = [query_weight, key_weight, value_weight]
    ffn.spread([add_own(line, ffn.keep[0], ffn.got[0], residual)])
    one = Sum("tp", *[product_back(line, tp_up[0], turn, heads_back, head_weights, PIECES) for turn in (0, 1)])
    up.halve()
    mixed_group = [
        [(normed_low, None, heads_back[2], None)],
        [(grad_residual_low, None, attended, None)],
    ]
    heads_group = [[(normed_low, None, heads_back[0] + heads_back[1], None)]]
    mixed_send = weight_grad(line, ups, True, mixed_group)
    halve_to_last(one, 0)
    down.total()
    mixed = Sum("dp", [mixed_send], [weight_grad(line, ups, False, mixed_group)])
    heads_send = weight_grad(line, ups, True, heads_group)
    heads_keep = weight_grad(line, ups, False, heads_group)
    halve_to_last(up, 1)
    down.fan()
    _, grad_tokens, sums_one = norm_back_own(
        line, one.keep[0], one.got[0], tokens, grad_residual, gain_one, start
    )
    one.spread([grad_tokens])
    mixed.halve()
    heads = Sum("dp", [heads_send], [heads_keep])

    table_size = NB * head_count
    slot = jnp.zeros((n_tp * table_size,), full)
    me_tp = lax.axis_index("tp")
    slot = lax.dynamic_update_slice(slot, grad_table.reshape(table_size), (me_tp * table_size,))
    slot = jnp.pad(slot, (0, -slot.size % features)).reshape(-1, features)
    small = [jnp.concatenate([sums_one[:2], sums_two[:2], slot])]
    steps = [("dp", n_dp, bit) for bit in dp_bits] + [("tp", n_tp, bit) for bit in tp_bits]

    small_line = []

    def small_step():
        if steps:
            axis, count, bit = steps.pop(0)
            small[0] = add_small(small_line, small[0], swap(small[0], axis, count, bit))

    up.total()
    for _ in tp_bits[1:]:
        ffn.double()
    small_step()
    halve_to_last(mixed, 1)
    heads.halve()
    small_step()
    for _ in tp_bits[1:]:
        one.double()
    result = ffn.double()
    small_step()
    up.fan()
    mixed.total()
    small_step()
    grad_down = down.finish([(0, features, False)])
    halve_to_last(heads, 1)
    small_step()
    grad_tokens = one.double(full)
    mixed.fan()
    heads.total()
    grad_up = up.finish([(0, up_weight.shape[1], False)])
    heads.fan()
    while steps:
        small_step()
    grad_vw, grad_out = mixed.finish([(0, width, False), (width, width, True)])
    grad_qw, grad_kw = heads.finish([(0, width, False), (width, width, False)])
    small = small[0]
    grad_table = lax.dynamic_slice(
        small[4:].reshape(-1), (me_tp * table_size,), (table_size,)
    ).reshape(NB, head_count)
    return (
        result,
        grad_tokens,
        grad_qw,
        grad_kw,
        grad_vw,
        grad_out,
        grad_up,
        grad_down,
        grad_table,
        small[0],
        small[1],
        small[2],
        small[3],
    )


def solution(mesh):
    placed = (
        P("dp", None),
        P(None, "tp"),
        P(None, "tp"),
        P(None, "tp"),
        P("tp", None),
        P(None, "tp"),
        P("tp", None),
        P(None, "tp"),
        P(),
        P(),
        P(),
        P(),
        P("dp"),
        P("dp", None),
    )
    return jax.shard_map(
        functools.partial(shards, mesh.shape["dp"], mesh.shape["tp"]),
        mesh=mesh,
        in_specs=placed,
        out_specs=(
            P("dp", None),
            P("dp", None),
            P(None, "tp"),
            P(None, "tp"),
            P(None, "tp"),
            P("tp", None),
            P(None, "tp"),
            P("tp", None),
            P(None, "tp"),
            P(),
            P(),
            P(),
            P(),
        ),
        check_vma=False,
    )
```

```python
import functools
import math

import jax
import jax.numpy as jnp
from jax import lax
from jax.experimental import pallas as pl
from jax.experimental.pallas import tpu as pltpu
from jax.sharding import PartitionSpec as P

HD = 64
NB = 32
MAXDIST = 128


epsilon = 1e-05
FRONT = {"norm_qkv": 3.5, "attn_forward": 4.5, "project_out": 6.0, "feed_forward": 7.0}
REST = {"split_add": 1.5, "join_rows": 2.0, "weight_grad": 3.0, "norm_back": 2.0, "product": 1.5, "product_back": 1.5, "attn_backward": 14.0, "add_own": 1.3, "add_up": 1.0, "join_four": 4.0, "add_small": 0.5}


def cost_of(name):
    us = FRONT[name] * 1.0 if name in FRONT else REST[name] * 0.3
    return pl.CostEstimate(flops=max(1, int(us * 1.15e9)), bytes_accessed=1, transcendentals=0)

VMEM_LIMIT = 32 * 1024 * 1024
PIECES = 2


def thresholds_list():
    exact_count = NB // 2
    thresholds = []
    for bucket in range(1, NB):
        if bucket <= exact_count:
            thresholds.append(bucket)
        else:
            thresholds.append(
                int(
                    math.ceil(
                        exact_count
                        * (MAXDIST / exact_count) ** ((bucket - exact_count) / exact_count)
                    )
                )
            )
    return thresholds


def distance_onehot(count):
    distance = jnp.arange(count, dtype=jnp.int32)
    buckets = jnp.zeros((count,), jnp.int32)
    for threshold in thresholds_list():
        buckets = buckets + (distance >= threshold).astype(jnp.int32)
    return (buckets[:, None] == jnp.arange(NB, dtype=jnp.int32)[None, :]).astype(jnp.float32)


def norm_parts(values, gain, shift):
    center = values - jnp.mean(values, axis=-1, keepdims=True)
    scaled = lax.rsqrt(jnp.mean(center * center, axis=-1, keepdims=True) + epsilon)
    normal = center * scaled
    return (normal, scaled, normal * gain + shift)


def norm_back(grad_out, normal, scaled, gain):
    grad_norm = grad_out * gain
    inner_mean = jnp.mean(grad_norm * normal, axis=-1, keepdims=True)
    return scaled * (grad_norm - jnp.mean(grad_norm, axis=-1, keepdims=True) - normal * inner_mean)


def gelu_pair(values):
    bell = jnp.exp(-0.5 * values * values)
    t = 1.0 / (1.0 + (0.3275911 * math.sqrt(0.5)) * jnp.abs(values))
    poly = 0.5 * 1.061405429
    for factor in (-1.453152027, 1.421413741, -0.284496736, 0.254829592):
        poly = poly * t + 0.5 * factor
    tail = poly * t * bell
    cdf = jnp.where(values < 0.0, tail, 1.0 - tail)
    return values * cdf, cdf + values * bell * (1.0 / math.sqrt(2.0 * math.pi))


BLK = 256
NEAR = 128
NEG = -1000000000.0
NT = (((1,), (1,)), ((), ()))
TN = (((0,), (0,)), ((), ()))


def dotf(a, b, dims=(((1,), (0,)), ((), ()))):
    return lax.dot_general(a, b, dims, preferred_element_type=jnp.float32)


def fill_bias(g_ref, bias_ref):
    row = lax.broadcasted_iota(jnp.int32, (2 * NEAR, NEAR), 0)
    col = lax.broadcasted_iota(jnp.int32, (2 * NEAR, NEAR), 1)
    hidden = row - NEAR > col
    for h in range(2):
        spread = jnp.broadcast_to(g_ref[h : h + 1, :], (2 * NEAR, 2 * NEAR))
        tile = pltpu.roll(spread, 0, 1, stride=1, stride_axis=0)[:, :NEAR]
        tile = jnp.where(hidden, NEG, tile)
        bias_ref[h, : 2 * NEAR, :NEAR] = tile
        bias_ref[h, 2 * NEAR :, :NEAR] = jnp.full((NEAR, NEAR), NEG, jnp.float32)
        bias_ref[h, :NEAR, NEAR:] = jnp.zeros((NEAR, NEAR), jnp.float32)
        bias_ref[h, NEAR:, NEAR:] = tile


def head_mask(x, h):
    lane = lax.broadcasted_iota(jnp.int32, x.shape, 1)
    return jnp.where((lane < HD) == (h == 0), x, jnp.zeros_like(x))


def add_near(st, bias_ref, h, low, blk):
    near = max(blk * BLK - NEAR, low)
    top = near - low
    tile = bias_ref[h, near - (blk * BLK - NEAR) :, :]
    if top == 0:
        return st + tile
    return jnp.concatenate([st[:top], st[top:] + tile], axis=0)


def each_block(row_count, single_ref, work):
    half = row_count // 2
    single = single_ref[0] == 1
    for blk in range(row_count // BLK):
        if blk * BLK < half:
            work(blk, 0)
        else:
            pl.when(single)(functools.partial(work, blk, 0))
            pl.when(jnp.logical_not(single))(functools.partial(work, blk, half))


def attn_fwd_kernel(single_ref, g_ref, q_ref, k_ref, v_ref, o_ref, lse_ref, bias_ref, vt_ref):
    row_count = q_ref.shape[0]
    fill_bias(g_ref, bias_ref)
    vt_ref[...] = v_ref[...].T

    def work(blk, low):
        high = (blk + 1) * BLK
        rows = slice(blk * BLK, high)
        q = q_ref[rows, :] * jnp.asarray(HD ** (-0.5), jnp.bfloat16)
        outs = []
        for h in range(2):
            st = dotf(k_ref[low:high, :], head_mask(q, h), NT)
            st = add_near(st, bias_ref, h, low, blk)
            m = jnp.max(st, axis=0, keepdims=True)
            p = jnp.exp(st - m)
            total = jnp.sum(p, axis=0, keepdims=True)
            ot = dotf(vt_ref[h * HD : (h + 1) * HD, low:high], p.astype(jnp.bfloat16))
            outs.append(ot / total)
            lse_ref[h : h + 1, rows] = m + jnp.log(total)
        o_ref[rows, :] = jnp.concatenate(outs, axis=0).T.astype(jnp.bfloat16)

    each_block(row_count, single_ref, work)


def attn_bwd_kernel(
    single_ref, g_ref, q_ref, k_ref, v_ref, o_ref, lse_ref, gr_ref, w_ref,
    dq_ref, dk_ref, dv_ref, near_ref, bias_ref, kt_ref, dk_acc, dv_acc, near_acc,
):
    row_count = q_ref.shape[0]
    fill_bias(g_ref, bias_ref)
    kt_ref[...] = k_ref[...].T
    dk_acc[...] = jnp.zeros_like(dk_acc)
    dv_acc[...] = jnp.zeros_like(dv_acc)
    near_acc[...] = jnp.zeros_like(near_acc)

    def work(blk, low):
        high = (blk + 1) * BLK
        rows = slice(blk * BLK, high)
        q = q_ref[rows, :] * jnp.asarray(HD ** (-0.5), jnp.bfloat16)
        da = dotf(gr_ref[rows, :], w_ref[...], NT).astype(jnp.bfloat16)
        prod_t = (da.astype(jnp.float32) * o_ref[rows, :].astype(jnp.float32)).T
        ps, dss, qms, dams, dqts = [], [], [], [], []
        for h in range(2):
            qm, dam = head_mask(q, h), head_mask(da, h)
            st = dotf(k_ref[low:high, :], qm, NT)
            st = add_near(st, bias_ref, h, low, blk)
            p = jnp.exp(st - lse_ref[h : h + 1, rows])
            dpt = dotf(v_ref[low:high, :], dam, NT)
            dd = jnp.sum(prod_t[h * HD : (h + 1) * HD], axis=0, keepdims=True)
            ds = p * (dpt - dd)
            own = blk * BLK - low
            if own:
                near_acc[h] += ds[own - NEAR : own + NEAR, :NEAR]
            else:
                near_acc[h, NEAR:] += ds[:NEAR, :NEAR]
            near_acc[h] += ds[own : own + 2 * NEAR, NEAR:]
            dsb = ds.astype(jnp.bfloat16)
            ps.append(p.astype(jnp.bfloat16))
            dss.append(dsb)
            qms.append(qm)
            dams.append(dam)
            dqts.append(dotf(kt_ref[h * HD : (h + 1) * HD, low:high], dsb))
        dv_acc[low:high] += dotf(jnp.concatenate(ps, axis=1), jnp.concatenate(dams, axis=0))
        dk_acc[low:high] += dotf(jnp.concatenate(dss, axis=1), jnp.concatenate(qms, axis=0))
        dq = jnp.concatenate(dqts, axis=0).T * HD ** (-0.5)
        dq_ref[rows, :] = dq.astype(jnp.bfloat16)

    each_block(row_count, single_ref, work)
    dk_ref[...] = dk_acc[...].astype(jnp.bfloat16)
    dv_ref[...] = dv_acc[...].astype(jnp.bfloat16)
    near_ref[...] = jnp.zeros_like(near_ref)
    for h in range(2):
        acc = jnp.concatenate([near_acc[h], jnp.zeros((2 * NEAR, NEAR), jnp.float32)], axis=1)
        row = lax.broadcasted_iota(jnp.int32, acc.shape, 0)
        for bit in range((2 * NEAR - 1).bit_length()):
            moved = pltpu.roll(acc, 2 * NEAR - (1 << bit), 1)
            acc = jnp.where((row & (1 << bit)) != 0, moved, acc)
        near_ref[h : h + 1, :] = jnp.sum(acc, axis=0, keepdims=True)


def pair_specs(row_count, first):
    smem = pl.BlockSpec(memory_space=pltpu.SMEM)
    cols = pl.BlockSpec((row_count, 2 * HD), lambda p: (0, first + p))
    near = pl.BlockSpec((None, 8, 2 * NEAR), lambda p: (first + p, 0, 0))
    lse = pl.BlockSpec((None, 8, row_count), lambda p: (first + p, 0, 0))
    return smem, cols, near, lse


def held(arrays):
    return [pl.BlockSpec(memory_space=pl.ANY)] * len(arrays)


def attn_forward(line, pair, single_item, g, q, k, v, also=()):
    row_count = q.shape[0]
    after = line + list(also)
    smem, cols, near, _ = pair_specs(row_count, pair)
    own = pl.BlockSpec((row_count, 2 * HD), lambda p: (0, 0))
    lse = pl.BlockSpec((8, row_count), lambda p: (0, 0))

    def kernel(*refs):
        attn_fwd_kernel(*refs[:5], *refs[5 + len(after) :])

    attended, lse_rows = pl.pallas_call(
        kernel,
        grid=(1,),
        in_specs=[smem, near, cols, cols, cols] + held(after),
        out_specs=[own, lse],
        out_shape=[
            jax.ShapeDtypeStruct((row_count, 2 * HD), jnp.bfloat16),
            jax.ShapeDtypeStruct((8, row_count), jnp.float32),
        ],
        scratch_shapes=[
            pltpu.VMEM((2, 3 * NEAR, BLK), jnp.float32),
            pltpu.VMEM((2 * HD, row_count), jnp.bfloat16),
        ],
        compiler_params=pltpu.CompilerParams(vmem_limit_bytes=VMEM_LIMIT),
        cost_estimate=cost_of("attn_forward"),
        name="attn_forward",
    )(single_item, g, q, k, v, *after)
    line[:] = [lse_rows]
    return attended, lse_rows


def attn_backward(line, single_item, g, q, k, v, o, lse_rows, grad, out_weight):
    row_count, width = q.shape
    pairs = len(o)
    after = list(line)
    smem = pl.BlockSpec(memory_space=pltpu.SMEM)
    cols = pl.BlockSpec((row_count, 2 * HD), lambda p: (0, p))
    near = pl.BlockSpec((None, 8, 2 * NEAR), lambda p: (p, 0, 0))
    flat = jax.ShapeDtypeStruct((row_count, width), jnp.bfloat16)

    def whole(x):
        return pl.BlockSpec(x.shape, lambda p: (0, 0))

    def kernel(*refs):
        o_refs, lse_refs = refs[5 : 5 + pairs], refs[5 + pairs : 5 + 2 * pairs]
        rest = refs[5 + 2 * pairs :]
        o_ref, lse_ref = rest[-2:]
        for p in range(pairs):

            @pl.when(pl.program_id(0) == p)
            def _():
                o_ref[...] = o_refs[p][...]
                lse_ref[...] = lse_refs[p][...]

        attn_bwd_kernel(*refs[:5], o_ref, lse_ref, *rest[:2], *rest[2 + len(after) : -2])

    *grads, near_totals = pl.pallas_call(
        kernel,
        grid=(pairs,),
        in_specs=[smem, near, cols, cols, cols]
        + [whole(x) for x in o]
        + [whole(x) for x in lse_rows]
        + [whole(grad), pl.BlockSpec((2 * HD, grad.shape[1]), lambda p: (p, 0))]
        + held(after),
        out_specs=[cols, cols, cols, near],
        out_shape=[flat, flat, flat, jax.ShapeDtypeStruct((pairs, 8, 2 * NEAR), jnp.float32)],
        scratch_shapes=[
            pltpu.VMEM((2, 3 * NEAR, BLK), jnp.float32),
            pltpu.VMEM((2 * HD, row_count), jnp.bfloat16),
            pltpu.VMEM((row_count, 2 * HD), jnp.float32),
            pltpu.VMEM((row_count, 2 * HD), jnp.float32),
            pltpu.VMEM((2, 2 * NEAR, NEAR), jnp.float32),
            pltpu.VMEM((row_count, 2 * HD), jnp.bfloat16),
            pltpu.VMEM((8, row_count), jnp.float32),
        ],
        compiler_params=pltpu.CompilerParams(vmem_limit_bytes=VMEM_LIMIT),
        cost_estimate=cost_of("attn_backward"),
        name="attn_backward",
    )(single_item, g, q, k, v, *o, *lse_rows, grad, out_weight, *after)
    line[:] = [near_totals]
    return *grads, near_totals


def near_bias(bias_table):
    head_count = bias_table.shape[1]
    rows = jnp.dot(
        distance_onehot(NEAR), bias_table - bias_table[NB - 1 :],
        precision=lax.Precision.HIGHEST, preferred_element_type=jnp.float32,
    ).T
    rows = jnp.pad(rows, ((0, 0), (NEAR, 0))).reshape(head_count // 2, 2, 2 * NEAR)
    return jnp.pad(rows, ((0, 0), (0, 6), (0, 0)))


def table_grad(near, head_count):
    by_dist = near[:, :2, NEAR:].reshape(head_count, NEAR)
    grad = jnp.dot(
        by_dist, distance_onehot(NEAR)[:, : NB - 1],
        precision=lax.Precision.HIGHEST, preferred_element_type=jnp.float32,
    )
    return jnp.concatenate([grad, -jnp.sum(grad, axis=1, keepdims=True)], axis=1).T


def index_bits(count):
    return [1 << i for i in range(count.bit_length() - 1)]


def sent(rows, cols):
    return pltpu.HBM((rows, cols), jnp.bfloat16)


def far(x):
    return pltpu.with_memory_space_constraint(x, pltpu.HBM)


def keep_far(x):
    return x


def swap(values, axis, count, bit):
    return lax.ppermute(values, axis, [(i, i ^ bit) for i in range(count)])


def rank_bit(axis, bit):
    return (lax.axis_index(axis) // bit) % 2


def gather_parts(values, axis, count, bits):
    parts = {0: values}
    for bit in bits:
        for k in list(parts):
            parts[k ^ bit] = swap(parts[k], axis, count, bit)
    return [parts[k] for k in range(count)]


def own_start(axis, bits, size):
    start = 0
    for bit in bits:
        size //= 2
        start = start + rank_bit(axis, bit) * size
    return start, size


def sum_over(values, axis, count, bits):
    for bit in bits:
        values = values + swap(values, axis, count, bit)
    return values


def spec(shape, index):
    return pl.BlockSpec(shape, index)


def scalars(values):
    values = values if isinstance(values, list) else [values]
    return jnp.stack([jnp.asarray(v, jnp.int32) for v in values])


def stage(line, name, body, grid, upper, ins, outs, scratch=(), also=()):
    after = line + list(also)
    shapes = [shape for shape, _ in outs] + [jax.ShapeDtypeStruct((8, 128), jnp.float32)]
    token = pl.BlockSpec((8, 128), lambda *a: (0, 0))
    held = pl.BlockSpec(memory_space=pl.ANY)

    def kernel(upper_ref, *refs):
        used = refs[: len(ins)]
        rest = refs[len(ins) + len(after) :]
        body(upper_ref, *used, *rest[: len(outs)], *rest[len(outs) + 1 :])
        rest[len(outs)][...] = jnp.zeros((8, 128), jnp.float32)

    *results, mark = pl.pallas_call(
        kernel,
        grid_spec=pltpu.PrefetchScalarGridSpec(
            num_scalar_prefetch=1,
            grid=grid,
            in_specs=[where for _, where in ins] + [held] * len(after),
            out_specs=[where for _, where in outs] + [token],
            scratch_shapes=list(scratch),
        ),
        out_shape=shapes,
        compiler_params=pltpu.CompilerParams(vmem_limit_bytes=VMEM_LIMIT),
        cost_estimate=cost_of(name),
        name=name,
    )(scalars(upper), *[x for x, _ in ins], *after)
    line[:] = [mark]
    return results if len(results) > 1 else results[0]


def cat(refs):
    return refs[0][...] if len(refs) == 1 else jnp.concatenate([r[...] for r in refs], axis=1)


def put(refs, values):
    at = 0
    for ref in refs:
        size = ref.shape[1]
        ref[...] = values[:, at : at + size].astype(ref.dtype)
        at += size


def columns(arrays, blk, index):
    return [(x, spec((blk, x.shape[1]), index)) for x in arrays]


def pieces_of(rows, cols, count, dtype=jnp.bfloat16):
    return [jax.ShapeDtypeStruct((rows, cols // count), dtype)] * count


def split_add(line, upper, kept, got, count=1):
    rows, cols = got[0].shape[0], sum(x.shape[1] for x in got)
    half = rows // 2
    blk = min(half, 128)
    n = half // blk
    a, b = len(kept), len(got)

    def body(u, *refs):
        for at, outs in ((0, refs[2 * a + 2 * b : -1]), (a + b, refs[-1:])):
            total = cat(refs[at : at + a]).astype(jnp.float32)
            put(outs, total + cat(refs[at + a : at + a + b]).astype(jnp.float32))

    away = lambda j, u: ((1 - u[0]) * n + j, 0)
    here = lambda j, u: (u[0] * n + j, 0)
    outs = pieces_of(half, cols, count) + pieces_of(half, cols, 1)
    *send, keep = stage(
        line, "split_add", body, (n,), upper,
        columns(kept + got, blk, away) + columns(kept + got, blk, here),
        [(x, spec((blk, x.shape[1]), lambda j, u: (j, 0))) for x in outs],
    )
    return send, [keep]


def add_up(line, kept, got):
    rows, cols = kept.shape
    blk = min(rows, 128)
    flat = lambda j, u: (j, 0)

    def body(u, k, g, out):
        out[...] = (k[...].astype(jnp.float32) + g[...].astype(jnp.float32)).astype(out.dtype)

    where = spec((blk, cols), flat)
    return stage(
        line, "add_up", body, (rows // blk,), 0, [(kept, where), (got, where)],
        [(jax.ShapeDtypeStruct(kept.shape, jnp.bfloat16), where)],
    )


def join_rows(line, upper, mine, got, dtype, count=1):
    rows, cols = mine[0].shape[0], sum(x.shape[1] for x in mine)
    blk = min(rows, 256)
    n = rows // blk
    a = len(mine)

    def body(u, *refs):
        i = pl.program_id(0)

        @pl.when(i == 0)
        def _():
            put(refs[2 * a :], cat(refs[:a]))

        @pl.when(i == 1)
        def _():
            put(refs[2 * a :], cat(refs[a : 2 * a]))

    joined = stage(
        line, "join_rows", body, (2, n), upper,
        columns(mine, blk, lambda i, j, u: (jnp.where(i == 0, j, n - 1), 0))
        + columns(got, blk, lambda i, j, u: (jnp.where(i == 0, 0, j), 0)),
        [
            (x, spec((blk, x.shape[1]), lambda i, j, u: (jnp.where(i == 0, u[0], 1 - u[0]) * n + j, 0)))
            for x in pieces_of(2 * rows, cols, count, dtype)
        ],
    )
    return joined if count > 1 else [joined]


def join_four(line, uppers, pieces, outs):
    rows, cols = pieces[0].shape
    blk = min(rows, 128)
    n = rows // blk

    def body(u, *refs):
        for p in range(4):

            @pl.when(pl.program_id(0) == p)
            def _():
                for out, (first, size, turned) in zip(refs[4:], outs):
                    x = refs[p][:, first : first + size].astype(jnp.float32)
                    out[...] = x.T if turned else x

    def place(i, j, u):
        high = jnp.where(i < 2, u[0], 1 - u[0])
        return (high * 2 + jnp.where(i % 2 == 0, u[1], 1 - u[1])) * n + j

    def turn(p):
        return lambda i, j, u: (jnp.where(i == p, j, jnp.where(i < p, 0, n - 1)), 0)

    results = []
    for _, size, turned in outs:
        if turned:
            results.append((jax.ShapeDtypeStruct((size, 4 * rows), jnp.float32), spec((size, blk), lambda i, j, u: (0, place(i, j, u)))))
        else:
            results.append((jax.ShapeDtypeStruct((4 * rows, size), jnp.float32), spec((blk, size), lambda i, j, u: (place(i, j, u), 0))))
    return stage(
        line, "join_four", body, (4, n), uppers,
        [(x, spec((blk, cols), turn(p))) for p, x in enumerate(pieces)], results,
    )


def weight_grad(line, upper, away, groups):
    left = groups[0][0][0]
    half = left.shape[1] // 2
    blk = min(half, 256)
    n = half // blk

    def row_spec(x, rows, cols, column, turn):
        if turn is None:
            return (x, spec((x.shape[0], cols), lambda j, u: (0, column(j, u))))
        pick = (lambda u: u[1]) if turn else (lambda u: 1 - u[1])
        if x.shape[0] == rows:
            pick = lambda u: 0
        return (x, spec((rows, cols), lambda j, u: (pick(u), column(j, u))))

    if away:
        block = lambda j, u: (1 - u[0]) * n + j
    else:
        block = lambda j, u: u[0] * n + j
    ins, plan = [], []
    for group in groups:
        terms = []
        for left, turn, rights, right_turn in group:
            rows = left.shape[0] if turn is None and right_turn is None else min(left.shape[0], rights[0].shape[0])
            if rows == left.shape[0] == rights[0].shape[0] and turn is not None:
                rows = left.shape[0] // 2
            terms.append((len(ins), len(rights)))
            ins.append(row_spec(left, rows, blk, block, turn))
            ins.extend(row_spec(r, rows, r.shape[1], lambda j, u: 0, right_turn) for r in rights)
        plan.append(terms)
    width = sum(r.shape[1] for group in groups for r in group[0][2])

    def body(u, *refs):
        out, col = refs[-1], 0
        for terms in plan:
            lefts = [refs[at][...] for at, _ in terms]
            for i in range(terms[0][1]):
                total = 0.0
                for (at, _), left_rows in zip(terms, lefts):
                    total = total + dotf(left_rows, refs[at + 1 + i][...], TN)
                out[:, col : col + total.shape[1]] = total.astype(jnp.bfloat16)
                col += total.shape[1]

    return stage(
        line, "weight_grad", body, (n,), upper, ins,
        [(jax.ShapeDtypeStruct((half, width), jnp.bfloat16), spec((blk, width), lambda j, u: (j, 0)))],
    )


def norm_back_own(line, kept, got, source, base, gain, start):
    rows, cols = kept.shape
    blk = min(rows, 128)
    n = rows // blk

    def body(s, k, g, x, b, gain_ref, out, low, sums):
        grad = k[...].astype(jnp.float32) + g[...].astype(jnp.float32)
        center = x[...].astype(jnp.float32)
        center = center - jnp.mean(center, axis=1, keepdims=True)
        scaled = lax.rsqrt(jnp.mean(center * center, axis=1, keepdims=True) + epsilon)
        normal = center * scaled
        moved = b[...].astype(jnp.float32) + norm_back(grad, normal, scaled, gain_ref[...])
        out[...] = moved
        low[...] = moved.astype(jnp.bfloat16)

        @pl.when(pl.program_id(0) == 0)
        def _():
            sums[...] = jnp.zeros_like(sums)

        sums[0:1, :] += jnp.sum(grad * normal, axis=0, keepdims=True)
        sums[1:2, :] += jnp.sum(grad, axis=0, keepdims=True)

    flat = lambda j, s: (j, 0)
    at = lambda j, s: (s[0] // blk + j, 0)
    base_at = at if base.shape[0] != rows else flat
    source_at = at if source.shape[0] != rows else flat
    whole = spec((blk, cols), flat)
    return stage(
        line, "norm_back", body, (n,), start,
        [
            (kept, whole), (got, whole), (source, spec((blk, cols), source_at)), (base, spec((blk, cols), base_at)),
            (gain.reshape(1, cols), spec((1, cols), lambda j, s: (0, 0))),
        ],
        [
            (jax.ShapeDtypeStruct((rows, cols), jnp.float32), whole),
            (jax.ShapeDtypeStruct((rows, cols), jnp.bfloat16), whole),
            (jax.ShapeDtypeStruct((8, cols), jnp.float32), spec((8, cols), lambda j, s: (0, 0))),
        ],
    )


def add_own(line, kept, got, source):
    rows, cols = kept.shape
    blk = min(rows, 128)
    flat = lambda j, s: (j, 0)

    def body(s, k, g, x, out):
        total = k[...].astype(jnp.float32) + g[...].astype(jnp.float32)
        out[...] = (x[...] + total).astype(jnp.bfloat16)

    whole = spec((blk, cols), flat)
    return stage(
        line, "add_own", body, (rows // blk,), 0,
        [(kept, whole), (got, whole), (source, whole)],
        [(jax.ShapeDtypeStruct((rows, cols), jnp.bfloat16), whole)],
    )


def fixed(x):
    return (x, spec(x.shape, lambda *a: (0, 0)))


def row(x):
    return x.reshape(1, x.shape[0])


def norm_qkv(line, tokens, gain, shift, weights):
    rows, features = tokens.shape
    blk = min(rows, 256)
    flat = lambda j, u: (j, 0)
    outs = [sent(rows, features)]
    outs += [jax.ShapeDtypeStruct((rows, w.shape[1]), jnp.bfloat16) for w in weights]

    def body(u, token_ref, gain_ref, shift_ref, *refs):
        count = len(weights)
        for part in range(2):
            at = slice(part * blk // 2, (part + 1) * blk // 2)
            normed = norm_parts(token_ref[at, :].astype(jnp.float32), gain_ref[...], shift_ref[...])[2].astype(jnp.bfloat16)
            refs[count][at, :] = normed
            for w, out in zip(refs[:count], refs[count + 1 :]):
                out[at, :] = dotf(normed, w[...]).astype(jnp.bfloat16)

    return stage(
        line, "norm_qkv", body, (rows // blk,), 0,
        [(tokens, spec((blk, features), flat)), fixed(far(row(gain))), fixed(far(row(shift)))] + [fixed(w) for w in weights],
        [(out, spec((blk, out.shape[1]), flat)) for out in outs],
    )


def project_out(line, start, own, parts, weights, tokens, gain, shift):
    rows, features = tokens.shape
    blk = min(rows, 256)
    flat = lambda j, u: (j, 0)
    pieces = [x for part in parts for x in part]
    depth = sum(w.shape[0] for w in weights)
    ins = [(tokens, spec((blk, features), flat)), fixed(far(row(gain))), fixed(far(row(shift)))]
    ins += [fixed(w) for w in weights]
    ins += [(x, spec((blk, x.shape[1]), flat)) for x in pieces]

    def body(u, *refs):
        token_ref, gain_ref, shift_ref = refs[:3]
        total_ref, normed_ref, weight = refs[-3:]
        at = 3 + len(weights)

        @pl.when(pl.program_id(0) == 0)
        def _():
            top = 0
            for ref in refs[3:at]:
                weight[top : top + ref.shape[0], :] = ref[...]
                top += ref.shape[0]

        for part in range(2):
            here = slice(part * blk // 2, (part + 1) * blk // 2)
            left = jnp.concatenate([r[here, :] for r in refs[at : at + len(pieces)]], axis=1)
            total = token_ref[here, :].astype(jnp.float32) + dotf(left, weight[...])
            first = pl.program_id(0) * blk + part * (blk // 2) - u[0]

            @pl.when(jnp.logical_and(first >= 0, first < own))
            def _():
                total_ref[pl.ds(pl.multiple_of(first, 16), blk // 2), :] = total

            normed_ref[here, :] = norm_parts(total, gain_ref[...], shift_ref[...])[2].astype(jnp.bfloat16)

    whole = spec((blk, features), flat)
    return stage(
        line, "project_out", body, (rows // blk,), start, ins,
        [
            (jax.ShapeDtypeStruct((own, features), jnp.float32), spec((own, features), lambda j, u: (0, 0))),
            (jax.ShapeDtypeStruct((rows, features), jnp.bfloat16), whole),
        ],
        scratch=[pltpu.VMEM((depth, features), jnp.bfloat16)],
    )


def turn_rows(rows, blk, turn):
    n = rows // 2 // blk
    if turn:
        return lambda j, u: (u[0] * n + j, 0)
    return lambda j, u: ((1 - u[0]) * n + j, 0)


def feed_forward(line, upper, turn, normed, cotangent, up, down, count):
    rows, features = normed.shape
    hidden = up.shape[1]
    blk = min(rows // 2, 256)
    at = turn_rows(rows, blk, turn)
    flat = lambda j, u: (j, 0)

    def body(u, normed_ref, cot_ref, up_ref, down_ref, active_ref, inner_ref, *back_refs):
        for part in range(2):
            here = slice(part * blk // 2, (part + 1) * blk // 2)
            gelu, slope = gelu_pair(dotf(normed_ref[here, :], up_ref[...]))
            active_ref[here, :] = gelu.astype(jnp.bfloat16)
            grad = (dotf(cot_ref[here, :], down_ref[...], NT) * slope).astype(jnp.bfloat16)
            inner_ref[here, :] = grad
            put([r.at[here, :] for r in back_refs], dotf(grad, up_ref[...], NT))

    outs = pieces_of(rows // 2, 2 * hidden, 2) + pieces_of(rows // 2, features, count)
    return stage(
        line, "feed_forward", body, (rows // 2 // blk,), upper,
        columns([normed, cotangent], blk, at) + [fixed(up), fixed(down)],
        [(out, spec((blk, out.shape[1]), flat)) for out in outs],
    )


def product(line, left, right, count):
    rows = left.shape[0]
    blk = min(rows, 256)
    flat = lambda j, u: (j, 0)

    def body(u, l, r, *outs):
        put(outs, dotf(l[...], r[...]))

    made = stage(
        line, "product", body, (rows // blk,), 0,
        columns([left], blk, flat) + [fixed(right)],
        [(x, spec((blk, x.shape[1]), flat)) for x in pieces_of(rows, right.shape[1], count)],
    )
    return made if count > 1 else [made]


def product_back(line, upper, turn, lefts, rights, pieces):
    rows = lefts[0][0].shape[0]
    features, width = rights[0].shape
    blk = min(rows // 2, 256)
    at = turn_rows(rows, blk, turn)
    flat = [x for left in lefts for x in left]

    def body(u, *refs):
        weight = refs[-1]

        @pl.when(pl.program_id(0) == 0)
        def _():
            for i, r in enumerate(refs[len(flat) : len(flat) + len(rights)]):
                weight[:, i * width : (i + 1) * width] = r[...]

        put(refs[len(flat) + len(rights) : -1], dotf(cat(refs[: len(flat)]), weight[...], NT))

    made = stage(
        line, "product_back", body, (rows // 2 // blk,), upper,
        columns(flat, blk, at) + [fixed(r) for r in rights],
        [(x, spec((blk, x.shape[1]), lambda j, u: (j, 0))) for x in pieces_of(rows // 2, features, pieces)],
        scratch=[pltpu.VMEM((features, len(rights) * width), jnp.bfloat16)],
    )
    return made if pieces > 1 else [made]


def hold_small(line, mine):
    def body(u, m, out):
        out[...] = m[...]

    return stage(line, "add_small", body, (1,), 0, [fixed(mine)], [(jax.ShapeDtypeStruct(mine.shape, mine.dtype), fixed(mine)[1])])


def add_small(line, mine, got):
    def body(u, m, g, out):
        out[...] = m[...] + g[...]

    return stage(line, "add_small", body, (1,), 0, [fixed(mine), fixed(got)], [(jax.ShapeDtypeStruct(mine.shape, mine.dtype), fixed(mine)[1])])


def shards(
    n_dp,
    n_tp,
    tokens,
    query_weight,
    key_weight,
    value_weight,
    out_weight,
    up_weight,
    down_weight,
    bias_table,
    gain_one,
    shift_one,
    gain_two,
    shift_two,
    single_item,
    cotangent,
):
    tp_bits = index_bits(n_tp)
    dp_bits = index_bits(n_dp)
    far_first = tp_bits[1:] + tp_bits[:1]
    low = jnp.bfloat16
    full = jnp.float32
    row_count, features = tokens.shape
    head_count = bias_table.shape[1]
    width = head_count * HD
    tp_up = [rank_bit("tp", bit) for bit in tp_bits]
    dp_up = [rank_bit("dp", bit) for bit in dp_bits]
    start, own_count = own_start("tp", tp_bits, row_count)

    def tp_swap(values, i):
        return swap(values, "tp", n_tp, tp_bits[i])

    def dp_swap(values, i):
        return swap(values, "dp", n_dp, dp_bits[i])

    line = []

    class Sum:
        def __init__(self, axis, send, keep):
            self.axis = axis
            self.up = tp_up if axis == "tp" else dp_up
            self.keep, self.at = keep, 0
            self.swap(send)

        def swap(self, arrays):
            self.got = [keep_far((tp_swap if self.axis == "tp" else dp_swap)(x, self.at)) for x in arrays]

        def count(self, at):
            return PIECES if self.axis == "tp" and at == 0 else 1

        def halve(self):
            self.at += 1
            send, self.keep = split_add(line, self.up[self.at], self.keep, self.got, self.count(self.at))
            self.swap(send)

        def spread(self, values):
            self.keep = values
            self.swap(values)

        def total(self):
            self.spread([add_up(line, self.keep[0], self.got[0])])
            for _ in range(len(self.up) - 3):
                self.double()

        def fan(self):
            joined = join_rows(line, self.up[self.at], self.keep, self.got, low) if self.at > 1 else self.keep
            self.mine = joined[0]
            self.near = dp_swap(self.mine, 1)
            self.far = [dp_swap(self.mine, 0), dp_swap(self.near, 0)]

        def finish(self, outs):
            return join_four(line, self.up[:2], [self.mine, self.near] + self.far, outs)

        def double(self, dtype=low):
            count = self.count(self.at - 1) if self.at else 1
            joined = join_rows(line, self.up[self.at], self.keep, self.got, dtype, count)
            if self.at == 0:
                return joined[0]
            self.at -= 1
            self.spread(joined)

    out_parts = gather_parts(out_weight, "tp", n_tp, far_first)
    near_rows = near_bias(bias_table)
    normed_low, queries, key_rows, value_rows = norm_qkv(
        line, far(tokens), gain_one, shift_one, [far(w) for w in (query_weight, key_weight, value_weight)]
    )
    pairs = width // (2 * HD)
    attended, lse_rows, parts = [], [], []
    for pair in range(pairs):
        also = [out_parts[far_first[0]][:8, :128]] if pair == pairs - 1 else ()
        columns, sums = attn_forward(
            line, pair, single_item, near_rows, queries, key_rows, value_rows, also
        )
        attended.append(columns)
        lse_rows.append(sums)
        parts.append(gather_parts(columns, "tp", n_tp, far_first))
    parts = [[far(parts[pair][k]) if k else parts[pair][k] for pair in range(pairs)] for k in range(n_tp)]
    out_parts = [far(w) for w in out_parts]
    residual, normed_two_low = project_out(
        line, start, own_count, parts, out_parts, far(tokens), gain_two, shift_two
    )
    fed = [
        feed_forward(line, tp_up[0], turn, normed_two_low, cotangent, up_weight, down_weight, PIECES)
        for turn in (0, 1)
    ]
    two = Sum("tp", fed[0][2:], fed[1][2:])
    ups = [dp_up[0], tp_up[0]]
    down_group = [[(fed[turn][0], turn, [cotangent], turn) for turn in (0, 1)]]
    up_group = [[(normed_two_low, turn, [fed[turn][1]], turn) for turn in (0, 1)]]

    def halve_to_last(total, done):
        for _ in range(len(total.up) - 1 - done):
            total.halve()

    halve_to_last(two, 0)
    down_send = weight_grad(line, ups, True, down_group)
    down_keep = weight_grad(line, ups, False, down_group)
    down = Sum("dp", [down_send], [down_keep])
    ffn = Sum("tp", *[product(line, fed[turn][0], down_weight, PIECES) for turn in (0, 1)])
    up_keep = weight_grad(line, ups, False, up_group)
    grad_residual, grad_residual_low, sums_two = norm_back_own(
        line, two.keep[0], two.got[0], residual, cotangent, gain_two, start
    )
    two.spread([grad_residual_low])
    down.halve()
    up_send = weight_grad(line, ups, True, up_group)
    up = Sum("dp", [up_send], [up_keep])
    for _ in tp_bits[1:]:
        two.double()
    halve_to_last(ffn, 0)
    grad_residual_low = two.double()
    grad_query, grad_key, grad_value, near_totals = attn_backward(
        line, single_item, near_rows, queries, key_rows, value_rows, attended, lse_rows,
        grad_residual_low, out_weight,
    )
    grad_table = table_grad(near_totals, head_count)
    heads_back = [[grad_query], [grad_key], [grad_value]]
    head_weights = [query_weight, key_weight, value_weight]
    mixed_group = [
        [(normed_low, None, heads_back[2], None)],
        [(grad_residual_low, None, attended, None)],
    ]
    heads_group = [[(normed_low, None, heads_back[0] + heads_back[1], None)]]
    halve_to_last(down, 1)
    one = Sum("tp", *[product_back(line, tp_up[0], turn, heads_back, head_weights, PIECES) for turn in (0, 1)])
    mixed_send = weight_grad(line, ups, True, mixed_group)
    halve_to_last(one, 0)
    up.halve()
    mixed = Sum("dp", [mixed_send], [weight_grad(line, ups, False, mixed_group)])
    heads_send = weight_grad(line, ups, True, heads_group)
    heads = Sum("dp", [heads_send], [weight_grad(line, ups, False, heads_group)])
    down.total()
    _, grad_tokens, sums_one = norm_back_own(
        line, one.keep[0], one.got[0], tokens, grad_residual, gain_one, start
    )
    one.spread([grad_tokens])
    table_size = NB * head_count
    slot = jnp.zeros((n_tp * table_size,), full)
    me_tp = lax.axis_index("tp")
    slot = lax.dynamic_update_slice(slot, grad_table.reshape(table_size), (me_tp * table_size,))
    slot = jnp.pad(slot, (0, -slot.size % features)).reshape(-1, features)
    small = [jnp.concatenate([sums_one[:2], sums_two[:2], slot])]
    steps = [("tp", n_tp, bit) for bit in tp_bits] + [("dp", n_dp, bit) for bit in dp_bits]
    small_line = []

    def small_step(use):
        if steps:
            axis, count, bit = steps.pop(0)
            small[0] = add_small(use, small[0], swap(small[0], axis, count, bit))

    mixed.halve()
    halve_to_last(up, 1)
    down.fan()
    ffn.spread([add_own(line, ffn.keep[0], ffn.got[0], residual)])
    heads.halve()
    up.total()
    halve_to_last(mixed, 1)
    for _ in tp_bits[1:]:
        ffn.double()
    for _ in tp_bits[1:]:
        one.double()
    halve_to_last(heads, 1)
    up.fan()
    mixed.total()
    result = ffn.double()
    grad_tokens = one.double(full)
    grad_down = down.finish([(0, features, False)])
    mixed.fan()
    heads.total()
    grad_up = up.finish([(0, up_weight.shape[1], False)])
    heads.fan()
    small[0] = hold_small(line, small[0])
    steps = steps[: len(tp_bits)] + steps[len(tp_bits) + 1 :] + steps[len(tp_bits) : len(tp_bits) + 1]
    while steps:
        small_step(small_line)
    grad_vw, grad_out = mixed.finish([(0, width, False), (width, width, True)])
    grad_qw, grad_kw = heads.finish([(0, width, False), (width, width, False)])
    small = small[0]
    grad_table = lax.dynamic_slice(
        small[4:].reshape(-1), (me_tp * table_size,), (table_size,)
    ).reshape(NB, head_count)
    return (
        result,
        grad_tokens,
        grad_qw,
        grad_kw,
        grad_vw,
        grad_out,
        grad_up,
        grad_down,
        grad_table,
        small[0],
        small[1],
        small[2],
        small[3],
    )


def solution(mesh):
    placed = (
        P("dp", None),
        P(None, "tp"),
        P(None, "tp"),
        P(None, "tp"),
        P("tp", None),
        P(None, "tp"),
        P("tp", None),
        P(None, "tp"),
        P(),
        P(),
        P(),
        P(),
        P("dp"),
        P("dp", None),
    )
    return jax.shard_map(
        functools.partial(shards, mesh.shape["dp"], mesh.shape["tp"]),
        mesh=mesh,
        in_specs=placed,
        out_specs=(
            P("dp", None),
            P("dp", None),
            P(None, "tp"),
            P(None, "tp"),
            P(None, "tp"),
            P("tp", None),
            P(None, "tp"),
            P("tp", None),
            P(None, "tp"),
            P(),
            P(),
            P(),
            P(),
        ),
        check_vma=False,
    )
```

```python
import functools
import math

import jax
import jax.numpy as jnp
from jax import lax
from jax.experimental import pallas as pl
from jax.experimental.pallas import tpu as pltpu
from jax.sharding import PartitionSpec as P

HD = 64
NB = 32
MAXDIST = 128


epsilon = 1e-05
FRONT = {"norm_qkv": 3.5, "attn_forward": 4.5, "project_out": 6.0, "feed_forward": 7.0}
REST = {"split_add": 1.5, "join_rows": 2.0, "weight_grad": 3.0, "norm_back": 2.0, "product": 1.5, "product_back": 1.5, "attn_backward": 14.0, "add_own": 1.3, "add_up": 1.0, "join_four": 4.0, "add_small": 0.5}


def cost_of(name):
    us = FRONT[name] * 1.0 if name in FRONT else REST[name] * 0.3
    return pl.CostEstimate(flops=max(1, int(us * 1.15e9)), bytes_accessed=1, transcendentals=0)

VMEM_LIMIT = 32 * 1024 * 1024
PIECES = 2


def thresholds_list():
    exact_count = NB // 2
    thresholds = []
    for bucket in range(1, NB):
        if bucket <= exact_count:
            thresholds.append(bucket)
        else:
            thresholds.append(
                int(
                    math.ceil(
                        exact_count
                        * (MAXDIST / exact_count) ** ((bucket - exact_count) / exact_count)
                    )
                )
            )
    return thresholds


def distance_onehot(count):
    distance = jnp.arange(count, dtype=jnp.int32)
    buckets = jnp.zeros((count,), jnp.int32)
    for threshold in thresholds_list():
        buckets = buckets + (distance >= threshold).astype(jnp.int32)
    return (buckets[:, None] == jnp.arange(NB, dtype=jnp.int32)[None, :]).astype(jnp.float32)


def norm_parts(values, gain, shift):
    center = values - jnp.mean(values, axis=-1, keepdims=True)
    scaled = lax.rsqrt(jnp.mean(center * center, axis=-1, keepdims=True) + epsilon)
    normal = center * scaled
    return (normal, scaled, normal * gain + shift)


def norm_back(grad_out, normal, scaled, gain):
    grad_norm = grad_out * gain
    inner_mean = jnp.mean(grad_norm * normal, axis=-1, keepdims=True)
    return scaled * (grad_norm - jnp.mean(grad_norm, axis=-1, keepdims=True) - normal * inner_mean)


def gelu_pair(values):
    bell = jnp.exp(-0.5 * values * values)
    t = 1.0 / (1.0 + (0.3275911 * math.sqrt(0.5)) * jnp.abs(values))
    poly = 0.5 * 1.061405429
    for factor in (-1.453152027, 1.421413741, -0.284496736, 0.254829592):
        poly = poly * t + 0.5 * factor
    tail = poly * t * bell
    cdf = jnp.where(values < 0.0, tail, 1.0 - tail)
    return values * cdf, cdf + values * bell * (1.0 / math.sqrt(2.0 * math.pi))


BLK = 256
NEAR = 128
NEG = -1000000000.0
NT = (((1,), (1,)), ((), ()))
TN = (((0,), (0,)), ((), ()))


def dotf(a, b, dims=(((1,), (0,)), ((), ()))):
    return lax.dot_general(a, b, dims, preferred_element_type=jnp.float32)


def fill_bias(g_ref, bias_ref):
    row = lax.broadcasted_iota(jnp.int32, (2 * NEAR, NEAR), 0)
    col = lax.broadcasted_iota(jnp.int32, (2 * NEAR, NEAR), 1)
    hidden = row - NEAR > col
    for h in range(2):
        spread = jnp.broadcast_to(g_ref[h : h + 1, :], (2 * NEAR, 2 * NEAR))
        tile = pltpu.roll(spread, 0, 1, stride=1, stride_axis=0)[:, :NEAR]
        tile = jnp.where(hidden, NEG, tile)
        bias_ref[h, : 2 * NEAR, :NEAR] = tile
        bias_ref[h, 2 * NEAR :, :NEAR] = jnp.full((NEAR, NEAR), NEG, jnp.float32)
        bias_ref[h, :NEAR, NEAR:] = jnp.zeros((NEAR, NEAR), jnp.float32)
        bias_ref[h, NEAR:, NEAR:] = tile


def head_mask(x, h):
    lane = lax.broadcasted_iota(jnp.int32, x.shape, 1)
    return jnp.where((lane < HD) == (h == 0), x, jnp.zeros_like(x))


def add_near(st, bias_ref, h, low, blk):
    near = max(blk * BLK - NEAR, low)
    top = near - low
    tile = bias_ref[h, near - (blk * BLK - NEAR) :, :]
    if top == 0:
        return st + tile
    return jnp.concatenate([st[:top], st[top:] + tile], axis=0)


def each_block(row_count, single_ref, work):
    half = row_count // 2
    single = single_ref[0] == 1
    for blk in range(row_count // BLK):
        if blk * BLK < half:
            work(blk, 0)
        else:
            pl.when(single)(functools.partial(work, blk, 0))
            pl.when(jnp.logical_not(single))(functools.partial(work, blk, half))


def attn_fwd_kernel(single_ref, g_ref, q_ref, k_ref, v_ref, o_ref, lse_ref, bias_ref, vt_ref):
    row_count = q_ref.shape[0]
    fill_bias(g_ref, bias_ref)
    vt_ref[...] = v_ref[...].T

    def work(blk, low):
        high = (blk + 1) * BLK
        rows = slice(blk * BLK, high)
        q = q_ref[rows, :] * jnp.asarray(HD ** (-0.5), jnp.bfloat16)
        outs = []
        for h in range(2):
            st = dotf(k_ref[low:high, :], head_mask(q, h), NT)
            st = add_near(st, bias_ref, h, low, blk)
            m = jnp.max(st, axis=0, keepdims=True)
            p = jnp.exp(st - m)
            total = jnp.sum(p, axis=0, keepdims=True)
            ot = dotf(vt_ref[h * HD : (h + 1) * HD, low:high], p.astype(jnp.bfloat16))
            outs.append(ot / total)
            lse_ref[h : h + 1, rows] = m + jnp.log(total)
        o_ref[rows, :] = jnp.concatenate(outs, axis=0).T.astype(jnp.bfloat16)

    each_block(row_count, single_ref, work)


def attn_bwd_kernel(
    single_ref, g_ref, q_ref, k_ref, v_ref, o_ref, lse_ref, gr_ref, w_ref,
    dq_ref, dk_ref, dv_ref, near_ref, bias_ref, kt_ref, dk_acc, dv_acc, near_acc,
):
    row_count = q_ref.shape[0]
    fill_bias(g_ref, bias_ref)
    kt_ref[...] = k_ref[...].T
    dk_acc[...] = jnp.zeros_like(dk_acc)
    dv_acc[...] = jnp.zeros_like(dv_acc)
    near_acc[...] = jnp.zeros_like(near_acc)

    def work(blk, low):
        high = (blk + 1) * BLK
        rows = slice(blk * BLK, high)
        q = q_ref[rows, :] * jnp.asarray(HD ** (-0.5), jnp.bfloat16)
        da = dotf(gr_ref[rows, :], w_ref[...], NT).astype(jnp.bfloat16)
        prod_t = (da.astype(jnp.float32) * o_ref[rows, :].astype(jnp.float32)).T
        ps, dss, qms, dams, dqts = [], [], [], [], []
        for h in range(2):
            qm, dam = head_mask(q, h), head_mask(da, h)
            st = dotf(k_ref[low:high, :], qm, NT)
            st = add_near(st, bias_ref, h, low, blk)
            p = jnp.exp(st - lse_ref[h : h + 1, rows])
            dpt = dotf(v_ref[low:high, :], dam, NT)
            dd = jnp.sum(prod_t[h * HD : (h + 1) * HD], axis=0, keepdims=True)
            ds = p * (dpt - dd)
            own = blk * BLK - low
            if own:
                near_acc[h] += ds[own - NEAR : own + NEAR, :NEAR]
            else:
                near_acc[h, NEAR:] += ds[:NEAR, :NEAR]
            near_acc[h] += ds[own : own + 2 * NEAR, NEAR:]
            dsb = ds.astype(jnp.bfloat16)
            ps.append(p.astype(jnp.bfloat16))
            dss.append(dsb)
            qms.append(qm)
            dams.append(dam)
            dqts.append(dotf(kt_ref[h * HD : (h + 1) * HD, low:high], dsb))
        dv_acc[low:high] += dotf(jnp.concatenate(ps, axis=1), jnp.concatenate(dams, axis=0))
        dk_acc[low:high] += dotf(jnp.concatenate(dss, axis=1), jnp.concatenate(qms, axis=0))
        dq = jnp.concatenate(dqts, axis=0).T * HD ** (-0.5)
        dq_ref[rows, :] = dq.astype(jnp.bfloat16)

    each_block(row_count, single_ref, work)
    dk_ref[...] = dk_acc[...].astype(jnp.bfloat16)
    dv_ref[...] = dv_acc[...].astype(jnp.bfloat16)
    near_ref[...] = jnp.zeros_like(near_ref)
    for h in range(2):
        acc = jnp.concatenate([near_acc[h], jnp.zeros((2 * NEAR, NEAR), jnp.float32)], axis=1)
        row = lax.broadcasted_iota(jnp.int32, acc.shape, 0)
        for bit in range((2 * NEAR - 1).bit_length()):
            moved = pltpu.roll(acc, 2 * NEAR - (1 << bit), 1)
            acc = jnp.where((row & (1 << bit)) != 0, moved, acc)
        near_ref[h : h + 1, :] = jnp.sum(acc, axis=0, keepdims=True)


def pair_specs(row_count, first):
    smem = pl.BlockSpec(memory_space=pltpu.SMEM)
    cols = pl.BlockSpec((row_count, 2 * HD), lambda p: (0, first + p))
    near = pl.BlockSpec((None, 8, 2 * NEAR), lambda p: (first + p, 0, 0))
    lse = pl.BlockSpec((None, 8, row_count), lambda p: (first + p, 0, 0))
    return smem, cols, near, lse


def held(arrays):
    return [pl.BlockSpec(memory_space=pl.ANY)] * len(arrays)


def attn_forward(line, pair, single_item, g, q, k, v, also=()):
    row_count = q.shape[0]
    after = line + list(also)
    smem, cols, near, _ = pair_specs(row_count, pair)
    own = pl.BlockSpec((row_count, 2 * HD), lambda p: (0, 0))
    lse = pl.BlockSpec((8, row_count), lambda p: (0, 0))

    def kernel(*refs):
        attn_fwd_kernel(*refs[:5], *refs[5 + len(after) :])

    attended, lse_rows = pl.pallas_call(
        kernel,
        grid=(1,),
        in_specs=[smem, near, cols, cols, cols] + held(after),
        out_specs=[own, lse],
        out_shape=[
            jax.ShapeDtypeStruct((row_count, 2 * HD), jnp.bfloat16),
            jax.ShapeDtypeStruct((8, row_count), jnp.float32),
        ],
        scratch_shapes=[
            pltpu.VMEM((2, 3 * NEAR, BLK), jnp.float32),
            pltpu.VMEM((2 * HD, row_count), jnp.bfloat16),
        ],
        compiler_params=pltpu.CompilerParams(vmem_limit_bytes=VMEM_LIMIT),
        cost_estimate=cost_of("attn_forward"),
        name="attn_forward",
    )(single_item, g, q, k, v, *after)
    line[:] = [lse_rows]
    return attended, lse_rows


def attn_backward(line, single_item, g, q, k, v, o, lse_rows, grad, out_weight):
    row_count, width = q.shape
    pairs = len(o)
    after = list(line)
    smem = pl.BlockSpec(memory_space=pltpu.SMEM)
    cols = pl.BlockSpec((row_count, 2 * HD), lambda p: (0, p))
    near = pl.BlockSpec((None, 8, 2 * NEAR), lambda p: (p, 0, 0))
    flat = jax.ShapeDtypeStruct((row_count, width), jnp.bfloat16)

    def whole(x):
        return pl.BlockSpec(x.shape, lambda p: (0, 0))

    def kernel(*refs):
        o_refs, lse_refs = refs[5 : 5 + pairs], refs[5 + pairs : 5 + 2 * pairs]
        rest = refs[5 + 2 * pairs :]
        o_ref, lse_ref = rest[-2:]
        for p in range(pairs):

            @pl.when(pl.program_id(0) == p)
            def _():
                o_ref[...] = o_refs[p][...]
                lse_ref[...] = lse_refs[p][...]

        attn_bwd_kernel(*refs[:5], o_ref, lse_ref, *rest[:2], *rest[2 + len(after) : -2])

    *grads, near_totals = pl.pallas_call(
        kernel,
        grid=(pairs,),
        in_specs=[smem, near, cols, cols, cols]
        + [whole(x) for x in o]
        + [whole(x) for x in lse_rows]
        + [whole(grad), pl.BlockSpec((2 * HD, grad.shape[1]), lambda p: (p, 0))]
        + held(after),
        out_specs=[cols, cols, cols, near],
        out_shape=[flat, flat, flat, jax.ShapeDtypeStruct((pairs, 8, 2 * NEAR), jnp.float32)],
        scratch_shapes=[
            pltpu.VMEM((2, 3 * NEAR, BLK), jnp.float32),
            pltpu.VMEM((2 * HD, row_count), jnp.bfloat16),
            pltpu.VMEM((row_count, 2 * HD), jnp.float32),
            pltpu.VMEM((row_count, 2 * HD), jnp.float32),
            pltpu.VMEM((2, 2 * NEAR, NEAR), jnp.float32),
            pltpu.VMEM((row_count, 2 * HD), jnp.bfloat16),
            pltpu.VMEM((8, row_count), jnp.float32),
        ],
        compiler_params=pltpu.CompilerParams(vmem_limit_bytes=VMEM_LIMIT),
        cost_estimate=cost_of("attn_backward"),
        name="attn_backward",
    )(single_item, g, q, k, v, *o, *lse_rows, grad, out_weight, *after)
    line[:] = [near_totals]
    return *grads, near_totals


def near_bias(bias_table):
    head_count = bias_table.shape[1]
    rows = jnp.dot(
        distance_onehot(NEAR), bias_table - bias_table[NB - 1 :],
        precision=lax.Precision.HIGHEST, preferred_element_type=jnp.float32,
    ).T
    rows = jnp.pad(rows, ((0, 0), (NEAR, 0))).reshape(head_count // 2, 2, 2 * NEAR)
    return jnp.pad(rows, ((0, 0), (0, 6), (0, 0)))


def table_grad(near, head_count):
    by_dist = near[:, :2, NEAR:].reshape(head_count, NEAR)
    grad = jnp.dot(
        by_dist, distance_onehot(NEAR)[:, : NB - 1],
        precision=lax.Precision.HIGHEST, preferred_element_type=jnp.float32,
    )
    return jnp.concatenate([grad, -jnp.sum(grad, axis=1, keepdims=True)], axis=1).T


def index_bits(count):
    return [1 << i for i in range(count.bit_length() - 1)]


def sent(rows, cols):
    return pltpu.HBM((rows, cols), jnp.bfloat16)


def far(x):
    return pltpu.with_memory_space_constraint(x, pltpu.HBM)


def keep_far(x):
    return x


def swap(values, axis, count, bit):
    return lax.ppermute(values, axis, [(i, i ^ bit) for i in range(count)])


def rank_bit(axis, bit):
    return (lax.axis_index(axis) // bit) % 2


def gather_parts(values, axis, count, bits):
    parts = {0: values}
    for bit in bits:
        for k in list(parts):
            parts[k ^ bit] = swap(parts[k], axis, count, bit)
    return [parts[k] for k in range(count)]


def own_start(axis, bits, size):
    start = 0
    for bit in bits:
        size //= 2
        start = start + rank_bit(axis, bit) * size
    return start, size


def sum_over(values, axis, count, bits):
    for bit in bits:
        values = values + swap(values, axis, count, bit)
    return values


def spec(shape, index):
    return pl.BlockSpec(shape, index)


def scalars(values):
    values = values if isinstance(values, list) else [values]
    return jnp.stack([jnp.asarray(v, jnp.int32) for v in values])


def stage(line, name, body, grid, upper, ins, outs, scratch=(), also=()):
    after = line + list(also)
    shapes = [shape for shape, _ in outs] + [jax.ShapeDtypeStruct((8, 128), jnp.float32)]
    token = pl.BlockSpec((8, 128), lambda *a: (0, 0))
    held = pl.BlockSpec(memory_space=pl.ANY)

    def kernel(upper_ref, *refs):
        used = refs[: len(ins)]
        rest = refs[len(ins) + len(after) :]
        body(upper_ref, *used, *rest[: len(outs)], *rest[len(outs) + 1 :])
        rest[len(outs)][...] = jnp.zeros((8, 128), jnp.float32)

    *results, mark = pl.pallas_call(
        kernel,
        grid_spec=pltpu.PrefetchScalarGridSpec(
            num_scalar_prefetch=1,
            grid=grid,
            in_specs=[where for _, where in ins] + [held] * len(after),
            out_specs=[where for _, where in outs] + [token],
            scratch_shapes=list(scratch),
        ),
        out_shape=shapes,
        compiler_params=pltpu.CompilerParams(vmem_limit_bytes=VMEM_LIMIT),
        cost_estimate=cost_of(name),
        name=name,
    )(scalars(upper), *[x for x, _ in ins], *after)
    line[:] = [mark]
    return results if len(results) > 1 else results[0]


def cat(refs):
    return refs[0][...] if len(refs) == 1 else jnp.concatenate([r[...] for r in refs], axis=1)


def put(refs, values):
    at = 0
    for ref in refs:
        size = ref.shape[1]
        ref[...] = values[:, at : at + size].astype(ref.dtype)
        at += size


def columns(arrays, blk, index):
    return [(x, spec((blk, x.shape[1]), index)) for x in arrays]


def pieces_of(rows, cols, count, dtype=jnp.bfloat16):
    return [jax.ShapeDtypeStruct((rows, cols // count), dtype)] * count


def split_add(line, upper, kept, got, count=1):
    rows, cols = got[0].shape[0], sum(x.shape[1] for x in got)
    half = rows // 2
    blk = min(half, 128)
    n = half // blk
    a, b = len(kept), len(got)

    def body(u, *refs):
        for at, outs in ((0, refs[2 * a + 2 * b : -1]), (a + b, refs[-1:])):
            total = cat(refs[at : at + a]).astype(jnp.float32)
            put(outs, total + cat(refs[at + a : at + a + b]).astype(jnp.float32))

    away = lambda j, u: ((1 - u[0]) * n + j, 0)
    here = lambda j, u: (u[0] * n + j, 0)
    outs = pieces_of(half, cols, count) + pieces_of(half, cols, 1)
    *send, keep = stage(
        line, "split_add", body, (n,), upper,
        columns(kept + got, blk, away) + columns(kept + got, blk, here),
        [(x, spec((blk, x.shape[1]), lambda j, u: (j, 0))) for x in outs],
    )
    return send, [keep]


def add_up(line, kept, got):
    rows, cols = kept.shape
    blk = min(rows, 128)
    flat = lambda j, u: (j, 0)

    def body(u, k, g, out):
        out[...] = (k[...].astype(jnp.float32) + g[...].astype(jnp.float32)).astype(out.dtype)

    where = spec((blk, cols), flat)
    return stage(
        line, "add_up", body, (rows // blk,), 0, [(kept, where), (got, where)],
        [(jax.ShapeDtypeStruct(kept.shape, jnp.bfloat16), where)],
    )


def join_rows(line, upper, mine, got, dtype, count=1):
    rows, cols = mine[0].shape[0], sum(x.shape[1] for x in mine)
    blk = min(rows, 256)
    n = rows // blk
    a = len(mine)

    def body(u, *refs):
        i = pl.program_id(0)

        @pl.when(i == 0)
        def _():
            put(refs[2 * a :], cat(refs[:a]))

        @pl.when(i == 1)
        def _():
            put(refs[2 * a :], cat(refs[a : 2 * a]))

    joined = stage(
        line, "join_rows", body, (2, n), upper,
        columns(mine, blk, lambda i, j, u: (jnp.where(i == 0, j, n - 1), 0))
        + columns(got, blk, lambda i, j, u: (jnp.where(i == 0, 0, j), 0)),
        [
            (x, spec((blk, x.shape[1]), lambda i, j, u: (jnp.where(i == 0, u[0], 1 - u[0]) * n + j, 0)))
            for x in pieces_of(2 * rows, cols, count, dtype)
        ],
    )
    return joined if count > 1 else [joined]


def join_four(line, uppers, pieces, outs):
    rows, cols = pieces[0].shape
    blk = min(rows, 128)
    n = rows // blk

    def body(u, *refs):
        for p in range(4):

            @pl.when(pl.program_id(0) == p)
            def _():
                for out, (first, size, turned) in zip(refs[4:], outs):
                    x = refs[p][:, first : first + size].astype(jnp.float32)
                    out[...] = x.T if turned else x

    def place(i, j, u):
        high = jnp.where(i < 2, u[0], 1 - u[0])
        return (high * 2 + jnp.where(i % 2 == 0, u[1], 1 - u[1])) * n + j

    def turn(p):
        return lambda i, j, u: (jnp.where(i == p, j, jnp.where(i < p, 0, n - 1)), 0)

    results = []
    for _, size, turned in outs:
        if turned:
            results.append((jax.ShapeDtypeStruct((size, 4 * rows), jnp.float32), spec((size, blk), lambda i, j, u: (0, place(i, j, u)))))
        else:
            results.append((jax.ShapeDtypeStruct((4 * rows, size), jnp.float32), spec((blk, size), lambda i, j, u: (place(i, j, u), 0))))
    return stage(
        line, "join_four", body, (4, n), uppers,
        [(x, spec((blk, cols), turn(p))) for p, x in enumerate(pieces)], results,
    )


def weight_grad(line, upper, away, groups):
    left = groups[0][0][0]
    half = left.shape[1] // 2
    blk = min(half, 256)
    n = half // blk

    def row_spec(x, rows, cols, column, turn):
        if turn is None:
            return (x, spec((x.shape[0], cols), lambda j, u: (0, column(j, u))))
        pick = (lambda u: u[1]) if turn else (lambda u: 1 - u[1])
        if x.shape[0] == rows:
            pick = lambda u: 0
        return (x, spec((rows, cols), lambda j, u: (pick(u), column(j, u))))

    if away:
        block = lambda j, u: (1 - u[0]) * n + j
    else:
        block = lambda j, u: u[0] * n + j
    ins, plan = [], []
    for group in groups:
        terms = []
        for left, turn, rights, right_turn in group:
            rows = left.shape[0] if turn is None and right_turn is None else min(left.shape[0], rights[0].shape[0])
            if rows == left.shape[0] == rights[0].shape[0] and turn is not None:
                rows = left.shape[0] // 2
            terms.append((len(ins), len(rights)))
            ins.append(row_spec(left, rows, blk, block, turn))
            ins.extend(row_spec(r, rows, r.shape[1], lambda j, u: 0, right_turn) for r in rights)
        plan.append(terms)
    width = sum(r.shape[1] for group in groups for r in group[0][2])

    def body(u, *refs):
        out, col = refs[-1], 0
        for terms in plan:
            lefts = [refs[at][...] for at, _ in terms]
            for i in range(terms[0][1]):
                total = 0.0
                for (at, _), left_rows in zip(terms, lefts):
                    total = total + dotf(left_rows, refs[at + 1 + i][...], TN)
                out[:, col : col + total.shape[1]] = total.astype(jnp.bfloat16)
                col += total.shape[1]

    return stage(
        line, "weight_grad", body, (n,), upper, ins,
        [(jax.ShapeDtypeStruct((half, width), jnp.bfloat16), spec((blk, width), lambda j, u: (j, 0)))],
    )


def norm_back_own(line, kept, got, source, base, gain, start):
    rows, cols = kept.shape
    blk = min(rows, 128)
    n = rows // blk

    def body(s, k, g, x, b, gain_ref, out, low, sums):
        grad = k[...].astype(jnp.float32) + g[...].astype(jnp.float32)
        center = x[...].astype(jnp.float32)
        center = center - jnp.mean(center, axis=1, keepdims=True)
        scaled = lax.rsqrt(jnp.mean(center * center, axis=1, keepdims=True) + epsilon)
        normal = center * scaled
        moved = b[...].astype(jnp.float32) + norm_back(grad, normal, scaled, gain_ref[...])
        out[...] = moved
        low[...] = moved.astype(jnp.bfloat16)

        @pl.when(pl.program_id(0) == 0)
        def _():
            sums[...] = jnp.zeros_like(sums)

        sums[0:1, :] += jnp.sum(grad * normal, axis=0, keepdims=True)
        sums[1:2, :] += jnp.sum(grad, axis=0, keepdims=True)

    flat = lambda j, s: (j, 0)
    at = lambda j, s: (s[0] // blk + j, 0)
    base_at = at if base.shape[0] != rows else flat
    source_at = at if source.shape[0] != rows else flat
    whole = spec((blk, cols), flat)
    return stage(
        line, "norm_back", body, (n,), start,
        [
            (kept, whole), (got, whole), (source, spec((blk, cols), source_at)), (base, spec((blk, cols), base_at)),
            (gain.reshape(1, cols), spec((1, cols), lambda j, s: (0, 0))),
        ],
        [
            (jax.ShapeDtypeStruct((rows, cols), jnp.float32), whole),
            (jax.ShapeDtypeStruct((rows, cols), jnp.bfloat16), whole),
            (jax.ShapeDtypeStruct((8, cols), jnp.float32), spec((8, cols), lambda j, s: (0, 0))),
        ],
    )


def add_own(line, kept, got, source):
    rows, cols = kept.shape
    blk = min(rows, 128)
    flat = lambda j, s: (j, 0)

    def body(s, k, g, x, out):
        total = k[...].astype(jnp.float32) + g[...].astype(jnp.float32)
        out[...] = (x[...] + total).astype(jnp.bfloat16)

    whole = spec((blk, cols), flat)
    return stage(
        line, "add_own", body, (rows // blk,), 0,
        [(kept, whole), (got, whole), (source, whole)],
        [(jax.ShapeDtypeStruct((rows, cols), jnp.bfloat16), whole)],
    )


def fixed(x):
    return (x, spec(x.shape, lambda *a: (0, 0)))


def row(x):
    return x.reshape(1, x.shape[0])


def norm_qkv(line, tokens, gain, shift, weights):
    rows, features = tokens.shape
    blk = min(rows, 256)
    flat = lambda j, u: (j, 0)
    outs = [sent(rows, features)]
    outs += [jax.ShapeDtypeStruct((rows, w.shape[1]), jnp.bfloat16) for w in weights]

    def body(u, token_ref, gain_ref, shift_ref, *refs):
        count = len(weights)
        for part in range(2):
            at = slice(part * blk // 2, (part + 1) * blk // 2)
            normed = norm_parts(token_ref[at, :].astype(jnp.float32), gain_ref[...], shift_ref[...])[2].astype(jnp.bfloat16)
            refs[count][at, :] = normed
            for w, out in zip(refs[:count], refs[count + 1 :]):
                out[at, :] = dotf(normed, w[...]).astype(jnp.bfloat16)

    return stage(
        line, "norm_qkv", body, (rows // blk,), 0,
        [(tokens, spec((blk, features), flat)), fixed(far(row(gain))), fixed(far(row(shift)))] + [fixed(w) for w in weights],
        [(out, spec((blk, out.shape[1]), flat)) for out in outs],
    )


def project_out(line, start, own, parts, weights, tokens, gain, shift):
    rows, features = tokens.shape
    blk = min(rows, 256)
    flat = lambda j, u: (j, 0)
    pieces = [x for part in parts for x in part]
    depth = sum(w.shape[0] for w in weights)
    ins = [(tokens, spec((blk, features), flat)), fixed(far(row(gain))), fixed(far(row(shift)))]
    ins += [fixed(w) for w in weights]
    ins += [(x, spec((blk, x.shape[1]), flat)) for x in pieces]

    def body(u, *refs):
        token_ref, gain_ref, shift_ref = refs[:3]
        total_ref, normed_ref, weight = refs[-3:]
        at = 3 + len(weights)

        @pl.when(pl.program_id(0) == 0)
        def _():
            top = 0
            for ref in refs[3:at]:
                weight[top : top + ref.shape[0], :] = ref[...]
                top += ref.shape[0]

        for part in range(2):
            here = slice(part * blk // 2, (part + 1) * blk // 2)
            left = jnp.concatenate([r[here, :] for r in refs[at : at + len(pieces)]], axis=1)
            total = token_ref[here, :].astype(jnp.float32) + dotf(left, weight[...])
            first = pl.program_id(0) * blk + part * (blk // 2) - u[0]

            @pl.when(jnp.logical_and(first >= 0, first < own))
            def _():
                total_ref[pl.ds(pl.multiple_of(first, 16), blk // 2), :] = total

            normed_ref[here, :] = norm_parts(total, gain_ref[...], shift_ref[...])[2].astype(jnp.bfloat16)

    whole = spec((blk, features), flat)
    return stage(
        line, "project_out", body, (rows // blk,), start, ins,
        [
            (jax.ShapeDtypeStruct((own, features), jnp.float32), spec((own, features), lambda j, u: (0, 0))),
            (jax.ShapeDtypeStruct((rows, features), jnp.bfloat16), whole),
        ],
        scratch=[pltpu.VMEM((depth, features), jnp.bfloat16)],
    )


def turn_rows(rows, blk, turn):
    n = rows // 2 // blk
    if turn:
        return lambda j, u: (u[0] * n + j, 0)
    return lambda j, u: ((1 - u[0]) * n + j, 0)


def feed_forward(line, upper, turn, normed, cotangent, up, down, count):
    rows, features = normed.shape
    hidden = up.shape[1]
    blk = min(rows // 2, 256)
    at = turn_rows(rows, blk, turn)
    flat = lambda j, u: (j, 0)

    def body(u, normed_ref, cot_ref, up_ref, down_ref, active_ref, inner_ref, *back_refs):
        for part in range(2):
            here = slice(part * blk // 2, (part + 1) * blk // 2)
            gelu, slope = gelu_pair(dotf(normed_ref[here, :], up_ref[...]))
            active_ref[here, :] = gelu.astype(jnp.bfloat16)
            grad = (dotf(cot_ref[here, :], down_ref[...], NT) * slope).astype(jnp.bfloat16)
            inner_ref[here, :] = grad
            put([r.at[here, :] for r in back_refs], dotf(grad, up_ref[...], NT))

    outs = pieces_of(rows // 2, 2 * hidden, 2) + pieces_of(rows // 2, features, count)
    return stage(
        line, "feed_forward", body, (rows // 2 // blk,), upper,
        columns([normed, cotangent], blk, at) + [fixed(up), fixed(down)],
        [(out, spec((blk, out.shape[1]), flat)) for out in outs],
    )


def product(line, left, right, count):
    rows = left.shape[0]
    blk = min(rows, 256)
    flat = lambda j, u: (j, 0)

    def body(u, l, r, *outs):
        put(outs, dotf(l[...], r[...]))

    made = stage(
        line, "product", body, (rows // blk,), 0,
        columns([left], blk, flat) + [fixed(right)],
        [(x, spec((blk, x.shape[1]), flat)) for x in pieces_of(rows, right.shape[1], count)],
    )
    return made if count > 1 else [made]


def product_back(line, upper, turn, lefts, rights, pieces):
    rows = lefts[0][0].shape[0]
    features, width = rights[0].shape
    blk = min(rows // 2, 256)
    at = turn_rows(rows, blk, turn)
    flat = [x for left in lefts for x in left]

    def body(u, *refs):
        weight = refs[-1]

        @pl.when(pl.program_id(0) == 0)
        def _():
            for i, r in enumerate(refs[len(flat) : len(flat) + len(rights)]):
                weight[:, i * width : (i + 1) * width] = r[...]

        put(refs[len(flat) + len(rights) : -1], dotf(cat(refs[: len(flat)]), weight[...], NT))

    made = stage(
        line, "product_back", body, (rows // 2 // blk,), upper,
        columns(flat, blk, at) + [fixed(r) for r in rights],
        [(x, spec((blk, x.shape[1]), lambda j, u: (j, 0))) for x in pieces_of(rows // 2, features, pieces)],
        scratch=[pltpu.VMEM((features, len(rights) * width), jnp.bfloat16)],
    )
    return made if pieces > 1 else [made]


def hold_small(line, mine):
    def body(u, m, out):
        out[...] = m[...]

    return stage(line, "add_small", body, (1,), 0, [fixed(mine)], [(jax.ShapeDtypeStruct(mine.shape, mine.dtype), fixed(mine)[1])])


def add_small(line, mine, got):
    def body(u, m, g, out):
        out[...] = m[...] + g[...]

    return stage(line, "add_small", body, (1,), 0, [fixed(mine), fixed(got)], [(jax.ShapeDtypeStruct(mine.shape, mine.dtype), fixed(mine)[1])])


def shards(
    n_dp,
    n_tp,
    tokens,
    query_weight,
    key_weight,
    value_weight,
    out_weight,
    up_weight,
    down_weight,
    bias_table,
    gain_one,
    shift_one,
    gain_two,
    shift_two,
    single_item,
    cotangent,
):
    tp_bits = index_bits(n_tp)
    dp_bits = index_bits(n_dp)
    far_first = tp_bits[1:] + tp_bits[:1]
    low = jnp.bfloat16
    full = jnp.float32
    row_count, features = tokens.shape
    head_count = bias_table.shape[1]
    width = head_count * HD
    tp_up = [rank_bit("tp", bit) for bit in tp_bits]
    dp_up = [rank_bit("dp", bit) for bit in dp_bits]
    start, own_count = own_start("tp", tp_bits, row_count)

    def tp_swap(values, i):
        return swap(values, "tp", n_tp, tp_bits[i])

    def dp_swap(values, i):
        return swap(values, "dp", n_dp, dp_bits[i])

    line = []

    class Sum:
        def __init__(self, axis, send, keep):
            self.axis = axis
            self.up = tp_up if axis == "tp" else dp_up
            self.keep, self.at = keep, 0
            self.swap(send)

        def swap(self, arrays):
            self.got = [keep_far((tp_swap if self.axis == "tp" else dp_swap)(x, self.at)) for x in arrays]

        def count(self, at):
            return PIECES if self.axis == "tp" and at == 0 else 1

        def halve(self):
            self.at += 1
            if self.axis == "dp" and self.at == len(self.up) - 1:
                self.keep = [add_up(line, self.keep[0], self.got[0])]
                self.swap(self.keep)
            else:
                send, self.keep = split_add(line, self.up[self.at], self.keep, self.got, self.count(self.at))
                self.swap(send)

        def spread(self, values):
            self.keep = values
            self.swap(values)

        def total(self):
            pass

        def fan(self):
            mine = [add_up(line, self.keep[0], self.got[0])]
            self.at -= 1
            while self.at > 1:
                self.spread(mine)
                mine = [join_rows(line, self.up[self.at], self.keep, self.got, low)[0]]
                self.at -= 1
            self.mine = mine[0]
            self.near = dp_swap(self.mine, 1)
            self.far = [dp_swap(self.mine, 0), dp_swap(self.near, 0)]

        def finish(self, outs):
            return join_four(line, self.up[:2], [self.mine, self.near] + self.far, outs)

        def double(self, dtype=low):
            count = self.count(self.at - 1) if self.at else 1
            joined = join_rows(line, self.up[self.at], self.keep, self.got, dtype, count)
            if self.at == 0:
                return joined[0]
            self.at -= 1
            self.spread(joined)

    out_parts = gather_parts(out_weight, "tp", n_tp, far_first)
    near_rows = near_bias(bias_table)
    normed_low, queries, key_rows, value_rows = norm_qkv(
        line, far(tokens), gain_one, shift_one, [far(w) for w in (query_weight, key_weight, value_weight)]
    )
    pairs = width // (2 * HD)
    attended, lse_rows, parts = [], [], []
    for pair in range(pairs):
        also = [out_parts[far_first[0]][:8, :128]] if pair == pairs - 1 else ()
        columns, sums = attn_forward(
            line, pair, single_item, near_rows, queries, key_rows, value_rows, also
        )
        attended.append(columns)
        lse_rows.append(sums)
        parts.append(gather_parts(columns, "tp", n_tp, far_first))
    parts = [[far(parts[pair][k]) if k else parts[pair][k] for pair in range(pairs)] for k in range(n_tp)]
    out_parts = [far(w) for w in out_parts]
    residual, normed_two_low = project_out(
        line, start, own_count, parts, out_parts, far(tokens), gain_two, shift_two
    )
    fed = [
        feed_forward(line, tp_up[0], turn, normed_two_low, cotangent, up_weight, down_weight, PIECES)
        for turn in (0, 1)
    ]
    two = Sum("tp", fed[0][2:], fed[1][2:])
    ups = [dp_up[0], tp_up[0]]
    down_group = [[(fed[turn][0], turn, [cotangent], turn) for turn in (0, 1)]]
    up_group = [[(normed_two_low, turn, [fed[turn][1]], turn) for turn in (0, 1)]]

    def halve_to_last(total, done):
        for _ in range(len(total.up) - 1 - done):
            total.halve()

    halve_to_last(two, 0)
    down_send = weight_grad(line, ups, True, down_group)
    down_keep = weight_grad(line, ups, False, down_group)
    down = Sum("dp", [down_send], [down_keep])
    ffn = Sum("tp", *[product(line, fed[turn][0], down_weight, PIECES) for turn in (0, 1)])
    up_keep = weight_grad(line, ups, False, up_group)
    grad_residual, grad_residual_low, sums_two = norm_back_own(
        line, two.keep[0], two.got[0], residual, cotangent, gain_two, start
    )
    two.spread([grad_residual_low])
    down.halve()
    up_send = weight_grad(line, ups, True, up_group)
    up = Sum("dp", [up_send], [up_keep])
    for _ in tp_bits[1:]:
        two.double()
    halve_to_last(ffn, 0)
    grad_residual_low = two.double()
    grad_query, grad_key, grad_value, near_totals = attn_backward(
        line, single_item, near_rows, queries, key_rows, value_rows, attended, lse_rows,
        grad_residual_low, out_weight,
    )
    grad_table = table_grad(near_totals, head_count)
    heads_back = [[grad_query], [grad_key], [grad_value]]
    head_weights = [query_weight, key_weight, value_weight]
    mixed_group = [
        [(normed_low, None, heads_back[2], None)],
        [(grad_residual_low, None, attended, None)],
    ]
    heads_group = [[(normed_low, None, heads_back[0] + heads_back[1], None)]]
    halve_to_last(down, 1)
    one = Sum("tp", *[product_back(line, tp_up[0], turn, heads_back, head_weights, PIECES) for turn in (0, 1)])
    mixed_send = weight_grad(line, ups, True, mixed_group)
    halve_to_last(one, 0)
    up.halve()
    mixed = Sum("dp", [mixed_send], [weight_grad(line, ups, False, mixed_group)])
    heads_send = weight_grad(line, ups, True, heads_group)
    heads = Sum("dp", [heads_send], [weight_grad(line, ups, False, heads_group)])
    _, grad_tokens, sums_one = norm_back_own(
        line, one.keep[0], one.got[0], tokens, grad_residual, gain_one, start
    )
    one.spread([grad_tokens])
    table_size = NB * head_count
    slot = jnp.zeros((n_tp * table_size,), full)
    me_tp = lax.axis_index("tp")
    slot = lax.dynamic_update_slice(slot, grad_table.reshape(table_size), (me_tp * table_size,))
    slot = jnp.pad(slot, (0, -slot.size % features)).reshape(-1, features)
    small = [jnp.concatenate([sums_one[:2], sums_two[:2], slot])]
    steps = [("tp", n_tp, bit) for bit in tp_bits] + [("dp", n_dp, bit) for bit in dp_bits]
    small_line = []

    def small_step(use):
        if steps:
            axis, count, bit = steps.pop(0)
            small[0] = add_small(use, small[0], swap(small[0], axis, count, bit))

    mixed.halve()
    halve_to_last(up, 1)
    down.total()
    down.fan()
    ffn.spread([add_own(line, ffn.keep[0], ffn.got[0], residual)])
    heads.halve()
    for _ in tp_bits[1:]:
        ffn.double()
    halve_to_last(mixed, 1)
    for _ in tp_bits[1:]:
        one.double()
    up.total()
    up.fan()
    halve_to_last(heads, 1)
    result = ffn.double()
    grad_down = down.finish([(0, features, False)])
    grad_tokens = one.double(full)
    mixed.total()
    mixed.fan()
    heads.total()
    grad_up = up.finish([(0, up_weight.shape[1], False)])
    heads.fan()
    small[0] = hold_small(line, small[0])
    steps = steps[: len(tp_bits)] + steps[len(tp_bits) + 1 :] + steps[len(tp_bits) : len(tp_bits) + 1]
    while steps:
        small_step(small_line)
    grad_vw, grad_out = mixed.finish([(0, width, False), (width, width, True)])
    grad_qw, grad_kw = heads.finish([(0, width, False), (width, width, False)])
    small = small[0]
    grad_table = lax.dynamic_slice(
        small[4:].reshape(-1), (me_tp * table_size,), (table_size,)
    ).reshape(NB, head_count)
    return (
        result,
        grad_tokens,
        grad_qw,
        grad_kw,
        grad_vw,
        grad_out,
        grad_up,
        grad_down,
        grad_table,
        small[0],
        small[1],
        small[2],
        small[3],
    )


def solution(mesh):
    placed = (
        P("dp", None),
        P(None, "tp"),
        P(None, "tp"),
        P(None, "tp"),
        P("tp", None),
        P(None, "tp"),
        P("tp", None),
        P(None, "tp"),
        P(),
        P(),
        P(),
        P(),
        P("dp"),
        P("dp", None),
    )
    return jax.shard_map(
        functools.partial(shards, mesh.shape["dp"], mesh.shape["tp"]),
        mesh=mesh,
        in_specs=placed,
        out_specs=(
            P("dp", None),
            P("dp", None),
            P(None, "tp"),
            P(None, "tp"),
            P(None, "tp"),
            P("tp", None),
            P(None, "tp"),
            P("tp", None),
            P(None, "tp"),
            P(),
            P(),
            P(),
            P(),
        ),
        check_vma=False,
    )
```

```python
import functools
import math

import jax
import jax.numpy as jnp
from jax import lax
from jax.experimental import pallas as pl
from jax.experimental.pallas import tpu as pltpu
from jax.sharding import PartitionSpec as P

HD = 64
NB = 32
MAXDIST = 128


epsilon = 1e-05
FRONT = {"norm_qkv": 3.5, "attn_forward": 4.5, "project_out": 6.0, "feed_forward": 7.0}
REST = {"split_add": 1.5, "join_rows": 2.0, "weight_grad": 3.0, "norm_back": 2.0, "product": 1.5, "product_back": 1.5, "attn_backward": 14.0, "add_own": 1.3, "add_up": 1.0, "join_four": 4.0, "add_small": 0.5}


def cost_of(name):
    us = FRONT[name] * 1.0 if name in FRONT else REST[name] * 0.3
    return pl.CostEstimate(flops=max(1, int(us * 1.15e9)), bytes_accessed=1, transcendentals=0)

VMEM_LIMIT = 32 * 1024 * 1024
PIECES = 2


def thresholds_list():
    exact_count = NB // 2
    thresholds = []
    for bucket in range(1, NB):
        if bucket <= exact_count:
            thresholds.append(bucket)
        else:
            thresholds.append(
                int(
                    math.ceil(
                        exact_count
                        * (MAXDIST / exact_count) ** ((bucket - exact_count) / exact_count)
                    )
                )
            )
    return thresholds


def distance_onehot(count):
    distance = jnp.arange(count, dtype=jnp.int32)
    buckets = jnp.zeros((count,), jnp.int32)
    for threshold in thresholds_list():
        buckets = buckets + (distance >= threshold).astype(jnp.int32)
    return (buckets[:, None] == jnp.arange(NB, dtype=jnp.int32)[None, :]).astype(jnp.float32)


def norm_parts(values, gain, shift):
    center = values - jnp.mean(values, axis=-1, keepdims=True)
    scaled = lax.rsqrt(jnp.mean(center * center, axis=-1, keepdims=True) + epsilon)
    normal = center * scaled
    return (normal, scaled, normal * gain + shift)


def norm_back(grad_out, normal, scaled, gain):
    grad_norm = grad_out * gain
    inner_mean = jnp.mean(grad_norm * normal, axis=-1, keepdims=True)
    return scaled * (grad_norm - jnp.mean(grad_norm, axis=-1, keepdims=True) - normal * inner_mean)


def gelu_pair(values):
    bell = jnp.exp(-0.5 * values * values)
    t = 1.0 / (1.0 + (0.3275911 * math.sqrt(0.5)) * jnp.abs(values))
    poly = 0.5 * 1.061405429
    for factor in (-1.453152027, 1.421413741, -0.284496736, 0.254829592):
        poly = poly * t + 0.5 * factor
    tail = poly * t * bell
    cdf = jnp.where(values < 0.0, tail, 1.0 - tail)
    return values * cdf, cdf + values * bell * (1.0 / math.sqrt(2.0 * math.pi))


BLK = 256
NEAR = 128
NEG = -1000000000.0
NT = (((1,), (1,)), ((), ()))
TN = (((0,), (0,)), ((), ()))


def dotf(a, b, dims=(((1,), (0,)), ((), ()))):
    return lax.dot_general(a, b, dims, preferred_element_type=jnp.float32)


def fill_bias(g_ref, bias_ref):
    row = lax.broadcasted_iota(jnp.int32, (2 * NEAR, NEAR), 0)
    col = lax.broadcasted_iota(jnp.int32, (2 * NEAR, NEAR), 1)
    hidden = row - NEAR > col
    for h in range(2):
        spread = jnp.broadcast_to(g_ref[h : h + 1, :], (2 * NEAR, 2 * NEAR))
        tile = pltpu.roll(spread, 0, 1, stride=1, stride_axis=0)[:, :NEAR]
        tile = jnp.where(hidden, NEG, tile)
        bias_ref[h, : 2 * NEAR, :NEAR] = tile
        bias_ref[h, 2 * NEAR :, :NEAR] = jnp.full((NEAR, NEAR), NEG, jnp.float32)
        bias_ref[h, :NEAR, NEAR:] = jnp.zeros((NEAR, NEAR), jnp.float32)
        bias_ref[h, NEAR:, NEAR:] = tile


def head_mask(x, h):
    lane = lax.broadcasted_iota(jnp.int32, x.shape, 1)
    return jnp.where((lane < HD) == (h == 0), x, jnp.zeros_like(x))


def add_near(st, bias_ref, h, low, blk):
    near = max(blk * BLK - NEAR, low)
    top = near - low
    tile = bias_ref[h, near - (blk * BLK - NEAR) :, :]
    if top == 0:
        return st + tile
    return jnp.concatenate([st[:top], st[top:] + tile], axis=0)


def each_block(row_count, single_ref, work):
    half = row_count // 2
    single = single_ref[0] == 1
    for blk in range(row_count // BLK):
        if blk * BLK < half:
            work(blk, 0)
        else:
            pl.when(single)(functools.partial(work, blk, 0))
            pl.when(jnp.logical_not(single))(functools.partial(work, blk, half))


def attn_fwd_kernel(single_ref, g_ref, q_ref, k_ref, v_ref, o_ref, lse_ref, bias_ref, vt_ref):
    row_count = q_ref.shape[0]
    fill_bias(g_ref, bias_ref)
    vt_ref[...] = v_ref[...].T

    def work(blk, low):
        high = (blk + 1) * BLK
        rows = slice(blk * BLK, high)
        q = q_ref[rows, :] * jnp.asarray(HD ** (-0.5), jnp.bfloat16)
        outs = []
        for h in range(2):
            st = dotf(k_ref[low:high, :], head_mask(q, h), NT)
            st = add_near(st, bias_ref, h, low, blk)
            m = jnp.max(st, axis=0, keepdims=True)
            p = jnp.exp(st - m)
            total = jnp.sum(p, axis=0, keepdims=True)
            ot = dotf(vt_ref[h * HD : (h + 1) * HD, low:high], p.astype(jnp.bfloat16))
            outs.append(ot / total)
            lse_ref[h : h + 1, rows] = m + jnp.log(total)
        o_ref[rows, :] = jnp.concatenate(outs, axis=0).T.astype(jnp.bfloat16)

    each_block(row_count, single_ref, work)


def attn_bwd_kernel(
    single_ref, g_ref, q_ref, k_ref, v_ref, o_ref, lse_ref, gr_ref, w_ref,
    dq_ref, dk_ref, dv_ref, near_ref, bias_ref, kt_ref, dk_acc, dv_acc, near_acc,
):
    row_count = q_ref.shape[0]
    fill_bias(g_ref, bias_ref)
    kt_ref[...] = k_ref[...].T
    dk_acc[...] = jnp.zeros_like(dk_acc)
    dv_acc[...] = jnp.zeros_like(dv_acc)
    near_acc[...] = jnp.zeros_like(near_acc)

    def work(blk, low):
        high = (blk + 1) * BLK
        rows = slice(blk * BLK, high)
        q = q_ref[rows, :] * jnp.asarray(HD ** (-0.5), jnp.bfloat16)
        da = dotf(gr_ref[rows, :], w_ref[...], NT).astype(jnp.bfloat16)
        prod_t = (da.astype(jnp.float32) * o_ref[rows, :].astype(jnp.float32)).T
        ps, dss, qms, dams, dqts = [], [], [], [], []
        for h in range(2):
            qm, dam = head_mask(q, h), head_mask(da, h)
            st = dotf(k_ref[low:high, :], qm, NT)
            st = add_near(st, bias_ref, h, low, blk)
            p = jnp.exp(st - lse_ref[h : h + 1, rows])
            dpt = dotf(v_ref[low:high, :], dam, NT)
            dd = jnp.sum(prod_t[h * HD : (h + 1) * HD], axis=0, keepdims=True)
            ds = p * (dpt - dd)
            own = blk * BLK - low
            if own:
                near_acc[h] += ds[own - NEAR : own + NEAR, :NEAR]
            else:
                near_acc[h, NEAR:] += ds[:NEAR, :NEAR]
            near_acc[h] += ds[own : own + 2 * NEAR, NEAR:]
            dsb = ds.astype(jnp.bfloat16)
            ps.append(p.astype(jnp.bfloat16))
            dss.append(dsb)
            qms.append(qm)
            dams.append(dam)
            dqts.append(dotf(kt_ref[h * HD : (h + 1) * HD, low:high], dsb))
        dv_acc[low:high] += dotf(jnp.concatenate(ps, axis=1), jnp.concatenate(dams, axis=0))
        dk_acc[low:high] += dotf(jnp.concatenate(dss, axis=1), jnp.concatenate(qms, axis=0))
        dq = jnp.concatenate(dqts, axis=0).T * HD ** (-0.5)
        dq_ref[rows, :] = dq.astype(jnp.bfloat16)

    each_block(row_count, single_ref, work)
    dk_ref[...] = dk_acc[...].astype(jnp.bfloat16)
    dv_ref[...] = dv_acc[...].astype(jnp.bfloat16)
    near_ref[...] = jnp.zeros_like(near_ref)
    for h in range(2):
        acc = jnp.concatenate([near_acc[h], jnp.zeros((2 * NEAR, NEAR), jnp.float32)], axis=1)
        row = lax.broadcasted_iota(jnp.int32, acc.shape, 0)
        for bit in range((2 * NEAR - 1).bit_length()):
            moved = pltpu.roll(acc, 2 * NEAR - (1 << bit), 1)
            acc = jnp.where((row & (1 << bit)) != 0, moved, acc)
        near_ref[h : h + 1, :] = jnp.sum(acc, axis=0, keepdims=True)


def pair_specs(row_count, first):
    smem = pl.BlockSpec(memory_space=pltpu.SMEM)
    cols = pl.BlockSpec((row_count, 2 * HD), lambda p: (0, first + p))
    near = pl.BlockSpec((None, 8, 2 * NEAR), lambda p: (first + p, 0, 0))
    lse = pl.BlockSpec((None, 8, row_count), lambda p: (first + p, 0, 0))
    return smem, cols, near, lse


def held(arrays):
    return [pl.BlockSpec(memory_space=pl.ANY)] * len(arrays)


def attn_forward(line, pair, single_item, g, q, k, v, also=()):
    row_count = q.shape[0]
    after = line + list(also)
    smem, cols, near, _ = pair_specs(row_count, pair)
    own = pl.BlockSpec((row_count, 2 * HD), lambda p: (0, 0))
    lse = pl.BlockSpec((8, row_count), lambda p: (0, 0))

    def kernel(*refs):
        attn_fwd_kernel(*refs[:5], *refs[5 + len(after) :])

    attended, lse_rows = pl.pallas_call(
        kernel,
        grid=(1,),
        in_specs=[smem, near, cols, cols, cols] + held(after),
        out_specs=[own, lse],
        out_shape=[
            jax.ShapeDtypeStruct((row_count, 2 * HD), jnp.bfloat16),
            jax.ShapeDtypeStruct((8, row_count), jnp.float32),
        ],
        scratch_shapes=[
            pltpu.VMEM((2, 3 * NEAR, BLK), jnp.float32),
            pltpu.VMEM((2 * HD, row_count), jnp.bfloat16),
        ],
        compiler_params=pltpu.CompilerParams(vmem_limit_bytes=VMEM_LIMIT),
        cost_estimate=cost_of("attn_forward"),
        name="attn_forward",
    )(single_item, g, q, k, v, *after)
    line[:] = [lse_rows]
    return attended, lse_rows


def attn_backward(line, single_item, g, q, k, v, o, lse_rows, grad, out_weight):
    row_count, width = q.shape
    pairs = len(o)
    after = list(line)
    smem = pl.BlockSpec(memory_space=pltpu.SMEM)
    cols = pl.BlockSpec((row_count, 2 * HD), lambda p: (0, p))
    near = pl.BlockSpec((None, 8, 2 * NEAR), lambda p: (p, 0, 0))
    flat = jax.ShapeDtypeStruct((row_count, width), jnp.bfloat16)

    def whole(x):
        return pl.BlockSpec(x.shape, lambda p: (0, 0))

    def kernel(*refs):
        o_refs, lse_refs = refs[5 : 5 + pairs], refs[5 + pairs : 5 + 2 * pairs]
        rest = refs[5 + 2 * pairs :]
        o_ref, lse_ref = rest[-2:]
        for p in range(pairs):

            @pl.when(pl.program_id(0) == p)
            def _():
                o_ref[...] = o_refs[p][...]
                lse_ref[...] = lse_refs[p][...]

        attn_bwd_kernel(*refs[:5], o_ref, lse_ref, *rest[:2], *rest[2 + len(after) : -2])

    *grads, near_totals = pl.pallas_call(
        kernel,
        grid=(pairs,),
        in_specs=[smem, near, cols, cols, cols]
        + [whole(x) for x in o]
        + [whole(x) for x in lse_rows]
        + [whole(grad), pl.BlockSpec((2 * HD, grad.shape[1]), lambda p: (p, 0))]
        + held(after),
        out_specs=[cols, cols, cols, near],
        out_shape=[flat, flat, flat, jax.ShapeDtypeStruct((pairs, 8, 2 * NEAR), jnp.float32)],
        scratch_shapes=[
            pltpu.VMEM((2, 3 * NEAR, BLK), jnp.float32),
            pltpu.VMEM((2 * HD, row_count), jnp.bfloat16),
            pltpu.VMEM((row_count, 2 * HD), jnp.float32),
            pltpu.VMEM((row_count, 2 * HD), jnp.float32),
            pltpu.VMEM((2, 2 * NEAR, NEAR), jnp.float32),
            pltpu.VMEM((row_count, 2 * HD), jnp.bfloat16),
            pltpu.VMEM((8, row_count), jnp.float32),
        ],
        compiler_params=pltpu.CompilerParams(vmem_limit_bytes=VMEM_LIMIT),
        cost_estimate=cost_of("attn_backward"),
        name="attn_backward",
    )(single_item, g, q, k, v, *o, *lse_rows, grad, out_weight, *after)
    line[:] = [near_totals]
    return *grads, near_totals


def near_bias(bias_table):
    head_count = bias_table.shape[1]
    rows = jnp.dot(
        distance_onehot(NEAR), bias_table - bias_table[NB - 1 :],
        precision=lax.Precision.HIGHEST, preferred_element_type=jnp.float32,
    ).T
    rows = jnp.pad(rows, ((0, 0), (NEAR, 0))).reshape(head_count // 2, 2, 2 * NEAR)
    return jnp.pad(rows, ((0, 0), (0, 6), (0, 0)))


def table_grad(near, head_count):
    by_dist = near[:, :2, NEAR:].reshape(head_count, NEAR)
    grad = jnp.dot(
        by_dist, distance_onehot(NEAR)[:, : NB - 1],
        precision=lax.Precision.HIGHEST, preferred_element_type=jnp.float32,
    )
    return jnp.concatenate([grad, -jnp.sum(grad, axis=1, keepdims=True)], axis=1).T


def index_bits(count):
    return [1 << i for i in range(count.bit_length() - 1)]


def sent(rows, cols):
    return pltpu.HBM((rows, cols), jnp.bfloat16)


def far(x):
    return pltpu.with_memory_space_constraint(x, pltpu.HBM)


def keep_far(x):
    return x


def swap(values, axis, count, bit):
    return lax.ppermute(values, axis, [(i, i ^ bit) for i in range(count)])


def rank_bit(axis, bit):
    return (lax.axis_index(axis) // bit) % 2


def gather_parts(values, axis, count, bits):
    parts = {0: values}
    for bit in bits:
        for k in list(parts):
            parts[k ^ bit] = swap(parts[k], axis, count, bit)
    return [parts[k] for k in range(count)]


def own_start(axis, bits, size):
    start = 0
    for bit in bits:
        size //= 2
        start = start + rank_bit(axis, bit) * size
    return start, size


def sum_over(values, axis, count, bits):
    for bit in bits:
        values = values + swap(values, axis, count, bit)
    return values


def spec(shape, index):
    return pl.BlockSpec(shape, index)


def scalars(values):
    values = values if isinstance(values, list) else [values]
    return jnp.stack([jnp.asarray(v, jnp.int32) for v in values])


def stage(line, name, body, grid, upper, ins, outs, scratch=(), also=()):
    after = line + list(also)
    shapes = [shape for shape, _ in outs] + [jax.ShapeDtypeStruct((8, 128), jnp.float32)]
    token = pl.BlockSpec((8, 128), lambda *a: (0, 0))
    held = pl.BlockSpec(memory_space=pl.ANY)

    def kernel(upper_ref, *refs):
        used = refs[: len(ins)]
        rest = refs[len(ins) + len(after) :]
        body(upper_ref, *used, *rest[: len(outs)], *rest[len(outs) + 1 :])
        rest[len(outs)][...] = jnp.zeros((8, 128), jnp.float32)

    *results, mark = pl.pallas_call(
        kernel,
        grid_spec=pltpu.PrefetchScalarGridSpec(
            num_scalar_prefetch=1,
            grid=grid,
            in_specs=[where for _, where in ins] + [held] * len(after),
            out_specs=[where for _, where in outs] + [token],
            scratch_shapes=list(scratch),
        ),
        out_shape=shapes,
        compiler_params=pltpu.CompilerParams(vmem_limit_bytes=VMEM_LIMIT),
        cost_estimate=cost_of(name),
        name=name,
    )(scalars(upper), *[x for x, _ in ins], *after)
    line[:] = [mark]
    return results if len(results) > 1 else results[0]


def cat(refs):
    return refs[0][...] if len(refs) == 1 else jnp.concatenate([r[...] for r in refs], axis=1)


def put(refs, values):
    at = 0
    for ref in refs:
        size = ref.shape[1]
        ref[...] = values[:, at : at + size].astype(ref.dtype)
        at += size


def columns(arrays, blk, index):
    return [(x, spec((blk, x.shape[1]), index)) for x in arrays]


def pieces_of(rows, cols, count, dtype=jnp.bfloat16):
    return [jax.ShapeDtypeStruct((rows, cols // count), dtype)] * count


def split_add(line, upper, kept, got, count=1):
    rows, cols = got[0].shape[0], sum(x.shape[1] for x in got)
    half = rows // 2
    blk = min(half, 128)
    n = half // blk
    a, b = len(kept), len(got)

    def body(u, *refs):
        for at, outs in ((0, refs[2 * a + 2 * b : -1]), (a + b, refs[-1:])):
            total = cat(refs[at : at + a]).astype(jnp.float32)
            put(outs, total + cat(refs[at + a : at + a + b]).astype(jnp.float32))

    away = lambda j, u: ((1 - u[0]) * n + j, 0)
    here = lambda j, u: (u[0] * n + j, 0)
    outs = pieces_of(half, cols, count) + pieces_of(half, cols, 1)
    *send, keep = stage(
        line, "split_add", body, (n,), upper,
        columns(kept + got, blk, away) + columns(kept + got, blk, here),
        [(x, spec((blk, x.shape[1]), lambda j, u: (j, 0))) for x in outs],
    )
    return send, [keep]


def add_up(line, kept, got):
    rows, cols = kept.shape
    blk = min(rows, 128)
    flat = lambda j, u: (j, 0)

    def body(u, k, g, out):
        out[...] = (k[...].astype(jnp.float32) + g[...].astype(jnp.float32)).astype(out.dtype)

    where = spec((blk, cols), flat)
    return stage(
        line, "add_up", body, (rows // blk,), 0, [(kept, where), (got, where)],
        [(jax.ShapeDtypeStruct(kept.shape, jnp.bfloat16), where)],
    )


def join_rows(line, upper, mine, got, dtype, count=1):
    rows, cols = mine[0].shape[0], sum(x.shape[1] for x in mine)
    blk = min(rows, 256)
    n = rows // blk
    a = len(mine)

    def body(u, *refs):
        i = pl.program_id(0)

        @pl.when(i == 0)
        def _():
            put(refs[2 * a :], cat(refs[:a]))

        @pl.when(i == 1)
        def _():
            put(refs[2 * a :], cat(refs[a : 2 * a]))

    joined = stage(
        line, "join_rows", body, (2, n), upper,
        columns(mine, blk, lambda i, j, u: (jnp.where(i == 0, j, n - 1), 0))
        + columns(got, blk, lambda i, j, u: (jnp.where(i == 0, 0, j), 0)),
        [
            (x, spec((blk, x.shape[1]), lambda i, j, u: (jnp.where(i == 0, u[0], 1 - u[0]) * n + j, 0)))
            for x in pieces_of(2 * rows, cols, count, dtype)
        ],
    )
    return joined if count > 1 else [joined]


def join_four(line, uppers, pieces, outs):
    rows, cols = pieces[0].shape
    blk = min(rows, 128)
    n = rows // blk

    def body(u, *refs):
        for p in range(4):

            @pl.when(pl.program_id(0) == p)
            def _():
                for out, (first, size, turned) in zip(refs[4:], outs):
                    x = refs[p][:, first : first + size].astype(jnp.float32)
                    out[...] = x.T if turned else x

    def place(i, j, u):
        high = jnp.where(i < 2, u[0], 1 - u[0])
        return (high * 2 + jnp.where(i % 2 == 0, u[1], 1 - u[1])) * n + j

    def turn(p):
        return lambda i, j, u: (jnp.where(i == p, j, jnp.where(i < p, 0, n - 1)), 0)

    results = []
    for _, size, turned in outs:
        if turned:
            results.append((jax.ShapeDtypeStruct((size, 4 * rows), jnp.float32), spec((size, blk), lambda i, j, u: (0, place(i, j, u)))))
        else:
            results.append((jax.ShapeDtypeStruct((4 * rows, size), jnp.float32), spec((blk, size), lambda i, j, u: (place(i, j, u), 0))))
    return stage(
        line, "join_four", body, (4, n), uppers,
        [(x, spec((blk, cols), turn(p))) for p, x in enumerate(pieces)], results,
    )


def weight_grad(line, upper, away, groups):
    left = groups[0][0][0]
    half = left.shape[1] // 2
    blk = min(half, 256)
    n = half // blk

    def row_spec(x, rows, cols, column, turn):
        if turn is None:
            return (x, spec((x.shape[0], cols), lambda j, u: (0, column(j, u))))
        pick = (lambda u: u[1]) if turn else (lambda u: 1 - u[1])
        if x.shape[0] == rows:
            pick = lambda u: 0
        return (x, spec((rows, cols), lambda j, u: (pick(u), column(j, u))))

    if away:
        block = lambda j, u: (1 - u[0]) * n + j
    else:
        block = lambda j, u: u[0] * n + j
    ins, plan = [], []
    for group in groups:
        terms = []
        for left, turn, rights, right_turn in group:
            rows = left.shape[0] if turn is None and right_turn is None else min(left.shape[0], rights[0].shape[0])
            if rows == left.shape[0] == rights[0].shape[0] and turn is not None:
                rows = left.shape[0] // 2
            terms.append((len(ins), len(rights)))
            ins.append(row_spec(left, rows, blk, block, turn))
            ins.extend(row_spec(r, rows, r.shape[1], lambda j, u: 0, right_turn) for r in rights)
        plan.append(terms)
    width = sum(r.shape[1] for group in groups for r in group[0][2])

    def body(u, *refs):
        out, col = refs[-1], 0
        for terms in plan:
            lefts = [refs[at][...] for at, _ in terms]
            for i in range(terms[0][1]):
                total = 0.0
                for (at, _), left_rows in zip(terms, lefts):
                    total = total + dotf(left_rows, refs[at + 1 + i][...], TN)
                out[:, col : col + total.shape[1]] = total.astype(jnp.bfloat16)
                col += total.shape[1]

    return stage(
        line, "weight_grad", body, (n,), upper, ins,
        [(jax.ShapeDtypeStruct((half, width), jnp.bfloat16), spec((blk, width), lambda j, u: (j, 0)))],
    )


def norm_back_own(line, kept, got, source, base, gain, start):
    rows, cols = kept.shape
    blk = min(rows, 128)
    n = rows // blk

    def body(s, k, g, x, b, gain_ref, out, low, sums):
        grad = k[...].astype(jnp.float32) + g[...].astype(jnp.float32)
        center = x[...].astype(jnp.float32)
        center = center - jnp.mean(center, axis=1, keepdims=True)
        scaled = lax.rsqrt(jnp.mean(center * center, axis=1, keepdims=True) + epsilon)
        normal = center * scaled
        moved = b[...].astype(jnp.float32) + norm_back(grad, normal, scaled, gain_ref[...])
        out[...] = moved
        low[...] = moved.astype(jnp.bfloat16)

        @pl.when(pl.program_id(0) == 0)
        def _():
            sums[...] = jnp.zeros_like(sums)

        sums[0:1, :] += jnp.sum(grad * normal, axis=0, keepdims=True)
        sums[1:2, :] += jnp.sum(grad, axis=0, keepdims=True)

    flat = lambda j, s: (j, 0)
    at = lambda j, s: (s[0] // blk + j, 0)
    base_at = at if base.shape[0] != rows else flat
    source_at = at if source.shape[0] != rows else flat
    whole = spec((blk, cols), flat)
    return stage(
        line, "norm_back", body, (n,), start,
        [
            (kept, whole), (got, whole), (source, spec((blk, cols), source_at)), (base, spec((blk, cols), base_at)),
            (gain.reshape(1, cols), spec((1, cols), lambda j, s: (0, 0))),
        ],
        [
            (jax.ShapeDtypeStruct((rows, cols), jnp.float32), whole),
            (jax.ShapeDtypeStruct((rows, cols), jnp.bfloat16), whole),
            (jax.ShapeDtypeStruct((8, cols), jnp.float32), spec((8, cols), lambda j, s: (0, 0))),
        ],
    )


def add_own(line, kept, got, source):
    rows, cols = kept.shape
    blk = min(rows, 128)
    flat = lambda j, s: (j, 0)

    def body(s, k, g, x, out):
        total = k[...].astype(jnp.float32) + g[...].astype(jnp.float32)
        out[...] = (x[...] + total).astype(jnp.bfloat16)

    whole = spec((blk, cols), flat)
    return stage(
        line, "add_own", body, (rows // blk,), 0,
        [(kept, whole), (got, whole), (source, whole)],
        [(jax.ShapeDtypeStruct((rows, cols), jnp.bfloat16), whole)],
    )


def fixed(x):
    return (x, spec(x.shape, lambda *a: (0, 0)))


def row(x):
    return x.reshape(1, x.shape[0])


def norm_qkv(line, tokens, gain, shift, weights):
    rows, features = tokens.shape
    blk = min(rows, 256)
    flat = lambda j, u: (j, 0)
    outs = [sent(rows, features)]
    outs += [jax.ShapeDtypeStruct((rows, w.shape[1]), jnp.bfloat16) for w in weights]

    def body(u, token_ref, gain_ref, shift_ref, *refs):
        count = len(weights)
        for part in range(2):
            at = slice(part * blk // 2, (part + 1) * blk // 2)
            normed = norm_parts(token_ref[at, :].astype(jnp.float32), gain_ref[...], shift_ref[...])[2].astype(jnp.bfloat16)
            refs[count][at, :] = normed
            for w, out in zip(refs[:count], refs[count + 1 :]):
                out[at, :] = dotf(normed, w[...]).astype(jnp.bfloat16)

    return stage(
        line, "norm_qkv", body, (rows // blk,), 0,
        [(tokens, spec((blk, features), flat)), fixed(far(row(gain))), fixed(far(row(shift)))] + [fixed(w) for w in weights],
        [(out, spec((blk, out.shape[1]), flat)) for out in outs],
    )


def project_out(line, start, own, parts, weights, tokens, gain, shift):
    rows, features = tokens.shape
    blk = min(rows, 256)
    flat = lambda j, u: (j, 0)
    pieces = [x for part in parts for x in part]
    depth = sum(w.shape[0] for w in weights)
    ins = [(tokens, spec((blk, features), flat)), fixed(far(row(gain))), fixed(far(row(shift)))]
    ins += [fixed(w) for w in weights]
    ins += [(x, spec((blk, x.shape[1]), flat)) for x in pieces]

    def body(u, *refs):
        token_ref, gain_ref, shift_ref = refs[:3]
        total_ref, normed_ref, weight = refs[-3:]
        at = 3 + len(weights)

        @pl.when(pl.program_id(0) == 0)
        def _():
            top = 0
            for ref in refs[3:at]:
                weight[top : top + ref.shape[0], :] = ref[...]
                top += ref.shape[0]

        for part in range(2):
            here = slice(part * blk // 2, (part + 1) * blk // 2)
            left = jnp.concatenate([r[here, :] for r in refs[at : at + len(pieces)]], axis=1)
            total = token_ref[here, :].astype(jnp.float32) + dotf(left, weight[...])
            first = pl.program_id(0) * blk + part * (blk // 2) - u[0]

            @pl.when(jnp.logical_and(first >= 0, first < own))
            def _():
                total_ref[pl.ds(pl.multiple_of(first, 16), blk // 2), :] = total

            normed_ref[here, :] = norm_parts(total, gain_ref[...], shift_ref[...])[2].astype(jnp.bfloat16)

    whole = spec((blk, features), flat)
    return stage(
        line, "project_out", body, (rows // blk,), start, ins,
        [
            (jax.ShapeDtypeStruct((own, features), jnp.float32), spec((own, features), lambda j, u: (0, 0))),
            (jax.ShapeDtypeStruct((rows, features), jnp.bfloat16), whole),
        ],
        scratch=[pltpu.VMEM((depth, features), jnp.bfloat16)],
    )


def turn_rows(rows, blk, turn):
    n = rows // 2 // blk
    if turn:
        return lambda j, u: (u[0] * n + j, 0)
    return lambda j, u: ((1 - u[0]) * n + j, 0)


def feed_forward(line, upper, turn, normed, cotangent, up, down, count):
    rows, features = normed.shape
    hidden = up.shape[1]
    blk = min(rows // 2, 256)
    at = turn_rows(rows, blk, turn)
    flat = lambda j, u: (j, 0)

    def body(u, normed_ref, cot_ref, up_ref, down_ref, active_ref, inner_ref, *back_refs):
        for part in range(2):
            here = slice(part * blk // 2, (part + 1) * blk // 2)
            gelu, slope = gelu_pair(dotf(normed_ref[here, :], up_ref[...]))
            active_ref[here, :] = gelu.astype(jnp.bfloat16)
            grad = (dotf(cot_ref[here, :], down_ref[...], NT) * slope).astype(jnp.bfloat16)
            inner_ref[here, :] = grad
            put([r.at[here, :] for r in back_refs], dotf(grad, up_ref[...], NT))

    outs = pieces_of(rows // 2, 2 * hidden, 2) + pieces_of(rows // 2, features, count)
    return stage(
        line, "feed_forward", body, (rows // 2 // blk,), upper,
        columns([normed, cotangent], blk, at) + [fixed(up), fixed(down)],
        [(out, spec((blk, out.shape[1]), flat)) for out in outs],
    )


def product(line, left, right, count):
    rows = left.shape[0]
    blk = min(rows, 256)
    flat = lambda j, u: (j, 0)

    def body(u, l, r, *outs):
        put(outs, dotf(l[...], r[...]))

    made = stage(
        line, "product", body, (rows // blk,), 0,
        columns([left], blk, flat) + [fixed(right)],
        [(x, spec((blk, x.shape[1]), flat)) for x in pieces_of(rows, right.shape[1], count)],
    )
    return made if count > 1 else [made]


def product_back(line, upper, turn, lefts, rights, pieces):
    rows = lefts[0][0].shape[0]
    features, width = rights[0].shape
    blk = min(rows // 2, 256)
    at = turn_rows(rows, blk, turn)
    flat = [x for left in lefts for x in left]

    def body(u, *refs):
        weight = refs[-1]

        @pl.when(pl.program_id(0) == 0)
        def _():
            for i, r in enumerate(refs[len(flat) : len(flat) + len(rights)]):
                weight[:, i * width : (i + 1) * width] = r[...]

        put(refs[len(flat) + len(rights) : -1], dotf(cat(refs[: len(flat)]), weight[...], NT))

    made = stage(
        line, "product_back", body, (rows // 2 // blk,), upper,
        columns(flat, blk, at) + [fixed(r) for r in rights],
        [(x, spec((blk, x.shape[1]), lambda j, u: (j, 0))) for x in pieces_of(rows // 2, features, pieces)],
        scratch=[pltpu.VMEM((features, len(rights) * width), jnp.bfloat16)],
    )
    return made if pieces > 1 else [made]


def hold_small(line, mine):
    def body(u, m, out):
        out[...] = m[...]

    return stage(line, "add_small", body, (1,), 0, [fixed(mine)], [(jax.ShapeDtypeStruct(mine.shape, mine.dtype), fixed(mine)[1])])


def add_small(line, mine, got):
    def body(u, m, g, out):
        out[...] = m[...] + g[...]

    return stage(line, "add_small", body, (1,), 0, [fixed(mine), fixed(got)], [(jax.ShapeDtypeStruct(mine.shape, mine.dtype), fixed(mine)[1])])


def shards(
    n_dp,
    n_tp,
    tokens,
    query_weight,
    key_weight,
    value_weight,
    out_weight,
    up_weight,
    down_weight,
    bias_table,
    gain_one,
    shift_one,
    gain_two,
    shift_two,
    single_item,
    cotangent,
):
    tp_bits = index_bits(n_tp)
    dp_bits = index_bits(n_dp)
    far_first = tp_bits[1:] + tp_bits[:1]
    low = jnp.bfloat16
    full = jnp.float32
    row_count, features = tokens.shape
    head_count = bias_table.shape[1]
    width = head_count * HD
    tp_up = [rank_bit("tp", bit) for bit in tp_bits]
    dp_up = [rank_bit("dp", bit) for bit in dp_bits]
    start, own_count = own_start("tp", tp_bits, row_count)

    def tp_swap(values, i):
        return swap(values, "tp", n_tp, tp_bits[i])

    def dp_swap(values, i):
        return swap(values, "dp", n_dp, dp_bits[i])

    line = []

    class Sum:
        def __init__(self, axis, send, keep):
            self.axis = axis
            self.up = tp_up if axis == "tp" else dp_up
            self.keep, self.at = keep, 0
            self.swap(send)

        def swap(self, arrays):
            self.got = [keep_far((tp_swap if self.axis == "tp" else dp_swap)(x, self.at)) for x in arrays]

        def count(self, at):
            return PIECES if self.axis == "tp" and at == 0 else 1

        def halve(self):
            self.at += 1
            if self.axis == "dp" and self.at == len(self.up) - 1:
                self.keep = [add_up(line, self.keep[0], self.got[0])]
                self.swap(self.keep)
            else:
                send, self.keep = split_add(line, self.up[self.at], self.keep, self.got, self.count(self.at))
                self.swap(send)

        def spread(self, values):
            self.keep = values
            self.swap(values)

        def total(self):
            pass

        def fan(self):
            mine = [add_up(line, self.keep[0], self.got[0])]
            self.at -= 1
            while self.at > 1:
                self.spread(mine)
                mine = [join_rows(line, self.up[self.at], self.keep, self.got, low)[0]]
                self.at -= 1
            self.mine = mine[0]
            self.near = dp_swap(self.mine, 1)
            self.far = [dp_swap(self.mine, 0), dp_swap(self.near, 0)]

        def finish(self, outs):
            return join_four(line, self.up[:2], [self.mine, self.near] + self.far, outs)

        def double(self, dtype=low):
            count = self.count(self.at - 1) if self.at else 1
            joined = join_rows(line, self.up[self.at], self.keep, self.got, dtype, count)
            if self.at == 0:
                return joined[0]
            self.at -= 1
            self.spread(joined)

    out_parts = gather_parts(out_weight, "tp", n_tp, far_first)
    near_rows = near_bias(bias_table)
    normed_low, queries, key_rows, value_rows = norm_qkv(
        line, far(tokens), gain_one, shift_one, [far(w) for w in (query_weight, key_weight, value_weight)]
    )
    pairs = width // (2 * HD)
    attended, lse_rows, parts = [], [], []
    for pair in range(pairs):
        also = [out_parts[far_first[0]][:8, :128]] if pair == pairs - 1 else ()
        columns, sums = attn_forward(
            line, pair, single_item, near_rows, queries, key_rows, value_rows, also
        )
        attended.append(columns)
        lse_rows.append(sums)
        parts.append(gather_parts(columns, "tp", n_tp, far_first))
    parts = [[far(parts[pair][k]) if k else parts[pair][k] for pair in range(pairs)] for k in range(n_tp)]
    out_parts = [far(w) for w in out_parts]
    residual, normed_two_low = project_out(
        line, start, own_count, parts, out_parts, far(tokens), gain_two, shift_two
    )
    fed = [
        feed_forward(line, tp_up[0], turn, normed_two_low, cotangent, up_weight, down_weight, PIECES)
        for turn in (0, 1)
    ]
    two = Sum("tp", fed[0][2:], fed[1][2:])
    ups = [dp_up[0], tp_up[0]]
    down_group = [[(fed[turn][0], turn, [cotangent], turn) for turn in (0, 1)]]
    up_group = [[(normed_two_low, turn, [fed[turn][1]], turn) for turn in (0, 1)]]

    def halve_to_last(total, done):
        for _ in range(len(total.up) - 1 - done):
            total.halve()

    halve_to_last(two, 0)
    down_send = weight_grad(line, ups, True, down_group)
    down_keep = weight_grad(line, ups, False, down_group)
    down = Sum("dp", [down_send], [down_keep])
    ffn = Sum("tp", *[product(line, fed[turn][0], down_weight, PIECES) for turn in (0, 1)])
    up_keep = weight_grad(line, ups, False, up_group)
    grad_residual, grad_residual_low, sums_two = norm_back_own(
        line, two.keep[0], two.got[0], residual, cotangent, gain_two, start
    )
    two.spread([grad_residual_low])
    down.halve()
    up_send = weight_grad(line, ups, True, up_group)
    up = Sum("dp", [up_send], [up_keep])
    for _ in tp_bits[1:]:
        two.double()
    halve_to_last(ffn, 0)
    grad_residual_low = two.double()
    grad_query, grad_key, grad_value, near_totals = attn_backward(
        line, single_item, near_rows, queries, key_rows, value_rows, attended, lse_rows,
        grad_residual_low, out_weight,
    )
    grad_table = table_grad(near_totals, head_count)
    heads_back = [[grad_query], [grad_key], [grad_value]]
    head_weights = [query_weight, key_weight, value_weight]
    mixed_group = [
        [(normed_low, None, heads_back[2], None)],
        [(grad_residual_low, None, attended, None)],
    ]
    heads_group = [[(normed_low, None, heads_back[0] + heads_back[1], None)]]
    halve_to_last(down, 1)
    one = Sum("tp", *[product_back(line, tp_up[0], turn, heads_back, head_weights, PIECES) for turn in (0, 1)])
    mixed_send = weight_grad(line, ups, True, mixed_group)
    halve_to_last(one, 0)
    up.halve()
    mixed = Sum("dp", [mixed_send], [weight_grad(line, ups, False, mixed_group)])
    heads_send = weight_grad(line, ups, True, heads_group)
    heads = Sum("dp", [heads_send], [weight_grad(line, ups, False, heads_group)])
    _, grad_tokens, sums_one = norm_back_own(
        line, one.keep[0], one.got[0], tokens, grad_residual, gain_one, start
    )
    one.spread([grad_tokens])
    table_size = NB * head_count
    slot = jnp.zeros((n_tp * table_size,), full)
    me_tp = lax.axis_index("tp")
    slot = lax.dynamic_update_slice(slot, grad_table.reshape(table_size), (me_tp * table_size,))
    slot = jnp.pad(slot, (0, -slot.size % features)).reshape(-1, features)
    small = [jnp.concatenate([sums_one[:2], sums_two[:2], slot])]
    steps = [("tp", n_tp, bit) for bit in tp_bits] + [("dp", n_dp, bit) for bit in dp_bits]
    small_line = []

    def small_step(use):
        if steps:
            axis, count, bit = steps.pop(0)
            small[0] = add_small(use, small[0], swap(small[0], axis, count, bit))

    mixed.halve()
    halve_to_last(up, 1)
    down.fan()
    heads.halve()
    halve_to_last(mixed, 1)
    for _ in tp_bits[1:]:
        one.double()
    up.fan()
    halve_to_last(heads, 1)
    ffn.spread([add_own(line, ffn.keep[0], ffn.got[0], residual)])
    grad_tokens = one.double(full)
    grad_down = down.finish([(0, features, False)])
    mixed.fan()
    for _ in tp_bits[1:]:
        ffn.double()
    grad_up = up.finish([(0, up_weight.shape[1], False)])
    heads.fan()
    result = ffn.double()
    small[0] = hold_small(line, small[0])
    steps = steps[: len(tp_bits)] + steps[len(tp_bits) + 1 :] + steps[len(tp_bits) : len(tp_bits) + 1]
    while steps:
        small_step(small_line)
    grad_vw, grad_out = mixed.finish([(0, width, False), (width, width, True)])
    grad_qw, grad_kw = heads.finish([(0, width, False), (width, width, False)])
    down.total()
    up.total()
    mixed.total()
    heads.total()
    small = small[0]
    grad_table = lax.dynamic_slice(
        small[4:].reshape(-1), (me_tp * table_size,), (table_size,)
    ).reshape(NB, head_count)
    return (
        result,
        grad_tokens,
        grad_qw,
        grad_kw,
        grad_vw,
        grad_out,
        grad_up,
        grad_down,
        grad_table,
        small[0],
        small[1],
        small[2],
        small[3],
    )


def solution(mesh):
    placed = (
        P("dp", None),
        P(None, "tp"),
        P(None, "tp"),
        P(None, "tp"),
        P("tp", None),
        P(None, "tp"),
        P("tp", None),
        P(None, "tp"),
        P(),
        P(),
        P(),
        P(),
        P("dp"),
        P("dp", None),
    )
    return jax.shard_map(
        functools.partial(shards, mesh.shape["dp"], mesh.shape["tp"]),
        mesh=mesh,
        in_specs=placed,
        out_specs=(
            P("dp", None),
            P("dp", None),
            P(None, "tp"),
            P(None, "tp"),
            P(None, "tp"),
            P("tp", None),
            P(None, "tp"),
            P("tp", None),
            P(None, "tp"),
            P(),
            P(),
            P(),
            P(),
        ),
        check_vma=False,
    )
```

```python
import functools
import math

import jax
import jax.numpy as jnp
from jax import lax
from jax.experimental import pallas as pl
from jax.experimental.pallas import tpu as pltpu
from jax.sharding import PartitionSpec as P

HD = 64
NB = 32
MAXDIST = 128


epsilon = 1e-05
FRONT = {"norm_qkv": 3.5, "attn_forward": 4.5, "project_out": 6.0, "feed_forward": 7.0}
REST = {"split_add": 1.5, "join_rows": 2.0, "weight_grad": 3.0, "norm_back": 2.0, "product": 1.5, "product_back": 1.5, "attn_backward": 14.0, "add_own": 1.3, "add_up": 1.0, "join_four": 4.0, "add_small": 0.5}


def cost_of(name):
    us = FRONT[name] * 1.0 if name in FRONT else REST[name] * 0.3
    return pl.CostEstimate(flops=max(1, int(us * 1.15e9)), bytes_accessed=1, transcendentals=0)

VMEM_LIMIT = 32 * 1024 * 1024
PIECES = 2


def thresholds_list():
    exact_count = NB // 2
    thresholds = []
    for bucket in range(1, NB):
        if bucket <= exact_count:
            thresholds.append(bucket)
        else:
            thresholds.append(
                int(
                    math.ceil(
                        exact_count
                        * (MAXDIST / exact_count) ** ((bucket - exact_count) / exact_count)
                    )
                )
            )
    return thresholds


def distance_onehot(count):
    distance = jnp.arange(count, dtype=jnp.int32)
    buckets = jnp.zeros((count,), jnp.int32)
    for threshold in thresholds_list():
        buckets = buckets + (distance >= threshold).astype(jnp.int32)
    return (buckets[:, None] == jnp.arange(NB, dtype=jnp.int32)[None, :]).astype(jnp.float32)


def norm_parts(values, gain, shift):
    center = values - jnp.mean(values, axis=-1, keepdims=True)
    scaled = lax.rsqrt(jnp.mean(center * center, axis=-1, keepdims=True) + epsilon)
    normal = center * scaled
    return (normal, scaled, normal * gain + shift)


def norm_back(grad_out, normal, scaled, gain):
    grad_norm = grad_out * gain
    inner_mean = jnp.mean(grad_norm * normal, axis=-1, keepdims=True)
    return scaled * (grad_norm - jnp.mean(grad_norm, axis=-1, keepdims=True) - normal * inner_mean)


def gelu_pair(values):
    bell = jnp.exp(-0.5 * values * values)
    t = 1.0 / (1.0 + (0.3275911 * math.sqrt(0.5)) * jnp.abs(values))
    poly = 0.5 * 1.061405429
    for factor in (-1.453152027, 1.421413741, -0.284496736, 0.254829592):
        poly = poly * t + 0.5 * factor
    tail = poly * t * bell
    cdf = jnp.where(values < 0.0, tail, 1.0 - tail)
    return values * cdf, cdf + values * bell * (1.0 / math.sqrt(2.0 * math.pi))


BLK = 256
NEAR = 128
NEG = -1000000000.0
NT = (((1,), (1,)), ((), ()))
TN = (((0,), (0,)), ((), ()))


def dotf(a, b, dims=(((1,), (0,)), ((), ()))):
    return lax.dot_general(a, b, dims, preferred_element_type=jnp.float32)


def fill_bias(g_ref, bias_ref):
    row = lax.broadcasted_iota(jnp.int32, (2 * NEAR, NEAR), 0)
    col = lax.broadcasted_iota(jnp.int32, (2 * NEAR, NEAR), 1)
    hidden = row - NEAR > col
    for h in range(2):
        spread = jnp.broadcast_to(g_ref[h : h + 1, :], (2 * NEAR, 2 * NEAR))
        tile = pltpu.roll(spread, 0, 1, stride=1, stride_axis=0)[:, :NEAR]
        tile = jnp.where(hidden, NEG, tile)
        bias_ref[h, : 2 * NEAR, :NEAR] = tile
        bias_ref[h, 2 * NEAR :, :NEAR] = jnp.full((NEAR, NEAR), NEG, jnp.float32)
        bias_ref[h, :NEAR, NEAR:] = jnp.zeros((NEAR, NEAR), jnp.float32)
        bias_ref[h, NEAR:, NEAR:] = tile


def head_mask(x, h):
    lane = lax.broadcasted_iota(jnp.int32, x.shape, 1)
    return jnp.where((lane < HD) == (h == 0), x, jnp.zeros_like(x))


def add_near(st, bias_ref, h, low, blk):
    near = max(blk * BLK - NEAR, low)
    top = near - low
    tile = bias_ref[h, near - (blk * BLK - NEAR) :, :]
    if top == 0:
        return st + tile
    return jnp.concatenate([st[:top], st[top:] + tile], axis=0)


def each_block(row_count, single_ref, work):
    half = row_count // 2
    single = single_ref[0] == 1
    for blk in range(row_count // BLK):
        if blk * BLK < half:
            work(blk, 0)
        else:
            pl.when(single)(functools.partial(work, blk, 0))
            pl.when(jnp.logical_not(single))(functools.partial(work, blk, half))


def attn_fwd_kernel(single_ref, g_ref, q_ref, k_ref, v_ref, o_ref, lse_ref, bias_ref, vt_ref):
    row_count = q_ref.shape[0]
    fill_bias(g_ref, bias_ref)
    vt_ref[...] = v_ref[...].T

    def work(blk, low):
        high = (blk + 1) * BLK
        rows = slice(blk * BLK, high)
        q = q_ref[rows, :] * jnp.asarray(HD ** (-0.5), jnp.bfloat16)
        outs = []
        for h in range(2):
            st = dotf(k_ref[low:high, :], head_mask(q, h), NT)
            st = add_near(st, bias_ref, h, low, blk)
            m = jnp.max(st, axis=0, keepdims=True)
            p = jnp.exp(st - m)
            total = jnp.sum(p, axis=0, keepdims=True)
            ot = dotf(vt_ref[h * HD : (h + 1) * HD, low:high], p.astype(jnp.bfloat16))
            outs.append(ot / total)
            lse_ref[h : h + 1, rows] = m + jnp.log(total)
        o_ref[rows, :] = jnp.concatenate(outs, axis=0).T.astype(jnp.bfloat16)

    each_block(row_count, single_ref, work)


def attn_bwd_kernel(
    single_ref, g_ref, q_ref, k_ref, v_ref, o_ref, lse_ref, gr_ref, w_ref,
    dq_ref, dk_ref, dv_ref, near_ref, bias_ref, kt_ref, dk_acc, dv_acc, near_acc,
):
    row_count = q_ref.shape[0]
    fill_bias(g_ref, bias_ref)
    kt_ref[...] = k_ref[...].T
    dk_acc[...] = jnp.zeros_like(dk_acc)
    dv_acc[...] = jnp.zeros_like(dv_acc)
    near_acc[...] = jnp.zeros_like(near_acc)

    def work(blk, low):
        high = (blk + 1) * BLK
        rows = slice(blk * BLK, high)
        q = q_ref[rows, :] * jnp.asarray(HD ** (-0.5), jnp.bfloat16)
        da = dotf(gr_ref[rows, :], w_ref[...], NT).astype(jnp.bfloat16)
        prod_t = (da.astype(jnp.float32) * o_ref[rows, :].astype(jnp.float32)).T
        ps, dss, qms, dams, dqts = [], [], [], [], []
        for h in range(2):
            qm, dam = head_mask(q, h), head_mask(da, h)
            st = dotf(k_ref[low:high, :], qm, NT)
            st = add_near(st, bias_ref, h, low, blk)
            p = jnp.exp(st - lse_ref[h : h + 1, rows])
            dpt = dotf(v_ref[low:high, :], dam, NT)
            dd = jnp.sum(prod_t[h * HD : (h + 1) * HD], axis=0, keepdims=True)
            ds = p * (dpt - dd)
            own = blk * BLK - low
            if own:
                near_acc[h] += ds[own - NEAR : own + NEAR, :NEAR]
            else:
                near_acc[h, NEAR:] += ds[:NEAR, :NEAR]
            near_acc[h] += ds[own : own + 2 * NEAR, NEAR:]
            dsb = ds.astype(jnp.bfloat16)
            ps.append(p.astype(jnp.bfloat16))
            dss.append(dsb)
            qms.append(qm)
            dams.append(dam)
            dqts.append(dotf(kt_ref[h * HD : (h + 1) * HD, low:high], dsb))
        dv_acc[low:high] += dotf(jnp.concatenate(ps, axis=1), jnp.concatenate(dams, axis=0))
        dk_acc[low:high] += dotf(jnp.concatenate(dss, axis=1), jnp.concatenate(qms, axis=0))
        dq = jnp.concatenate(dqts, axis=0).T * HD ** (-0.5)
        dq_ref[rows, :] = dq.astype(jnp.bfloat16)

    each_block(row_count, single_ref, work)
    dk_ref[...] = dk_acc[...].astype(jnp.bfloat16)
    dv_ref[...] = dv_acc[...].astype(jnp.bfloat16)
    near_ref[...] = jnp.zeros_like(near_ref)
    for h in range(2):
        acc = jnp.concatenate([near_acc[h], jnp.zeros((2 * NEAR, NEAR), jnp.float32)], axis=1)
        row = lax.broadcasted_iota(jnp.int32, acc.shape, 0)
        for bit in range((2 * NEAR - 1).bit_length()):
            moved = pltpu.roll(acc, 2 * NEAR - (1 << bit), 1)
            acc = jnp.where((row & (1 << bit)) != 0, moved, acc)
        near_ref[h : h + 1, :] = jnp.sum(acc, axis=0, keepdims=True)


def pair_specs(row_count, first):
    smem = pl.BlockSpec(memory_space=pltpu.SMEM)
    cols = pl.BlockSpec((row_count, 2 * HD), lambda p: (0, first + p))
    near = pl.BlockSpec((None, 8, 2 * NEAR), lambda p: (first + p, 0, 0))
    lse = pl.BlockSpec((None, 8, row_count), lambda p: (first + p, 0, 0))
    return smem, cols, near, lse


def held(arrays):
    return [pl.BlockSpec(memory_space=pl.ANY)] * len(arrays)


def attn_forward(line, pair, single_item, g, q, k, v, also=()):
    row_count = q.shape[0]
    after = line + list(also)
    smem, cols, near, _ = pair_specs(row_count, pair)
    own = pl.BlockSpec((row_count, 2 * HD), lambda p: (0, 0))
    lse = pl.BlockSpec((8, row_count), lambda p: (0, 0))

    def kernel(*refs):
        attn_fwd_kernel(*refs[:5], *refs[5 + len(after) :])

    attended, lse_rows = pl.pallas_call(
        kernel,
        grid=(1,),
        in_specs=[smem, near, cols, cols, cols] + held(after),
        out_specs=[own, lse],
        out_shape=[
            jax.ShapeDtypeStruct((row_count, 2 * HD), jnp.bfloat16),
            jax.ShapeDtypeStruct((8, row_count), jnp.float32),
        ],
        scratch_shapes=[
            pltpu.VMEM((2, 3 * NEAR, BLK), jnp.float32),
            pltpu.VMEM((2 * HD, row_count), jnp.bfloat16),
        ],
        compiler_params=pltpu.CompilerParams(vmem_limit_bytes=VMEM_LIMIT),
        cost_estimate=cost_of("attn_forward"),
        name="attn_forward",
    )(single_item, g, q, k, v, *after)
    line[:] = [lse_rows]
    return attended, lse_rows


def attn_backward(line, single_item, g, q, k, v, o, lse_rows, grad, out_weight):
    row_count, width = q.shape
    pairs = len(o)
    after = list(line)
    smem = pl.BlockSpec(memory_space=pltpu.SMEM)
    cols = pl.BlockSpec((row_count, 2 * HD), lambda p: (0, p))
    near = pl.BlockSpec((None, 8, 2 * NEAR), lambda p: (p, 0, 0))
    flat = jax.ShapeDtypeStruct((row_count, width), jnp.bfloat16)

    def whole(x):
        return pl.BlockSpec(x.shape, lambda p: (0, 0))

    def kernel(*refs):
        o_refs, lse_refs = refs[5 : 5 + pairs], refs[5 + pairs : 5 + 2 * pairs]
        rest = refs[5 + 2 * pairs :]
        o_ref, lse_ref = rest[-2:]
        for p in range(pairs):

            @pl.when(pl.program_id(0) == p)
            def _():
                o_ref[...] = o_refs[p][...]
                lse_ref[...] = lse_refs[p][...]

        attn_bwd_kernel(*refs[:5], o_ref, lse_ref, *rest[:2], *rest[2 + len(after) : -2])

    *grads, near_totals = pl.pallas_call(
        kernel,
        grid=(pairs,),
        in_specs=[smem, near, cols, cols, cols]
        + [whole(x) for x in o]
        + [whole(x) for x in lse_rows]
        + [whole(grad), pl.BlockSpec((2 * HD, grad.shape[1]), lambda p: (p, 0))]
        + held(after),
        out_specs=[cols, cols, cols, near],
        out_shape=[flat, flat, flat, jax.ShapeDtypeStruct((pairs, 8, 2 * NEAR), jnp.float32)],
        scratch_shapes=[
            pltpu.VMEM((2, 3 * NEAR, BLK), jnp.float32),
            pltpu.VMEM((2 * HD, row_count), jnp.bfloat16),
            pltpu.VMEM((row_count, 2 * HD), jnp.float32),
            pltpu.VMEM((row_count, 2 * HD), jnp.float32),
            pltpu.VMEM((2, 2 * NEAR, NEAR), jnp.float32),
            pltpu.VMEM((row_count, 2 * HD), jnp.bfloat16),
            pltpu.VMEM((8, row_count), jnp.float32),
        ],
        compiler_params=pltpu.CompilerParams(vmem_limit_bytes=VMEM_LIMIT),
        cost_estimate=cost_of("attn_backward"),
        name="attn_backward",
    )(single_item, g, q, k, v, *o, *lse_rows, grad, out_weight, *after)
    line[:] = [near_totals]
    return *grads, near_totals


def near_bias(bias_table):
    head_count = bias_table.shape[1]
    rows = jnp.dot(
        distance_onehot(NEAR), bias_table - bias_table[NB - 1 :],
        precision=lax.Precision.HIGHEST, preferred_element_type=jnp.float32,
    ).T
    rows = jnp.pad(rows, ((0, 0), (NEAR, 0))).reshape(head_count // 2, 2, 2 * NEAR)
    return jnp.pad(rows, ((0, 0), (0, 6), (0, 0)))


def table_grad(near, head_count):
    by_dist = near[:, :2, NEAR:].reshape(head_count, NEAR)
    grad = jnp.dot(
        by_dist, distance_onehot(NEAR)[:, : NB - 1],
        precision=lax.Precision.HIGHEST, preferred_element_type=jnp.float32,
    )
    return jnp.concatenate([grad, -jnp.sum(grad, axis=1, keepdims=True)], axis=1).T


def index_bits(count):
    return [1 << i for i in range(count.bit_length() - 1)]


def sent(rows, cols):
    return pltpu.HBM((rows, cols), jnp.bfloat16)


def far(x):
    return pltpu.with_memory_space_constraint(x, pltpu.HBM)


def keep_far(x):
    return x


def swap(values, axis, count, bit):
    return lax.ppermute(values, axis, [(i, i ^ bit) for i in range(count)])


def rank_bit(axis, bit):
    return (lax.axis_index(axis) // bit) % 2


def gather_parts(values, axis, count, bits):
    parts = {0: values}
    for bit in bits:
        for k in list(parts):
            parts[k ^ bit] = swap(parts[k], axis, count, bit)
    return [parts[k] for k in range(count)]


def own_start(axis, bits, size):
    start = 0
    for bit in bits:
        size //= 2
        start = start + rank_bit(axis, bit) * size
    return start, size


def sum_over(values, axis, count, bits):
    for bit in bits:
        values = values + swap(values, axis, count, bit)
    return values


def spec(shape, index):
    return pl.BlockSpec(shape, index)


def scalars(values):
    values = values if isinstance(values, list) else [values]
    return jnp.stack([jnp.asarray(v, jnp.int32) for v in values])


def stage(line, name, body, grid, upper, ins, outs, scratch=(), also=()):
    after = line + list(also)
    shapes = [shape for shape, _ in outs] + [jax.ShapeDtypeStruct((8, 128), jnp.float32)]
    token = pl.BlockSpec((8, 128), lambda *a: (0, 0))
    held = pl.BlockSpec(memory_space=pl.ANY)

    def kernel(upper_ref, *refs):
        used = refs[: len(ins)]
        rest = refs[len(ins) + len(after) :]
        body(upper_ref, *used, *rest[: len(outs)], *rest[len(outs) + 1 :])
        rest[len(outs)][...] = jnp.zeros((8, 128), jnp.float32)

    *results, mark = pl.pallas_call(
        kernel,
        grid_spec=pltpu.PrefetchScalarGridSpec(
            num_scalar_prefetch=1,
            grid=grid,
            in_specs=[where for _, where in ins] + [held] * len(after),
            out_specs=[where for _, where in outs] + [token],
            scratch_shapes=list(scratch),
        ),
        out_shape=shapes,
        compiler_params=pltpu.CompilerParams(vmem_limit_bytes=VMEM_LIMIT),
        cost_estimate=cost_of(name),
        name=name,
    )(scalars(upper), *[x for x, _ in ins], *after)
    line[:] = [mark]
    return results if len(results) > 1 else results[0]


def cat(refs):
    return refs[0][...] if len(refs) == 1 else jnp.concatenate([r[...] for r in refs], axis=1)


def put(refs, values):
    at = 0
    for ref in refs:
        size = ref.shape[1]
        ref[...] = values[:, at : at + size].astype(ref.dtype)
        at += size


def columns(arrays, blk, index):
    return [(x, spec((blk, x.shape[1]), index)) for x in arrays]


def pieces_of(rows, cols, count, dtype=jnp.bfloat16):
    return [jax.ShapeDtypeStruct((rows, cols // count), dtype)] * count


def split_add(line, upper, kept, got, count=1):
    rows, cols = got[0].shape[0], sum(x.shape[1] for x in got)
    half = rows // 2
    blk = min(half, 128)
    n = half // blk
    a, b = len(kept), len(got)

    def body(u, *refs):
        for at, outs in ((0, refs[2 * a + 2 * b : -1]), (a + b, refs[-1:])):
            total = cat(refs[at : at + a]).astype(jnp.float32)
            put(outs, total + cat(refs[at + a : at + a + b]).astype(jnp.float32))

    away = lambda j, u: ((1 - u[0]) * n + j, 0)
    here = lambda j, u: (u[0] * n + j, 0)
    outs = pieces_of(half, cols, count) + pieces_of(half, cols, 1)
    *send, keep = stage(
        line, "split_add", body, (n,), upper,
        columns(kept + got, blk, away) + columns(kept + got, blk, here),
        [(x, spec((blk, x.shape[1]), lambda j, u: (j, 0))) for x in outs],
    )
    return send, [keep]


def add_up(line, kept, got):
    rows, cols = kept.shape
    blk = min(rows, 128)
    flat = lambda j, u: (j, 0)

    def body(u, k, g, out):
        out[...] = (k[...].astype(jnp.float32) + g[...].astype(jnp.float32)).astype(out.dtype)

    where = spec((blk, cols), flat)
    return stage(
        line, "add_up", body, (rows // blk,), 0, [(kept, where), (got, where)],
        [(jax.ShapeDtypeStruct(kept.shape, jnp.bfloat16), where)],
    )


def join_rows(line, upper, mine, got, dtype, count=1):
    rows, cols = mine[0].shape[0], sum(x.shape[1] for x in mine)
    blk = min(rows, 256)
    n = rows // blk
    a = len(mine)

    def body(u, *refs):
        i = pl.program_id(0)

        @pl.when(i == 0)
        def _():
            put(refs[2 * a :], cat(refs[:a]))

        @pl.when(i == 1)
        def _():
            put(refs[2 * a :], cat(refs[a : 2 * a]))

    joined = stage(
        line, "join_rows", body, (2, n), upper,
        columns(mine, blk, lambda i, j, u: (jnp.where(i == 0, j, n - 1), 0))
        + columns(got, blk, lambda i, j, u: (jnp.where(i == 0, 0, j), 0)),
        [
            (x, spec((blk, x.shape[1]), lambda i, j, u: (jnp.where(i == 0, u[0], 1 - u[0]) * n + j, 0)))
            for x in pieces_of(2 * rows, cols, count, dtype)
        ],
    )
    return joined if count > 1 else [joined]


def join_four(line, uppers, pieces, outs):
    rows, cols = pieces[0].shape
    blk = min(rows, 256)
    n = rows // blk

    def body(u, *refs):
        for p in range(4):

            @pl.when(pl.program_id(0) == p)
            def _():
                for out, (first, size, turned) in zip(refs[4:], outs):
                    x = refs[p][:, first : first + size].astype(jnp.float32)
                    out[...] = x.T if turned else x

    def place(i, j, u):
        high = jnp.where(i < 2, u[0], 1 - u[0])
        return (high * 2 + jnp.where(i % 2 == 0, u[1], 1 - u[1])) * n + j

    def turn(p):
        return lambda i, j, u: (jnp.where(i == p, j, jnp.where(i < p, 0, n - 1)), 0)

    results = []
    for _, size, turned in outs:
        if turned:
            results.append((jax.ShapeDtypeStruct((size, 4 * rows), jnp.float32), spec((size, blk), lambda i, j, u: (0, place(i, j, u)))))
        else:
            results.append((jax.ShapeDtypeStruct((4 * rows, size), jnp.float32), spec((blk, size), lambda i, j, u: (place(i, j, u), 0))))
    return stage(
        line, "join_four", body, (4, n), uppers,
        [(x, spec((blk, cols), turn(p))) for p, x in enumerate(pieces)], results,
    )


def weight_grad(line, upper, away, groups):
    left = groups[0][0][0]
    half = left.shape[1] // 2
    blk = min(half, 256)
    n = half // blk

    def row_spec(x, rows, cols, column, turn):
        if turn is None:
            return (x, spec((x.shape[0], cols), lambda j, u: (0, column(j, u))))
        pick = (lambda u: u[1]) if turn else (lambda u: 1 - u[1])
        if x.shape[0] == rows:
            pick = lambda u: 0
        return (x, spec((rows, cols), lambda j, u: (pick(u), column(j, u))))

    if away:
        block = lambda j, u: (1 - u[0]) * n + j
    else:
        block = lambda j, u: u[0] * n + j
    ins, plan = [], []
    for group in groups:
        terms = []
        for left, turn, rights, right_turn in group:
            rows = left.shape[0] if turn is None and right_turn is None else min(left.shape[0], rights[0].shape[0])
            if rows == left.shape[0] == rights[0].shape[0] and turn is not None:
                rows = left.shape[0] // 2
            terms.append((len(ins), len(rights)))
            ins.append(row_spec(left, rows, blk, block, turn))
            ins.extend(row_spec(r, rows, r.shape[1], lambda j, u: 0, right_turn) for r in rights)
        plan.append(terms)
    width = sum(r.shape[1] for group in groups for r in group[0][2])

    def body(u, *refs):
        out, col = refs[-1], 0
        for terms in plan:
            lefts = [refs[at][...] for at, _ in terms]
            for i in range(terms[0][1]):
                total = 0.0
                for (at, _), left_rows in zip(terms, lefts):
                    total = total + dotf(left_rows, refs[at + 1 + i][...], TN)
                out[:, col : col + total.shape[1]] = total.astype(jnp.bfloat16)
                col += total.shape[1]

    return stage(
        line, "weight_grad", body, (n,), upper, ins,
        [(jax.ShapeDtypeStruct((half, width), jnp.bfloat16), spec((blk, width), lambda j, u: (j, 0)))],
    )


def norm_back_own(line, kept, got, source, base, gain, start):
    rows, cols = kept.shape
    blk = min(rows, 128)
    n = rows // blk

    def body(s, k, g, x, b, gain_ref, out, low, sums):
        grad = k[...].astype(jnp.float32) + g[...].astype(jnp.float32)
        center = x[...].astype(jnp.float32)
        center = center - jnp.mean(center, axis=1, keepdims=True)
        scaled = lax.rsqrt(jnp.mean(center * center, axis=1, keepdims=True) + epsilon)
        normal = center * scaled
        moved = b[...].astype(jnp.float32) + norm_back(grad, normal, scaled, gain_ref[...])
        out[...] = moved
        low[...] = moved.astype(jnp.bfloat16)

        @pl.when(pl.program_id(0) == 0)
        def _():
            sums[...] = jnp.zeros_like(sums)

        sums[0:1, :] += jnp.sum(grad * normal, axis=0, keepdims=True)
        sums[1:2, :] += jnp.sum(grad, axis=0, keepdims=True)

    flat = lambda j, s: (j, 0)
    at = lambda j, s: (s[0] // blk + j, 0)
    base_at = at if base.shape[0] != rows else flat
    source_at = at if source.shape[0] != rows else flat
    whole = spec((blk, cols), flat)
    return stage(
        line, "norm_back", body, (n,), start,
        [
            (kept, whole), (got, whole), (source, spec((blk, cols), source_at)), (base, spec((blk, cols), base_at)),
            (gain.reshape(1, cols), spec((1, cols), lambda j, s: (0, 0))),
        ],
        [
            (jax.ShapeDtypeStruct((rows, cols), jnp.float32), whole),
            (jax.ShapeDtypeStruct((rows, cols), jnp.bfloat16), whole),
            (jax.ShapeDtypeStruct((8, cols), jnp.float32), spec((8, cols), lambda j, s: (0, 0))),
        ],
    )


def add_own(line, kept, got, source):
    rows, cols = kept.shape
    blk = min(rows, 128)
    flat = lambda j, s: (j, 0)

    def body(s, k, g, x, out):
        total = k[...].astype(jnp.float32) + g[...].astype(jnp.float32)
        out[...] = (x[...] + total).astype(jnp.bfloat16)

    whole = spec((blk, cols), flat)
    return stage(
        line, "add_own", body, (rows // blk,), 0,
        [(kept, whole), (got, whole), (source, whole)],
        [(jax.ShapeDtypeStruct((rows, cols), jnp.bfloat16), whole)],
    )


def fixed(x):
    return (x, spec(x.shape, lambda *a: (0, 0)))


def row(x):
    return x.reshape(1, x.shape[0])


def norm_qkv(line, tokens, gain, shift, weights):
    rows, features = tokens.shape
    blk = min(rows, 256)
    flat = lambda j, u: (j, 0)
    outs = [sent(rows, features)]
    outs += [jax.ShapeDtypeStruct((rows, w.shape[1]), jnp.bfloat16) for w in weights]

    def body(u, token_ref, gain_ref, shift_ref, *refs):
        count = len(weights)
        for part in range(2):
            at = slice(part * blk // 2, (part + 1) * blk // 2)
            normed = norm_parts(token_ref[at, :].astype(jnp.float32), gain_ref[...], shift_ref[...])[2].astype(jnp.bfloat16)
            refs[count][at, :] = normed
            for w, out in zip(refs[:count], refs[count + 1 :]):
                out[at, :] = dotf(normed, w[...]).astype(jnp.bfloat16)

    return stage(
        line, "norm_qkv", body, (rows // blk,), 0,
        [(tokens, spec((blk, features), flat)), fixed(far(row(gain))), fixed(far(row(shift)))] + [fixed(w) for w in weights],
        [(out, spec((blk, out.shape[1]), flat)) for out in outs],
    )


def project_out(line, start, own, parts, weights, tokens, gain, shift):
    rows, features = tokens.shape
    blk = min(rows, 256)
    flat = lambda j, u: (j, 0)
    pieces = [x for part in parts for x in part]
    depth = sum(w.shape[0] for w in weights)
    ins = [(tokens, spec((blk, features), flat)), fixed(far(row(gain))), fixed(far(row(shift)))]
    ins += [fixed(w) for w in weights]
    ins += [(x, spec((blk, x.shape[1]), flat)) for x in pieces]

    def body(u, *refs):
        token_ref, gain_ref, shift_ref = refs[:3]
        total_ref, normed_ref, weight = refs[-3:]
        at = 3 + len(weights)

        @pl.when(pl.program_id(0) == 0)
        def _():
            top = 0
            for ref in refs[3:at]:
                weight[top : top + ref.shape[0], :] = ref[...]
                top += ref.shape[0]

        for part in range(2):
            here = slice(part * blk // 2, (part + 1) * blk // 2)
            left = jnp.concatenate([r[here, :] for r in refs[at : at + len(pieces)]], axis=1)
            total = token_ref[here, :].astype(jnp.float32) + dotf(left, weight[...])
            first = pl.program_id(0) * blk + part * (blk // 2) - u[0]

            @pl.when(jnp.logical_and(first >= 0, first < own))
            def _():
                total_ref[pl.ds(pl.multiple_of(first, 16), blk // 2), :] = total

            normed_ref[here, :] = norm_parts(total, gain_ref[...], shift_ref[...])[2].astype(jnp.bfloat16)

    whole = spec((blk, features), flat)
    return stage(
        line, "project_out", body, (rows // blk,), start, ins,
        [
            (jax.ShapeDtypeStruct((own, features), jnp.float32), spec((own, features), lambda j, u: (0, 0))),
            (jax.ShapeDtypeStruct((rows, features), jnp.bfloat16), whole),
        ],
        scratch=[pltpu.VMEM((depth, features), jnp.bfloat16)],
    )


def turn_rows(rows, blk, turn):
    n = rows // 2 // blk
    if turn:
        return lambda j, u: (u[0] * n + j, 0)
    return lambda j, u: ((1 - u[0]) * n + j, 0)


def feed_forward(line, upper, turn, normed, cotangent, up, down, count):
    rows, features = normed.shape
    hidden = up.shape[1]
    blk = min(rows // 2, 256)
    at = turn_rows(rows, blk, turn)
    flat = lambda j, u: (j, 0)

    def body(u, normed_ref, cot_ref, up_ref, down_ref, active_ref, inner_ref, *back_refs):
        for part in range(2):
            here = slice(part * blk // 2, (part + 1) * blk // 2)
            gelu, slope = gelu_pair(dotf(normed_ref[here, :], up_ref[...]))
            active_ref[here, :] = gelu.astype(jnp.bfloat16)
            grad = (dotf(cot_ref[here, :], down_ref[...], NT) * slope).astype(jnp.bfloat16)
            inner_ref[here, :] = grad
            put([r.at[here, :] for r in back_refs], dotf(grad, up_ref[...], NT))

    outs = pieces_of(rows // 2, 2 * hidden, 2) + pieces_of(rows // 2, features, count)
    return stage(
        line, "feed_forward", body, (rows // 2 // blk,), upper,
        columns([normed, cotangent], blk, at) + [fixed(up), fixed(down)],
        [(out, spec((blk, out.shape[1]), flat)) for out in outs],
    )


def product(line, left, right, count):
    rows = left.shape[0]
    blk = min(rows, 256)
    flat = lambda j, u: (j, 0)

    def body(u, l, r, *outs):
        put(outs, dotf(l[...], r[...]))

    made = stage(
        line, "product", body, (rows // blk,), 0,
        columns([left], blk, flat) + [fixed(right)],
        [(x, spec((blk, x.shape[1]), flat)) for x in pieces_of(rows, right.shape[1], count)],
    )
    return made if count > 1 else [made]


def product_back(line, upper, turn, lefts, rights, pieces):
    rows = lefts[0][0].shape[0]
    features, width = rights[0].shape
    blk = min(rows // 2, 256)
    at = turn_rows(rows, blk, turn)
    flat = [x for left in lefts for x in left]

    def body(u, *refs):
        weight = refs[-1]

        @pl.when(pl.program_id(0) == 0)
        def _():
            for i, r in enumerate(refs[len(flat) : len(flat) + len(rights)]):
                weight[:, i * width : (i + 1) * width] = r[...]

        put(refs[len(flat) + len(rights) : -1], dotf(cat(refs[: len(flat)]), weight[...], NT))

    made = stage(
        line, "product_back", body, (rows // 2 // blk,), upper,
        columns(flat, blk, at) + [fixed(r) for r in rights],
        [(x, spec((blk, x.shape[1]), lambda j, u: (j, 0))) for x in pieces_of(rows // 2, features, pieces)],
        scratch=[pltpu.VMEM((features, len(rights) * width), jnp.bfloat16)],
    )
    return made if pieces > 1 else [made]


def hold_small(line, mine):
    def body(u, m, out):
        out[...] = m[...]

    return stage(line, "add_small", body, (1,), 0, [fixed(mine)], [(jax.ShapeDtypeStruct(mine.shape, mine.dtype), fixed(mine)[1])])


def add_small(line, mine, got):
    def body(u, m, g, out):
        out[...] = m[...] + g[...]

    return stage(line, "add_small", body, (1,), 0, [fixed(mine), fixed(got)], [(jax.ShapeDtypeStruct(mine.shape, mine.dtype), fixed(mine)[1])])


def shards(
    n_dp,
    n_tp,
    tokens,
    query_weight,
    key_weight,
    value_weight,
    out_weight,
    up_weight,
    down_weight,
    bias_table,
    gain_one,
    shift_one,
    gain_two,
    shift_two,
    single_item,
    cotangent,
):
    tp_bits = index_bits(n_tp)
    dp_bits = index_bits(n_dp)
    far_first = tp_bits[1:] + tp_bits[:1]
    low = jnp.bfloat16
    full = jnp.float32
    row_count, features = tokens.shape
    head_count = bias_table.shape[1]
    width = head_count * HD
    tp_up = [rank_bit("tp", bit) for bit in tp_bits]
    dp_up = [rank_bit("dp", bit) for bit in dp_bits]
    start, own_count = own_start("tp", tp_bits, row_count)

    def tp_swap(values, i):
        return swap(values, "tp", n_tp, tp_bits[i])

    def dp_swap(values, i):
        return swap(values, "dp", n_dp, dp_bits[i])

    line = []

    class Sum:
        def __init__(self, axis, send, keep):
            self.axis = axis
            self.up = tp_up if axis == "tp" else dp_up
            self.keep, self.at = keep, 0
            self.swap(send)

        def swap(self, arrays):
            self.got = [keep_far((tp_swap if self.axis == "tp" else dp_swap)(x, self.at)) for x in arrays]

        def count(self, at):
            return PIECES if self.axis == "tp" and at == 0 else 1

        def halve(self):
            self.at += 1
            if self.axis == "dp" and self.at == len(self.up) - 1:
                self.keep = [add_up(line, self.keep[0], self.got[0])]
                self.swap(self.keep)
            else:
                send, self.keep = split_add(line, self.up[self.at], self.keep, self.got, self.count(self.at))
                self.swap(send)

        def spread(self, values):
            self.keep = values
            self.swap(values)

        def total(self):
            pass

        def fan(self):
            mine = [add_up(line, self.keep[0], self.got[0])]
            self.at -= 1
            while self.at > 1:
                self.spread(mine)
                mine = [join_rows(line, self.up[self.at], self.keep, self.got, low)[0]]
                self.at -= 1
            self.mine = mine[0]
            self.near = dp_swap(self.mine, 1)
            self.far = [dp_swap(self.mine, 0), dp_swap(self.near, 0)]

        def finish(self, outs):
            return join_four(line, self.up[:2], [self.mine, self.near] + self.far, outs)

        def double(self, dtype=low):
            count = self.count(self.at - 1) if self.at else 1
            joined = join_rows(line, self.up[self.at], self.keep, self.got, dtype, count)
            if self.at == 0:
                return joined[0]
            self.at -= 1
            self.spread(joined)

    out_parts = gather_parts(out_weight, "tp", n_tp, far_first)
    near_rows = near_bias(bias_table)
    normed_low, queries, key_rows, value_rows = norm_qkv(
        line, far(tokens), gain_one, shift_one, [far(w) for w in (query_weight, key_weight, value_weight)]
    )
    pairs = width // (2 * HD)
    attended, lse_rows, parts = [], [], []
    for pair in range(pairs):
        also = [out_parts[far_first[0]][:8, :128]] if pair == pairs - 1 else ()
        columns, sums = attn_forward(
            line, pair, single_item, near_rows, queries, key_rows, value_rows, also
        )
        attended.append(columns)
        lse_rows.append(sums)
        parts.append(gather_parts(columns, "tp", n_tp, far_first))
    parts = [[far(parts[pair][k]) if k else parts[pair][k] for pair in range(pairs)] for k in range(n_tp)]
    out_parts = [far(w) for w in out_parts]
    residual, normed_two_low = project_out(
        line, start, own_count, parts, out_parts, far(tokens), gain_two, shift_two
    )
    fed = [
        feed_forward(line, tp_up[0], turn, normed_two_low, cotangent, up_weight, down_weight, PIECES)
        for turn in (0, 1)
    ]
    two = Sum("tp", fed[0][2:], fed[1][2:])
    ups = [dp_up[0], tp_up[0]]
    down_group = [[(fed[turn][0], turn, [cotangent], turn) for turn in (0, 1)]]
    up_group = [[(normed_two_low, turn, [fed[turn][1]], turn) for turn in (0, 1)]]

    def halve_to_last(total, done):
        for _ in range(len(total.up) - 1 - done):
            total.halve()

    halve_to_last(two, 0)
    down_send = weight_grad(line, ups, True, down_group)
    down_keep = weight_grad(line, ups, False, down_group)
    down = Sum("dp", [down_send], [down_keep])
    ffn = Sum("tp", *[product(line, fed[turn][0], down_weight, PIECES) for turn in (0, 1)])
    up_keep = weight_grad(line, ups, False, up_group)
    grad_residual, grad_residual_low, sums_two = norm_back_own(
        line, two.keep[0], two.got[0], residual, cotangent, gain_two, start
    )
    two.spread([grad_residual_low])
    down.halve()
    up_send = weight_grad(line, ups, True, up_group)
    up = Sum("dp", [up_send], [up_keep])
    for _ in tp_bits[1:]:
        two.double()
    halve_to_last(ffn, 0)
    grad_residual_low = two.double()
    grad_query, grad_key, grad_value, near_totals = attn_backward(
        line, single_item, near_rows, queries, key_rows, value_rows, attended, lse_rows,
        grad_residual_low, out_weight,
    )
    grad_table = table_grad(near_totals, head_count)
    heads_back = [[grad_query], [grad_key], [grad_value]]
    head_weights = [query_weight, key_weight, value_weight]
    mixed_group = [
        [(normed_low, None, heads_back[2], None)],
        [(grad_residual_low, None, attended, None)],
    ]
    heads_group = [[(normed_low, None, heads_back[0] + heads_back[1], None)]]
    halve_to_last(down, 1)
    one = Sum("tp", *[product_back(line, tp_up[0], turn, heads_back, head_weights, PIECES) for turn in (0, 1)])
    mixed_send = weight_grad(line, ups, True, mixed_group)
    halve_to_last(one, 0)
    up.halve()
    mixed = Sum("dp", [mixed_send], [weight_grad(line, ups, False, mixed_group)])
    heads_send = weight_grad(line, ups, True, heads_group)
    heads = Sum("dp", [heads_send], [weight_grad(line, ups, False, heads_group)])
    _, grad_tokens, sums_one = norm_back_own(
        line, one.keep[0], one.got[0], tokens, grad_residual, gain_one, start
    )
    one.spread([grad_tokens])
    table_size = NB * head_count
    slot = jnp.zeros((n_tp * table_size,), full)
    me_tp = lax.axis_index("tp")
    slot = lax.dynamic_update_slice(slot, grad_table.reshape(table_size), (me_tp * table_size,))
    slot = jnp.pad(slot, (0, -slot.size % features)).reshape(-1, features)
    small = [jnp.concatenate([sums_one[:2], sums_two[:2], slot])]
    steps = [("tp", n_tp, bit) for bit in tp_bits] + [("dp", n_dp, bit) for bit in dp_bits]
    small_line = []

    def small_step(use):
        if steps:
            axis, count, bit = steps.pop(0)
            small[0] = add_small(use, small[0], swap(small[0], axis, count, bit))

    mixed.halve()
    halve_to_last(up, 1)
    down.fan()
    heads.halve()
    halve_to_last(mixed, 1)
    for _ in tp_bits[1:]:
        one.double()
    up.fan()
    halve_to_last(heads, 1)
    ffn.spread([add_own(line, ffn.keep[0], ffn.got[0], residual)])
    grad_tokens = one.double(full)
    grad_down = down.finish([(0, features, False)])
    mixed.fan()
    for _ in tp_bits[1:]:
        ffn.double()
    grad_up = up.finish([(0, up_weight.shape[1], False)])
    heads.fan()
    result = ffn.double()
    small[0] = hold_small(line, small[0])
    steps = steps[: len(tp_bits)] + steps[len(tp_bits) + 1 :] + steps[len(tp_bits) : len(tp_bits) + 1]
    while steps:
        small_step(small_line)
    grad_vw, grad_out = mixed.finish([(0, width, False), (width, width, True)])
    grad_qw, grad_kw = heads.finish([(0, width, False), (width, width, False)])
    down.total()
    up.total()
    mixed.total()
    heads.total()
    small = small[0]
    grad_table = lax.dynamic_slice(
        small[4:].reshape(-1), (me_tp * table_size,), (table_size,)
    ).reshape(NB, head_count)
    return (
        result,
        grad_tokens,
        grad_qw,
        grad_kw,
        grad_vw,
        grad_out,
        grad_up,
        grad_down,
        grad_table,
        small[0],
        small[1],
        small[2],
        small[3],
    )


def solution(mesh):
    placed = (
        P("dp", None),
        P(None, "tp"),
        P(None, "tp"),
        P(None, "tp"),
        P("tp", None),
        P(None, "tp"),
        P("tp", None),
        P(None, "tp"),
        P(),
        P(),
        P(),
        P(),
        P("dp"),
        P("dp", None),
    )
    return jax.shard_map(
        functools.partial(shards, mesh.shape["dp"], mesh.shape["tp"]),
        mesh=mesh,
        in_specs=placed,
        out_specs=(
            P("dp", None),
            P("dp", None),
            P(None, "tp"),
            P(None, "tp"),
            P(None, "tp"),
            P("tp", None),
            P(None, "tp"),
            P("tp", None),
            P(None, "tp"),
            P(),
            P(),
            P(),
            P(),
        ),
        check_vma=False,
    )
```
